512 devices in a mesh: storage: 32 (over x, z), batch: 16 (over y, core).
Axes of the slice: x: 4, y: 8, z: 8, core: 2. Of those that a mesh axis runs over, the one named last changes fastest.
Arguments:
- node_features: bfloat16 [65536, 768], P(('storage', 'batch')), may hold values from -16 to 16
- history: float32 [65536, 768], P(('storage', 'batch')), may hold values from -6 to 6
- requests: int32 [16384, 8], P(('storage', 'batch')), may hold values from 0 to 127
- neighbours: int32 [65536, 16], P(('storage', 'batch')), may hold values from 0 to 255
- pattern: int32 [512, 16], P('storage'), may hold values from 0 to 1, as said below
- push_owner: int32 [65536], P(('storage', 'batch')), may hold values from 0 to 31, as said below
- push_slot: int32 [16384, 4], P(('storage', 'batch')), may hold values from 0 to 127, as said below
- w_query: bfloat16 [768, 384], replicated, may hold values from -1 to 1
- w_key: bfloat16 [768, 384], replicated, may hold values from -1 to 1
- w_value: bfloat16 [768, 384], replicated, may hold values from -0.21875 to 0.21875
- w_gate: bfloat16 [768, 384], replicated, may hold values from -0.21875 to 0.21875
- w_out: bfloat16 [384, 768], replicated, may hold values from -0.3125 to 0.3125
- cotangent: bfloat16 [65536, 768], P(('storage', 'batch')), may hold values from -0.75 to 0.75
Outputs:
- out_features: bfloat16 [65536, 768], P(('storage', 'batch'))
- new_history: float32 [65536, 768], P(('storage', 'batch'))
- grad_gate: float32 [768, 384], P('batch', 'storage')
- grad_value: float32 [768, 384], P('batch', 'storage')
The draws below stay inside these ranges and needn't reach their ends.
Inputs may be any that keep to these rules, and one draw needn't show every extreme that they name: `pattern`: 0 or 1; every query block attends its own block. `push_owner`: exactly 4 nodes of each device name each storage index. `push_slot`: the 128 entries of one device are distinct.
All inputs are finite; a program needn't handle non-finite values.
Results may differ from the reference program's by a relative error of at most 0.035.
Values may be sent and summed in bfloat16 or wider, within the bound.
A program may use at most 64 MiB of HBM per device.

```python
import jax
import jax.numpy as jnp
from jax import lax

D = 768
HEADS = 6
HEAD_DIM = 64
ATT_WIDTH = 384
BLOCK = 128
ROWS = 128
HIST_DEV = 128
SLOTS = 8
NEIGHBOURS = 16
PUSH_CAP = 4
CLUSTER = 2048
CLUSTER_BLOCKS = 16
NODES = 65536
HIST_ROWS = 65536
N_STORAGE = 32
N_BATCH = 16
DEVICES = 512


def query_base(key):
    return jax.random.truncated_normal(key, -6.0, 6.0, (D, HEADS * HEAD_DIM), jnp.float32) * (2.0 * D ** (-0.5))


def draw_node_features(key, part):
    key = jax.random.fold_in(key, 3)
    return jax.random.truncated_normal(key, -6.0, 6.0, (NODES, D), jnp.float32).astype(jnp.bfloat16)


def draw_w_query(key, part):
    shared = query_base(key)
    return shared.astype(jnp.bfloat16)


def draw_w_key(key, part):
    key = jax.random.fold_in(key, 13)
    own = query_base(key)
    return own.astype(jnp.bfloat16)


def draw_pattern(key, part):
    key = jax.random.fold_in(key, 5)
    key_level, key_dice = jax.random.split(key)
    total_rows = N_STORAGE * CLUSTER_BLOCKS
    level = jax.random.randint(key_level, (total_rows, 1), 0, 4)
    limit = jnp.array([16, 8, 4, 1], jnp.int32)[level]
    dice = jax.random.randint(key_dice, (total_rows, CLUSTER_BLOCKS), 0, 16)
    own_block = jnp.arange(total_rows, dtype=jnp.int32)[:, None] % CLUSTER_BLOCKS
    column = jnp.arange(CLUSTER_BLOCKS, dtype=jnp.int32)[None, :]
    return jnp.where((dice < limit) | (own_block == column), 1, 0).astype(jnp.int32)


def draw_push_owner(key, part):
    key = jax.random.fold_in(key, 7)
    device_keys = jax.random.split(key, DEVICES)
    placed = jax.vmap(lambda single: jax.random.permutation(single, ROWS))(device_keys)
    return (placed // (ROWS // N_STORAGE)).reshape(-1).astype(jnp.int32)


def draw_push_slot(key, part):
    key = jax.random.fold_in(key, 9)
    device_keys = jax.random.split(key, DEVICES)
    chosen = jax.vmap(lambda single: jax.random.permutation(single, HIST_DEV)[:ROWS])(device_keys)
    return chosen.reshape(DEVICES * N_STORAGE, ROWS // N_STORAGE).astype(jnp.int32)


def set_ends(entries, stream_key, least, top_value):
    dims = entries.shape
    index_at = [jax.random.randint(jax.random.fold_in(stream_key, axis), (), 0, dims[axis]) for axis in range(len(dims))]
    entries = entries.at[tuple(index_at)].set(least)
    longest = dims.index(max(dims))
    index_at[longest] = (index_at[longest] + 1) % dims[longest]
    return entries.at[tuple(index_at)].set(top_value)


def spiked(drawn, key, source, target, blocks, factor):
    def block_of(dim):
        return (jnp.arange(drawn.shape[dim]) // (drawn.shape[dim] // blocks)).reshape((-1,) + (1,) * (drawn.ndim - 1 - dim))

    first = jax.random.permutation(key, blocks)[block_of(target)]
    far = (block_of(target) + blocks // 2) % blocks
    return jnp.where((block_of(source) == first) | (block_of(source) == far), factor * drawn, drawn)


def level_of(rng, extent, cuts, smallest, high):
    factor_of = 1.0
    for axis_at, shards_of in cuts:
        steps = jax.random.uniform(jax.random.fold_in(jax.random.fold_in(rng, 6), axis_at), (shards_of,), jnp.float32, smallest / len(cuts), high / len(cuts))
        factor_of = factor_of * jnp.repeat(jnp.exp(steps), extent[axis_at] // shards_of).reshape((-1,) + (1,) * (len(extent) - 1 - axis_at))
    return factor_of


def gaussian(key, extent, width, bound, shards=(), kind=jnp.bfloat16):
    gain = level_of(key, extent, shards, -0.22, 0.18) if shards else 1.0
    entries = jax.random.normal(key, extent, jnp.float32) * width * gain
    return jnp.minimum(jnp.maximum(entries, -bound), bound).astype(kind)


def bell_draw_with(own_key, extent, width, reach, shards, heavy, kind=jnp.bfloat16):
    entries = width * jax.random.normal(own_key, extent, jnp.float32)
    if shards:
        entries = entries * level_of(own_key, extent, shards, -0.22, 0.18)
    return jnp.clip(spiked(entries, jax.random.fold_in(own_key, 3), *heavy), -reach, reach).astype(kind)


def setup_inputs(seed: int = 0) -> dict:
    splits = jax.random.split(jax.random.key(seed), 14)
    return {
        "node_features": draw_node_features(jax.random.fold_in(splits[13], 71), 0),
        "history": gaussian(splits[1], (HIST_ROWS, D), 1.0, 6.0, ((0, 512),), jnp.float32),
        "requests": set_ends(jax.random.randint(splits[2], (DEVICES * N_STORAGE, SLOTS), 0, HIST_DEV), jax.random.fold_in(splits[2], 1), 0, HIST_DEV - 1).astype(jnp.int32),
        "neighbours": set_ends(jax.random.randint(splits[3], (NODES, NEIGHBOURS), 0, N_STORAGE * SLOTS), jax.random.fold_in(splits[3], 1), 0, (N_STORAGE * SLOTS) - 1).astype(jnp.int32),
        "pattern": draw_pattern(jax.random.fold_in(splits[13], 71), 0),
        "push_owner": draw_push_owner(jax.random.fold_in(splits[13], 71), 0),
        "push_slot": draw_push_slot(jax.random.fold_in(splits[13], 71), 0),
        "w_query": draw_w_query(jax.random.fold_in(splits[13], 71), 0),
        "w_key": draw_w_key(jax.random.fold_in(splits[13], 71), 0),
        "w_value": gaussian(splits[9], (D, ATT_WIDTH), D ** -0.5, 0.21875),
        "w_gate": gaussian(splits[10], (D, ATT_WIDTH), D ** -0.5, 0.21875),
        "w_out": gaussian(splits[11], (ATT_WIDTH, D), ATT_WIDTH ** -0.5, 0.3125),
        "cotangent": bell_draw_with(splits[12], (NODES, D), (3.0 * NODES ** -0.5), 0.75, ((0, 512),), (0, 1, 256, 6.0)),
    }


NEG = -1e+30

def reference(node_features, history, requests, neighbours, pattern, push_owner, push_slot, w_query, w_key, w_value, w_gate, w_out, cotangent):
    inv_root = HEAD_DIM ** (-0.5)
    request_rows = jnp.arange(DEVICES * N_STORAGE, dtype=jnp.int32)
    column = request_rows // N_STORAGE % N_BATCH
    owner = request_rows % N_STORAGE
    first_row = (owner * N_BATCH + column) * HIST_DEV
    pulled = history[(first_row[:, None] + requests).reshape(-1)].astype(jnp.bfloat16)
    node_device = jnp.arange(NODES, dtype=jnp.int32) // ROWS
    positions = node_device[:, None] * (N_STORAGE * SLOTS) + neighbours

    def add_neighbour(step_index, running):
        chosen = lax.dynamic_index_in_dim(positions, step_index, 1, keepdims=False)
        return running + pulled[chosen].astype(jnp.float32)
    summed = lax.fori_loop(0, NEIGHBOURS, add_neighbour, jnp.zeros((NODES, D), jnp.float32))
    hidden_in = (node_features.astype(jnp.float32) + summed / NEIGHBOURS).astype(jnp.bfloat16)
    query = jnp.dot(hidden_in, w_query, preferred_element_type=jnp.float32).astype(jnp.bfloat16)
    keys = jnp.dot(hidden_in, w_key, preferred_element_type=jnp.float32).astype(jnp.bfloat16)
    values = jnp.dot(hidden_in, w_value, preferred_element_type=jnp.float32).astype(jnp.bfloat16)
    gate = jnp.dot(hidden_in, w_gate, preferred_element_type=jnp.float32).astype(jnp.bfloat16)

    def split_heads(matrix):
        return matrix.reshape(CLUSTER, HEADS, HEAD_DIM).transpose(1, 0, 2)

    def cluster(members):
        feats, inner, query_c, keys_c, values_c, gate_c, cot_c, pattern_c = members
        visible = jnp.repeat(jnp.repeat(pattern_c > 0, BLOCK, axis=0), BLOCK, axis=1)

        def head(parts):
            query_h, keys_h, values_h = parts
            scores = jnp.dot(query_h, keys_h.T, preferred_element_type=jnp.float32) * inv_root
            scores = jnp.where(visible, scores, NEG)
            row_max = lax.optimization_barrier(lax.optimization_barrier(jnp.max(scores, axis=1)).astype(jnp.bfloat16)).astype(jnp.float32)
            raised = jnp.exp(scores - row_max[:, None])
            row_sum = lax.optimization_barrier(lax.optimization_barrier(jnp.sum(raised, axis=1)).astype(jnp.bfloat16)).astype(jnp.float32)
            weights = (raised / row_sum[:, None]).astype(jnp.bfloat16)
            attended_h = jnp.dot(weights, values_h, preferred_element_type=jnp.float32).astype(jnp.bfloat16)
            return (attended_h, weights)
        attended_heads, weights = lax.map(head, (split_heads(query_c), split_heads(keys_c), split_heads(values_c)))
        attended = attended_heads.transpose(1, 0, 2).reshape(CLUSTER, ATT_WIDTH)
        gated = (attended.astype(jnp.float32) * gate_c.astype(jnp.float32)).astype(jnp.bfloat16)
        output = (feats.astype(jnp.float32) + jnp.dot(gated, w_out, preferred_element_type=jnp.float32)).astype(jnp.bfloat16)
        back_gated = jnp.dot(cot_c, w_out.T, preferred_element_type=jnp.float32).astype(jnp.bfloat16)
        back_gate = (back_gated.astype(jnp.float32) * attended.astype(jnp.float32)).astype(jnp.bfloat16)
        back_attended = (back_gated.astype(jnp.float32) * gate_c.astype(jnp.float32)).astype(jnp.bfloat16)
        grad_g = jnp.dot(inner.T, back_gate, preferred_element_type=jnp.float32)

        def value_grad(parts):
            weights_h, back_h = parts
            return jnp.dot(weights_h.T, back_h, preferred_element_type=jnp.float32).astype(jnp.bfloat16)
        back_values = lax.map(value_grad, (weights, split_heads(back_attended)))
        back_values = back_values.transpose(1, 0, 2).reshape(CLUSTER, ATT_WIDTH)
        grad_v = jnp.dot(inner.T, back_values, preferred_element_type=jnp.float32)
        return (output, grad_g, grad_v)

    def by_cluster(matrix):
        return matrix.reshape(N_STORAGE, CLUSTER, matrix.shape[1])
    outputs, grads_g, grads_v = lax.map(cluster, (by_cluster(node_features), by_cluster(hidden_in), by_cluster(query), by_cluster(keys), by_cluster(values), by_cluster(gate), by_cluster(cotangent), pattern.reshape(N_STORAGE, CLUSTER_BLOCKS, CLUSTER_BLOCKS)))
    out_features = outputs.reshape(NODES, D)
    owners = push_owner.reshape(DEVICES, ROWS)
    onehot = (owners[:, :, None] == jnp.arange(N_STORAGE, dtype=jnp.int32)[None, None, :]).astype(jnp.int32)
    rank = lax.optimization_barrier(jnp.sum((jnp.cumsum(onehot, axis=1) - onehot) * onehot, axis=2))
    devices = jnp.arange(DEVICES, dtype=jnp.int32)
    sender = devices // N_BATCH
    owner_device = owners * N_BATCH + (devices % N_BATCH)[:, None]
    slot = push_slot.reshape(DEVICES, N_STORAGE, PUSH_CAP)[owner_device, jnp.broadcast_to(sender[:, None], (DEVICES, ROWS)), rank]
    target = (owner_device * HIST_DEV + slot).reshape(-1)
    new_history = history.at[target].set(out_features.astype(jnp.float32))
    return (out_features, new_history, lax.optimization_barrier(jnp.sum(grads_g, axis=0)), lax.optimization_barrier(jnp.sum(grads_v, axis=0)))
```

```python
import functools

import jax
import jax.numpy as jnp
from jax import lax
from jax.experimental import pallas as pl
from jax.experimental.pallas import tpu as pltpu
from jax.sharding import PartitionSpec as P

F32, BF16, I32 = jnp.float32, jnp.bfloat16, jnp.int32
MESH = pl.DeviceIdType.MESH
STORE = 32
RING = 8
HEADS_CORE = 3
NEG = 1e30


def iota(shape, dim):
    return lax.broadcasted_iota(I32, shape, dim)


def onehot(cond):
    return jnp.where(cond, 1.0, 0.0).astype(BF16)


def mm(a, b):
    return lax.dot_general(a, b, (((1,), (0,)), ((), ())), preferred_element_type=F32)


def mm_nt(a, b):
    return lax.dot_general(a, b, (((1,), (1,)), ((), ())), preferred_element_type=F32)


def mm_tn(a, b):
    return lax.dot_general(a, b, (((0,), (0,)), ((), ())), preferred_element_type=F32)


def kernel(
    nf_ref, hist_ref, req_ref, nbr_ref, pat_ref, owner_ref, slot_ref,
    cot_hbm, wq_hbm, wk_hbm, wv_hbm, wg_hbm, wo_hbm,
    out_ref, newh_ref, grad_ref,
    wq, wk, wv, wg, wo, wvt, wgt, cot,
    req_src, asked, found, table,
    cl_ref, cr_ref, psel, nsel, bias_ref,
    hid, qm, vt, s_ref, p_ref, acc_ref, mx_ref, gate_t, bg_t,
    gated, gsib, psend, parr, gsend, grecv, tsend, tfin,
    load_sem, cot_sems, req_sems, pull_sems, ring_send, ring_recv, sib_send, sib_recv,
    gated_sems, push_sems, gy_send, gy_recv, gf_sems,
):
    s = lax.axis_index("storage")
    b = lax.axis_index("batch")
    y = lax.div(b, 2)
    c = lax.rem(b, 2)
    sib = b + 1 - 2 * c
    win = pl.multiple_of(c * 128, 128)

    loads = [
        pltpu.make_async_copy(src.at[:, pl.ds(win, 256)], dst, load_sem.at[i])
        for i, (src, dst) in enumerate(((wq_hbm, wq), (wk_hbm, wk), (wv_hbm, wv), (wg_hbm, wg)))
    ]
    loads.append(pltpu.make_async_copy(wo_hbm, wo, load_sem.at[4]))
    loads.append(
        pltpu.make_async_copy(cot_hbm, cot.at[pl.ds(pl.multiple_of(c * 128, 128), 128)], load_sem.at[5])
    )
    for copy in loads:
        copy.start()

    barrier = pltpu.get_barrier_semaphore()

    def greet_store(k, _):
        peer = lax.rem(s + k, STORE)
        pl.semaphore_signal(barrier, inc=1, device_id=(peer, b), device_id_type=MESH)
        pl.semaphore_signal(barrier, inc=1, device_id=(peer, sib), device_id_type=MESH)
        return 0

    lax.fori_loop(1, STORE, greet_store, 0)
    pl.semaphore_signal(barrier, inc=1, device_id=(s, sib), device_id_type=MESH)

    def greet_ring(k, _):
        peer = lax.rem(y + k, RING) * 2 + c
        pl.semaphore_signal(barrier, inc=1, device_id=(s, peer), device_id_type=MESH)
        return 0

    lax.fori_loop(1, RING, greet_ring, 0)

    req_src[...] = jnp.zeros_like(req_src)
    req_src[:, 0, 0:8] = req_ref[...]
    pl.semaphore_wait(barrier, 2 * (STORE - 1) + 1 + RING - 1)

    def store_copy(src, dst, sems, peer):
        return pltpu.make_async_remote_copy(
            src_ref=src, dst_ref=dst, send_sem=sems.at[0], recv_sem=sems.at[1],
            device_id=(peer, b), device_id_type=MESH,
        )

    def send_all(src, dst, sems):
        def body(k, _):
            peer = lax.rem(s + k, STORE)
            store_copy(src.at[peer], dst.at[s], sems, peer).start()
            return 0

        lax.fori_loop(1, STORE, body, 0)

    def bulk_wait(ref, sem):
        pltpu.make_async_copy(ref, ref, sem).wait()

    others = pl.ds(0, STORE - 1)

    send_all(req_src, asked, req_sems)
    asked[s] = req_src[s]
    cot_copy = pltpu.make_async_remote_copy(
        src_ref=cot_hbm, dst_ref=cot.at[pl.ds(pl.multiple_of(c * 128, 128), 128)],
        send_sem=cot_sems.at[0], recv_sem=cot_sems.at[1],
        device_id=(s, sib), device_id_type=MESH,
    )
    cot_copy.start()

    hist_b = hist_ref[...].astype(BF16)
    rep = onehot(iota((STORE * 16, STORE), 1) == (iota((STORE * 16, STORE), 0) >> 4))
    bulk_wait(asked.at[others], req_sems.at[1])

    asked_f = asked[...].reshape(STORE, 128).astype(F32).astype(BF16)
    spread = mm(rep, asked_f)
    prow = iota((STORE * 16, 128), 0)
    lane = iota((STORE * 16, 128), 1)
    mine = jnp.sum(jnp.where(lane == (prow & 7), spread, 0.0), axis=1, keepdims=True).astype(I32)
    hit = mine == lane
    pick_l = onehot(hit & ((prow & 8) == 0))
    pick_r = onehot(hit & ((prow & 8) != 0))
    rows = mm(pick_l, hist_b[:, :384]) + mm(pick_r, hist_b[:, 384:])
    found[...] = rows.astype(BF16).reshape(STORE, 16, 384)
    send_all(found, table, pull_sems)
    table[s] = found[s]

    nbr = nbr_ref[...]
    at = iota((128, 256), 1)
    count = jnp.zeros((128, 256), F32)
    for k in range(16):
        count = count + jnp.where(nbr[:, k : k + 1] == at, 1.0, 0.0)
    count = count.astype(BF16)
    src_i = iota((256, 512), 0)
    dst_i = iota((256, 512), 1)
    home = src_i + (src_i & -8)
    cl_ref[...] = mm(count, onehot(dst_i == home)).astype(BF16)
    cr_ref[...] = mm(count, onehot(dst_i == home + 8)).astype(BF16)

    owner_row = owner_ref[...]
    i0 = iota((128, 128), 0)
    i1 = iota((128, 128), 1)
    owner_all = jnp.broadcast_to(owner_row, (128, 128))
    owner_col = jnp.sum(jnp.where(i0 == i1, owner_all, 0), axis=1, keepdims=True)
    rank = jnp.sum(
        jnp.where((owner_col == owner_all) & (i0 < i1), 1, 0), axis=0, keepdims=True
    )
    pos = owner_row * 4 + rank
    pr = iota((512, 128), 0)
    place = ((pr >> 4) << 2) + (pr & 3) == pos
    for u in range(3):
        psel[u] = onehot(place & (((pr >> 2) & 3) == u))
    slots = slot_ref[...]
    kk = iota((STORE, 512), 1)
    flat = jnp.zeros((STORE, 512), I32)
    for e in range(4):
        flat = flat + jnp.where((kk & 3) == e, slots[:, e : e + 1], 0)
    slot_row = jnp.sum(
        jnp.where((kk >> 4) == iota((STORE, 512), 0), flat, 0), axis=0, keepdims=True
    )
    kc = iota((128, 512), 1)
    lands = iota((128, 512), 0) == slot_row
    for u in range(3):
        nsel[u] = onehot(lands & (((kc >> 2) & 3) == u))

    qsel = onehot(iota((16, 256), 0) == 2 * y + (iota((16, 256), 1) >> 7))
    seen = mm_tn(pat_ref[...].astype(F32).astype(BF16), qsel)
    bias_ref[...] = (seen - 1.0) * NEG
    mx_ref[...] = jnp.full_like(mx_ref, -2.0 * NEG)

    for copy in loads:
        copy.wait()
    wvt[...] = wv[...].T
    wgt[...] = wg[...].T

    bulk_wait(table.at[others], pull_sems.at[1])
    t2 = table[...].reshape(STORE * 16, 384)
    my_rows = pl.multiple_of(b * 128, 128)
    hid[pl.ds(my_rows, 128), 0:384] = (
        nf_ref[:, 0:384].astype(F32) + mm(cl_ref[...], t2) * (1.0 / 16)
    ).astype(BF16)
    hid[pl.ds(my_rows, 128), 384:768] = (
        nf_ref[:, 384:768].astype(F32) + mm(cr_ref[...], t2) * (1.0 / 16)
    ).astype(BF16)

    right = lax.rem(y + 1, RING)
    left = lax.rem(y + RING - 1, RING)

    def chip_at(direction, dist):
        return lax.rem(y + (RING - dist if direction == 0 else dist), RING)

    def half_of(chip, core, half):
        return hid.at[pl.ds(pl.multiple_of(chip * 256 + core * 128 + half * 64, 64), 64)]

    def ring_copy(direction, dist, half, chip):
        ref = half_of(chip, c, half)
        idx = (direction * 4 + dist - 1) * 2 + half
        to = right if direction == 0 else left
        return pltpu.make_async_remote_copy(
            src_ref=ref, dst_ref=ref, send_sem=ring_send.at[idx], recv_sem=ring_recv.at[idx],
            device_id=(s, to * 2 + c), device_id_type=MESH,
        )

    def sib_copy(direction, dist, half, chip, core):
        ref = half_of(chip, core, half)
        idx = (direction * 4 + (dist if dist else 0) - 1) * 2 + half if dist else 16 + half
        return pltpu.make_async_remote_copy(
            src_ref=ref, dst_ref=ref, send_sem=sib_send.at[idx], recv_sem=sib_recv.at[idx],
            device_id=(s, sib), device_id_type=MESH,
        )

    def halves(direction, dist):
        if dist < 4:
            return (0, 1)
        return (0,) if direction == 0 else (1,)

    sent = []

    def go(copy):
        copy.start()
        sent.append(copy)

    for half in (0, 1):
        for direction in (0, 1):
            go(ring_copy(direction, 1, half, y))
        go(sib_copy(0, 0, half, y, c))

    def wait_sib(direction, dist):
        chip = chip_at(direction, dist)
        for half in halves(direction, dist) if dist else (0, 1):
            sib_copy(direction, dist, half, chip, 1 - c).wait_recv()

    def process(chip):
        r0 = pl.multiple_of(chip * 256, 256)
        hc = hid[pl.ds(r0, 256), :]
        kc_ = mm(hc, wk[...]).astype(BF16)
        vt[chip] = mm_nt(wvt[...], hc).astype(BF16)
        b0 = bias_ref[pl.ds(2 * chip, 1), :]
        b1 = bias_ref[pl.ds(2 * chip + 1, 1), :]
        for h in range(HEADS_CORE):
            sc = mm_nt(kc_, qm[h])
            lo = sc[0:128] + b0
            hi = sc[128:256] + b1
            s_ref[h, pl.ds(r0, 128), :] = lo
            s_ref[h, pl.ds(r0 + 128, 128), :] = hi
            top = jnp.max(jnp.maximum(lo, hi), axis=0, keepdims=True)
            mx_ref[h : h + 1, :] = jnp.maximum(mx_ref[h : h + 1, :], top)

    dcol = iota((256, 256), 0) - c * 64
    masks = [(dcol >> 6) == h for h in range(HEADS_CORE)]
    my_chip = pl.multiple_of(y * 256, 256)

    for dist in range(1, 5):
        for half in (0, 1):
            for direction in (0, 1):
                if half not in halves(direction, dist):
                    continue
                chip = chip_at(direction, dist)
                ring_copy(direction, dist, half, chip).wait_recv()
                if dist < 4 and half in halves(direction, dist + 1):
                    go(ring_copy(direction, dist + 1, half, chip))
                go(sib_copy(direction, dist, half, chip, c))
        if dist == 1:
            wait_sib(0, 0)
            hc = hid[pl.ds(my_chip, 256), :]
            q = (mm(hc, wq[...]) * 0.125).astype(BF16).astype(F32)
            lq = (iota((256, 256), 1) - c * 64) >> 6
            for h in range(HEADS_CORE):
                qm[h] = jnp.where(lq == h, q, 0.0).astype(BF16)
            gate_t[...] = mm_nt(wgt[...], hc).astype(BF16)
            cot_copy.wait_recv()
            bg_t[...] = mm_nt(wo[pl.ds(win, 256), :], cot[...]).astype(BF16)
            process(y)
        else:
            for direction in (0, 1):
                wait_sib(direction, dist - 1)
                process(chip_at(direction, dist - 1))
    wait_sib(0, 4)
    wait_sib(1, 4)
    process(chip_at(0, 4))

    acc_ref[...] = jnp.zeros_like(acc_ref)

    def soft(j, sums):
        r0 = pl.multiple_of(j * 256, 256)
        new = []
        for h in range(HEADS_CORE):
            p = jnp.exp(s_ref[h, pl.ds(r0, 256), :] - mx_ref[h : h + 1, :])
            new.append(sums[h] + jnp.sum(p, axis=0, keepdims=True))
            pb = p.astype(BF16)
            p_ref[h, pl.ds(r0, 256), :] = pb
            acc_ref[h] += mm(vt[j], pb)
        return tuple(new)

    zero_row = jnp.zeros((1, 256), F32)
    sums = lax.fori_loop(0, RING, soft, (zero_row,) * HEADS_CORE)
    inv = jnp.zeros((256, 256), F32)
    att = jnp.zeros((256, 256), F32)
    for h in range(HEADS_CORE):
        one = 1.0 / sums[h]
        inv = jnp.where(masks[h], one, inv)
        att = jnp.where(masks[h], acc_ref[h] * one, att)
    att = att.astype(BF16).astype(F32)
    gate = gate_t[...].astype(F32)
    bg = bg_t[...].astype(F32)
    gated_t = (att * gate).astype(BF16)
    for qb in (0, 1):
        gated[qb] = gated_t[:, qb * 128 : (qb + 1) * 128]
    gated_copy = pltpu.make_async_remote_copy(
        src_ref=gated.at[1 - c], dst_ref=gsib, send_sem=gated_sems.at[0],
        recv_sem=gated_sems.at[1], device_id=(s, sib), device_id_type=MESH,
    )
    gated_copy.start()

    def send_grad(which, grad_t):
        gsend[which] = grad_t.T.astype(BF16)
        my_part = pl.multiple_of(y * 96, 32)
        grecv[which, y] = gsend[which, pl.ds(my_part, 96), :]

        def body(k, _):
            to = lax.rem(y + k, RING)
            pltpu.make_async_remote_copy(
                src_ref=gsend.at[which, pl.ds(pl.multiple_of(to * 96, 32), 96)],
                dst_ref=grecv.at[which, y],
                send_sem=gy_send.at[which], recv_sem=gy_recv.at[which],
                device_id=(s, to * 2 + c), device_id_type=MESH,
            ).start()
            return 0

        lax.fori_loop(1, RING, body, 0)

    send_grad(0, mm((bg * att).astype(BF16), hid[pl.ds(my_chip, 256), :]))

    gated_copy.wait_recv()
    out = nf_ref[...].astype(F32) + (
        mm_tn(gated[c], wo[pl.ds(win, 256), :])
        + mm_tn(gsib[...], wo[pl.ds(pl.multiple_of((1 - c) * 128, 128), 256), :])
    )
    out_b = out.astype(BF16)
    out_ref[...] = out_b
    pushed = mm(psel[0], out_b[:, 0:256])
    pushed = pushed + mm(psel[1], out_b[:, 256:512])
    pushed = pushed + mm(psel[2], out_b[:, 512:768])
    psend[...] = pushed.astype(BF16).reshape(STORE, 16, 256)
    send_all(psend, parr, push_sems)
    parr[s] = psend[s]

    back = (bg * gate).astype(BF16).astype(F32) * inv
    backs = [jnp.where(masks[h], back, 0.0).astype(BF16) for h in range(HEADS_CORE)]

    def value_part(j, total):
        r0 = pl.multiple_of(j * 256, 256)
        dv = mm_nt(backs[0], p_ref[0, pl.ds(r0, 256), :])
        dv = dv + mm_nt(backs[1], p_ref[1, pl.ds(r0, 256), :])
        dv = dv + mm_nt(backs[2], p_ref[2, pl.ds(r0, 256), :])
        return total + mm(dv.astype(BF16), hid[pl.ds(r0, 256), :])

    send_grad(1, lax.fori_loop(0, RING, value_part, jnp.zeros((256, 768), F32)))

    bulk_wait(parr.at[others], push_sems.at[1])
    arrived = parr[...].reshape(STORE * 16, 256)
    for u in range(3):
        newh_ref[:, u * 256 : (u + 1) * 256] = mm(nsel[u], arrived).astype(BF16)

    rr = iota((96, 256), 0)
    ll = iota((96, 256), 1)
    lm = ll & 127
    row_of = rr - (ll >> 7) * 48
    spread_g = onehot((row_of == lm) & (lm < 48))
    spread_v = onehot((row_of == lm - 64) & (lm >= 64) & (lm < 112))
    e0 = iota((256, 256), 0)
    e1 = iota((256, 256), 1)
    col_pick = onehot((e1 == c * 64 + (e0 >> 4) * 12 + (e0 & 15)) & ((e0 & 15) < 12))
    sums_y = []
    for which in (0, 1):
        bulk_wait(grecv.at[which, pl.ds(0, RING - 1)], gy_recv.at[which])
        total = grecv[which, 0].astype(F32)
        for j in range(1, RING):
            total = total + grecv[which, j].astype(F32)
        sums_y.append(total.astype(BF16))
    mixed = mm_tn(sums_y[0], spread_g) + mm_tn(sums_y[1], spread_v)
    tiles = mm(col_pick, mixed.astype(BF16)).astype(BF16)
    for core in (0, 1):
        tsend[core] = tiles[:, core * 128 : (core + 1) * 128].reshape(16, 16, 128)
    in_half = lax.div(s, 16)

    def send_tile(i, _):
        dest = lax.div(i, 2)
        core = lax.rem(i, 2)
        to = c * 16 + dest
        own = (to == s) & (core == c)

        @pl.when(own)
        def _():
            tfin[s] = tsend[core, dest]

        @pl.when(jnp.logical_not(own))
        def _():
            pltpu.make_async_remote_copy(
                src_ref=tsend.at[core, dest], dst_ref=tfin.at[s],
                send_sem=gf_sems.at[0], recv_sem=gf_sems.at[1],
                device_id=(to, y * 2 + core), device_id_type=MESH,
            ).start()

        return 0

    lax.fori_loop(0, 32, send_tile, 0)

    @pl.when(in_half == c)
    def _():
        bulk_wait(tfin.at[others], gf_sems.at[1])
        bulk_wait(tfin.at[others], gf_sems.at[0])

    @pl.when(in_half != c)
    def _():
        bulk_wait(tfin, gf_sems.at[1])
        bulk_wait(tfin, gf_sems.at[0])

    final = tfin[0].astype(F32)
    for j in range(1, STORE):
        final = final + tfin[j].astype(F32)
    grad_ref[...] = final

    bulk_wait(req_src.at[others], req_sems.at[0])
    bulk_wait(found.at[others], pull_sems.at[0])
    bulk_wait(psend.at[others], push_sems.at[0])
    cot_copy.wait_send()
    for copy in sent:
        copy.wait_send()
    gated_copy.wait_send()
    for which in (0, 1):
        bulk_wait(grecv.at[which, pl.ds(0, RING - 1)], gy_send.at[which])


def on_device(
    node_features, history, requests, neighbours, pattern, push_owner, push_slot,
    w_query, w_key, w_value, w_gate, w_out, cotangent,
):
    vmem = pl.BlockSpec(memory_space=pltpu.VMEM)
    hbm = pl.BlockSpec(memory_space=pl.ANY)
    out, newh, grads = pl.pallas_call(
        kernel,
        out_shape=(
            jax.ShapeDtypeStruct((128, 768), BF16),
            jax.ShapeDtypeStruct((128, 768), BF16),
            jax.ShapeDtypeStruct((16, 128), F32),
        ),
        in_specs=[vmem] * 7 + [hbm] * 6,
        out_specs=(vmem, vmem, vmem),
        scratch_shapes=[
            pltpu.VMEM((768, 256), BF16),
            pltpu.VMEM((768, 256), BF16),
            pltpu.VMEM((768, 256), BF16),
            pltpu.VMEM((768, 256), BF16),
            pltpu.VMEM((384, 768), BF16),
            pltpu.VMEM((256, 768), BF16),
            pltpu.VMEM((256, 768), BF16),
            pltpu.VMEM((256, 768), BF16),
            pltpu.VMEM((STORE, 1, 128), I32),
            pltpu.VMEM((STORE, 1, 128), I32),
            pltpu.VMEM((STORE, 16, 384), BF16),
            pltpu.VMEM((STORE, 16, 384), BF16),
            pltpu.VMEM((128, 512), BF16),
            pltpu.VMEM((128, 512), BF16),
            pltpu.VMEM((3, 512, 128), BF16),
            pltpu.VMEM((3, 128, 512), BF16),
            pltpu.VMEM((16, 256), F32),
            pltpu.VMEM((2048, 768), BF16),
            pltpu.VMEM((3, 256, 256), BF16),
            pltpu.VMEM((8, 256, 256), BF16),
            pltpu.VMEM((3, 2048, 256), F32),
            pltpu.VMEM((3, 2048, 256), BF16),
            pltpu.VMEM((3, 256, 256), F32),
            pltpu.VMEM((8, 256), F32),
            pltpu.VMEM((256, 256), BF16),
            pltpu.VMEM((256, 256), BF16),
            pltpu.VMEM((2, 256, 128), BF16),
            pltpu.VMEM((256, 128), BF16),
            pltpu.VMEM((STORE, 16, 256), BF16),
            pltpu.VMEM((STORE, 16, 256), BF16),
            pltpu.VMEM((2, 768, 256), BF16),
            pltpu.VMEM((2, 8, 96, 256), BF16),
            pltpu.VMEM((2, 16, 16, 128), BF16),
            pltpu.VMEM((STORE, 16, 128), BF16),
            pltpu.SemaphoreType.DMA((6,)),
            pltpu.SemaphoreType.DMA((2,)),
            pltpu.SemaphoreType.DMA((2,)),
            pltpu.SemaphoreType.DMA((2,)),
            pltpu.SemaphoreType.DMA((16,)),
            pltpu.SemaphoreType.DMA((16,)),
            pltpu.SemaphoreType.DMA((18,)),
            pltpu.SemaphoreType.DMA((18,)),
            pltpu.SemaphoreType.DMA((2,)),
            pltpu.SemaphoreType.DMA((2,)),
            pltpu.SemaphoreType.DMA((2,)),
            pltpu.SemaphoreType.DMA((2,)),
            pltpu.SemaphoreType.DMA((2,)),
        ],
        compiler_params=pltpu.CompilerParams(
            collective_id=0, has_side_effects=True, vmem_limit_bytes=48 * 1024 * 1024
        ),
        cost_estimate=pl.CostEstimate(
            flops=7_000_000_000, bytes_accessed=6_000_000, transcendentals=1_600_000
        ),
    )(
        node_features, history, requests, neighbours, pattern, push_owner.reshape(1, -1), push_slot,
        cotangent, w_query, w_key, w_value, w_gate, w_out,
    )
    return (
        out,
        newh.astype(F32),
        grads[0:12, 0:48].T,
        grads[0:12, 64:112].T,
    )


def solution(mesh):
    rows = P(("storage", "batch"), None)
    in_specs = (
        rows, rows, rows, rows, P("storage", None), P(("storage", "batch")), rows,
        P(), P(), P(), P(), P(), rows,
    )
    out_specs = (rows, rows, P("batch", "storage"), P("batch", "storage"))
    return jax.shard_map(
        on_device, mesh=mesh, in_specs=in_specs, out_specs=out_specs, check_vma=False
    )
```

```python
import functools

import jax
import jax.numpy as jnp
from jax import lax
from jax.experimental import pallas as pl
from jax.experimental.pallas import tpu as pltpu
from jax.sharding import PartitionSpec as P

F32, BF16, I32 = jnp.float32, jnp.bfloat16, jnp.int32
MESH = pl.DeviceIdType.MESH
STORE = 32
RING = 8
HEADS_CORE = 3
NEG = 1e30


def iota(shape, dim):
    return lax.broadcasted_iota(I32, shape, dim)


def onehot(cond):
    return jnp.where(cond, 1.0, 0.0).astype(BF16)


def mm(a, b):
    return lax.dot_general(a, b, (((1,), (0,)), ((), ())), preferred_element_type=F32)


def mm_nt(a, b):
    return lax.dot_general(a, b, (((1,), (1,)), ((), ())), preferred_element_type=F32)


def mm_tn(a, b):
    return lax.dot_general(a, b, (((0,), (0,)), ((), ())), preferred_element_type=F32)


def kernel(
    nf_hbm, hist_hbm, req_hbm, nbr_hbm, pat_hbm, owner_hbm, slot_hbm,
    cot_hbm, wq_hbm, wk_hbm, wv_hbm, wg_hbm, wo_hbm,
    out_ref, newh_ref, grad_ref,
    nf_ref, hist_ref, req_ref, nbr_ref, pat_ref, owner_ref, slot_ref,
    wq, wk, wv, wg, wo, wvt, wgt, cot,
    req_src, asked, found, table, mix, psel, nsel, bias_ref, lanes96,
    hid, qm, p_ref, acc_ref, mx_ref, sum_ref, mx_chip, gate_t, bg_t,
    gated, gsib, psend, parr, vsend, vrecv, tsend, tfin, gsend, grecv, hsend, gfin,
    load_sem, small_sem, cot_sems, req_sems, pull_send, pull_recv,
    ring_send, ring_recv, sib_send, sib_recv,
    gated_sems, push_sems, vy_sems, vs_sems, gs_sems, gy_sems,
):
    s = lax.axis_index("storage")
    b = lax.axis_index("batch")
    y = lax.div(b, 2)
    c = lax.rem(b, 2)
    sib = b + 1 - 2 * c
    in_half = lax.div(s, 16)
    win = pl.multiple_of(c * 128, 128)
    c64 = pl.multiple_of(c * 64, 64)

    small = [
        pltpu.make_async_copy(src, dst, small_sem.at[i])
        for i, (src, dst) in enumerate((
            (req_hbm, req_ref), (hist_hbm, hist_ref), (nbr_hbm, nbr_ref), (owner_hbm, owner_ref),
            (slot_hbm, slot_ref), (pat_hbm, pat_ref), (nf_hbm, nf_ref),
        ))
    ]
    for copy in small:
        copy.start()
    loads = [
        pltpu.make_async_copy(src.at[:, pl.ds(win, 256)], dst, load_sem.at[i])
        for i, (src, dst) in enumerate(((wq_hbm, wq), (wk_hbm, wk), (wv_hbm, wv), (wg_hbm, wg)))
    ]
    loads.append(pltpu.make_async_copy(wo_hbm, wo, load_sem.at[4]))
    loads.append(pltpu.make_async_copy(cot_hbm, cot.at[pl.ds(win, 128)], load_sem.at[5]))
    for copy in loads:
        copy.start()

    barrier = pltpu.get_barrier_semaphore()

    def greet_store(k, _):
        peer = lax.rem(s + k, STORE)
        pl.semaphore_signal(barrier, inc=1, device_id=(peer, b), device_id_type=MESH)
        pl.semaphore_signal(barrier, inc=1, device_id=(peer, sib), device_id_type=MESH)
        return 0

    lax.fori_loop(1, STORE, greet_store, 0)

    def greet_ring(k, _):
        peer = lax.rem(b + k, 2 * RING)
        pl.semaphore_signal(barrier, inc=1, device_id=(s, peer), device_id_type=MESH)
        return 0

    lax.fori_loop(1, 2 * RING, greet_ring, 0)

    small[0].wait()
    eye8 = onehot(iota((8, 128), 0) == iota((8, 128), 1))
    req_src[...] = mm_tn(req_ref[...].astype(F32).astype(BF16), eye8).astype(I32).reshape(STORE, 1, 128)
    pl.semaphore_wait(barrier, 2 * (STORE - 1) + 2 * RING - 1)

    def store_copy(src, dst, send_sem, recv_sem, peer):
        return pltpu.make_async_remote_copy(
            src_ref=src, dst_ref=dst, send_sem=send_sem, recv_sem=recv_sem,
            device_id=(peer, b), device_id_type=MESH,
        )

    def send_all(src, dst, send_sem, recv_sem):
        def body(k, _):
            peer = lax.rem(s + k, STORE)
            store_copy(src.at[peer], dst.at[s], send_sem, recv_sem, peer).start()
            return 0

        lax.fori_loop(1, STORE, body, 0)

    def bulk_wait(ref, sem):
        pltpu.make_async_copy(ref, ref, sem).wait()

    others = pl.ds(0, STORE - 1)

    send_all(req_src, asked, req_sems.at[0], req_sems.at[1])
    asked[s] = req_src[s]
    cot_copy = pltpu.make_async_remote_copy(
        src_ref=cot_hbm, dst_ref=cot.at[pl.ds(win, 128)],
        send_sem=cot_sems.at[0], recv_sem=cot_sems.at[1],
        device_id=(s, sib), device_id_type=MESH,
    )
    cot_copy.start()

    for copy in small[1:]:
        copy.wait()
    hist_b = hist_ref[...].astype(BF16)
    hist_l = jnp.concatenate([hist_b[:, p * 256 : p * 256 + 128] for p in range(3)], axis=1)
    hist_r = jnp.concatenate([hist_b[:, p * 256 + 128 : p * 256 + 256] for p in range(3)], axis=1)
    rep = onehot(iota((STORE * 16, STORE), 1) == (iota((STORE * 16, STORE), 0) >> 4))
    nbr = nbr_ref[...]
    at = iota((256, 128), 0)
    count = jnp.zeros((256, 128), F32)
    for k in range(16):
        count = count + jnp.where(nbr[k : k + 1, :] == at, 1.0, 0.0)
    count = count.astype(BF16)
    src_i = iota((256, 512), 0)
    dst_i = iota((256, 512), 1)
    home = src_i + (src_i & -8)
    mix[0:128] = mm_tn(count, onehot(dst_i == home)).astype(BF16)
    mix[128:256] = mm_tn(count, onehot(dst_i == home + 8)).astype(BF16)

    bulk_wait(asked.at[others], req_sems.at[1])

    asked_f = asked[...].reshape(STORE, 128).astype(F32).astype(BF16)
    spread = mm(rep, asked_f)
    prow = iota((STORE * 16, 128), 0)
    lane = iota((STORE * 16, 128), 1)
    mine = jnp.sum(jnp.where(lane == (prow & 7), spread, 0.0), axis=1, keepdims=True).astype(I32)
    hit = mine == lane
    pick_l = onehot(hit & ((prow & 8) == 0))
    pick_r = onehot(hit & ((prow & 8) != 0))
    rows = (mm(pick_l, hist_l) + mm(pick_r, hist_r)).astype(BF16)
    for p in range(3):
        found[p] = rows[:, p * 128 : (p + 1) * 128].reshape(STORE, 16, 128)
    for p in range(3):
        send_all(found.at[p], table.at[p], pull_send.at[p], pull_recv.at[p])
    for p in range(3):
        table[p, s] = found[p, s]

    for copy in loads:
        copy.wait()
    wvt[...] = wv[...].T
    wgt[...] = wg[...].T
    qsel = onehot(iota((16, 256), 0) == 2 * y + (iota((16, 256), 1) >> 7))
    seen = mm_tn(pat_ref[...].astype(F32).astype(BF16), qsel)
    bias_ref[...] = (seen - 1.0) * NEG
    mx_ref[...] = jnp.full_like(mx_ref, -2.0 * NEG)
    sum_ref[...] = jnp.zeros_like(sum_ref)
    acc_ref[...] = jnp.zeros_like(acc_ref)
    cot_copy.wait_recv()
    wo_mine = pl.multiple_of(c * 192, 64)
    wo_sib = pl.multiple_of((1 - c) * 192, 64)
    bg_t[...] = mm_nt(wo[pl.ds(wo_mine, 192), :], cot[...]).astype(BF16)

    lr = iota((768, 1024), 0)
    ll = iota((768, 1024), 1)
    lanes96[...] = onehot((lr == (ll >> 7) * 96 + (ll & 127)) & ((ll & 127) < 96))

    owner_row = owner_ref[...]
    i0 = iota((128, 128), 0)
    i1 = iota((128, 128), 1)
    owner_all = jnp.broadcast_to(owner_row, (128, 128))
    owner_col = jnp.sum(jnp.where(i0 == i1, owner_all, 0), axis=1, keepdims=True)
    rank = jnp.sum(
        jnp.where((owner_col == owner_all) & (i0 < i1), 1, 0), axis=0, keepdims=True
    )
    pos = owner_row * 4 + rank
    pr = iota((512, 128), 0)
    place = ((pr >> 4) << 2) + (pr & 3) == pos
    for u in range(3):
        psel[u] = onehot(place & (((pr >> 2) & 3) == u))
    sel = onehot(iota((STORE, 512), 0) == (iota((STORE, 512), 1) >> 4))
    wide = mm(slot_ref[...].astype(F32).astype(BF16), sel)
    slot_row = jnp.sum(
        jnp.where(iota((4, 512), 0) == (iota((4, 512), 1) & 3), wide, 0.0), axis=0, keepdims=True
    ).astype(I32)
    col = iota((128, 512), 1)
    lands = iota((128, 512), 0) == slot_row
    for u in range(3):
        nsel[u] = onehot(lands & (((col >> 2) & 3) == u))

    right = lax.rem(y + 1, RING)
    left = lax.rem(y + RING - 1, RING)
    my_rows = pl.multiple_of(b * 128, 128)
    my_chip = pl.multiple_of(y * 256, 256)

    def chip_at(direction, dist):
        return lax.rem(y + (RING - dist if direction == 0 else dist), RING)

    def unit(chip, core, part, half):
        row = pl.multiple_of(chip * 256 + core * 128 + half * 64, 64)
        return hid.at[pl.ds(row, 64), pl.ds(part * 256, 256)]

    def ring_copy(direction, dist, part, half):
        ref = unit(chip_at(direction, dist - 1), c, part, half)
        idx = ((direction * 4 + dist - 1) * 3 + part) * 2 + half
        to = right if direction == 0 else left
        return pltpu.make_async_remote_copy(
            src_ref=ref, dst_ref=ref, send_sem=ring_send.at[idx], recv_sem=ring_recv.at[idx],
            device_id=(s, to * 2 + c), device_id_type=MESH,
        )

    def ring_arrived(direction, dist, part, half):
        ref = unit(chip_at(direction, dist), c, part, half)
        idx = ((direction * 4 + dist - 1) * 3 + part) * 2 + half
        pltpu.make_async_copy(ref, ref, ring_recv.at[idx]).wait()

    def sib_copy(direction, dist, part, half, core):
        ref = unit(chip_at(direction, dist), core, part, half)
        idx = ((direction * 4 + dist - 1) * 3 + part) * 2 + half if dist else 48 + part * 2 + half
        return pltpu.make_async_remote_copy(
            src_ref=ref, dst_ref=ref, send_sem=sib_send.at[idx], recv_sem=sib_recv.at[idx],
            device_id=(s, sib), device_id_type=MESH,
        )

    def halves(direction, dist):
        if dist < 4:
            return (0, 1)
        return (0,) if direction == 0 else (1,)

    sent = []

    def go(copy):
        copy.start()
        sent.append(copy)

    def own(part):
        bulk_wait(table.at[part, others], pull_recv.at[part])
        t = table[part].reshape(STORE * 16, 128)
        mean = mm(mix[...], t) * (1.0 / 16)
        for i in (0, 1):
            col = pl.ds(part * 256 + i * 128, 128)
            hid[pl.ds(my_rows, 128), col] = (
                nf_ref[:, col].astype(F32) + mean[i * 128 : (i + 1) * 128]
            ).astype(BF16)
        for half in (0, 1):
            for direction in (0, 1):
                go(ring_copy(direction, 1, part, half))
        for half in (0, 1):
            go(sib_copy(0, 0, part, half, c))

    def hop(dist, part):
        for half in (0, 1):
            for direction in (0, 1):
                if half not in halves(direction, dist):
                    continue
                ring_arrived(direction, dist, part, half)
                if dist < 4 and half in halves(direction, dist + 1):
                    go(ring_copy(direction, dist + 1, part, half))
                go(sib_copy(direction, dist, part, half, c))

    def wait_sib(direction, dist):
        for part in range(3):
            for half in halves(direction, dist) if dist else (0, 1):
                sib_copy(direction, dist, part, half, 1 - c).wait_recv()

    def process(chip):
        r0 = pl.multiple_of(chip * 256, 256)
        hc = hid[pl.ds(r0, 256), :]
        kc = mm(hc, wk[...]).astype(BF16)
        vt = mm_nt(wvt[pl.ds(c64, 192), :], hc).astype(BF16)
        b0 = bias_ref[pl.ds(2 * chip, 1), :]
        b1 = bias_ref[pl.ds(2 * chip + 1, 1), :]
        for h in range(HEADS_CORE):
            sc = mm_nt(kc, qm[h])
            lo = sc[0:128] + b0
            hi = sc[128:256] + b1
            top = jnp.max(jnp.maximum(lo, hi), axis=0, keepdims=True)
            old = mx_ref[h : h + 1, :]
            new = jnp.maximum(old, top)
            keep = jnp.exp(old - new)
            lo = jnp.exp(lo - new)
            hi = jnp.exp(hi - new)
            mx_ref[h : h + 1, :] = new
            mx_chip[h, pl.ds(chip, 1), :] = new
            sum_ref[h : h + 1, :] = sum_ref[h : h + 1, :] * keep + jnp.sum(lo + hi, axis=0, keepdims=True)
            pb = jnp.concatenate([lo.astype(BF16), hi.astype(BF16)], axis=0)
            p_ref[h, pl.ds(r0, 256), :] = pb
            acc_ref[h] = acc_ref[h] * keep + mm(vt[h * 64 : (h + 1) * 64], pb)

    def near(direction, dist):
        wait_sib(direction, dist)
        process(chip_at(direction, dist))

    own(0)
    own(1)
    hop(1, 0)
    own(2)
    hop(1, 1)
    hop(2, 0)
    wait_sib(0, 0)
    hc_own = hid[pl.ds(my_chip, 256), :]
    q = (mm(hc_own, wq[...]) * 0.125).astype(BF16).astype(F32)
    lq = (iota((256, 256), 1) - c * 64) >> 6
    for h in range(HEADS_CORE):
        qm[h] = jnp.where(lq == h, q, 0.0).astype(BF16)
    hop(1, 2)
    process(y)
    hop(2, 1)
    hop(3, 0)
    near(0, 1)
    hop(2, 2)
    hop(3, 1)
    near(1, 1)
    hop(4, 0)
    hop(3, 2)
    near(0, 2)
    hop(4, 1)
    near(1, 2)
    near(0, 3)
    hop(4, 2)
    gate_t[...] = mm_nt(wgt[pl.ds(c64, 192), :], hid[pl.ds(my_chip, 256), :]).astype(BF16)
    near(1, 3)
    wait_sib(0, 4)
    wait_sib(1, 4)
    process(chip_at(0, 4))

    ones = [1.0 / sum_ref[h : h + 1, :] for h in range(HEADS_CORE)]
    att = jnp.concatenate([acc_ref[h] * ones[h] for h in range(HEADS_CORE)], axis=0)
    att = att.astype(BF16).astype(F32)
    gate = gate_t[...].astype(F32)
    bg = bg_t[...].astype(F32)
    gated_t = (att * gate).astype(BF16)
    for qb in (0, 1):
        gated[qb] = gated_t[:, qb * 128 : (qb + 1) * 128]
    gated_copy = pltpu.make_async_remote_copy(
        src_ref=gated.at[1 - c], dst_ref=gsib, send_sem=gated_sems.at[0],
        recv_sem=gated_sems.at[1], device_id=(s, sib), device_id_type=MESH,
    )
    gated_copy.start()

    e0 = iota((256, 192), 0)
    tile_rows = onehot((iota((256, 192), 1) == (e0 >> 4) * 12 + (e0 & 15)) & ((e0 & 15) < 12))
    gg = mm((bg * att).astype(BF16), hid[pl.ds(my_chip, 256), :]).astype(BF16)
    gsend[...] = mm(tile_rows, gg).astype(BF16).reshape(16, 16, 768)

    def send_gate(i, _):
        to = c * 16 + lax.rem(s + i, 16)
        dest = lax.rem(s + i, 16)

        @pl.when(to == s)
        def _():
            grecv[s] = gsend[dest]

        @pl.when(to != s)
        def _():
            store_copy(gsend.at[dest], grecv.at[s], gs_sems.at[0], gs_sems.at[1], to).start()

        return 0

    lax.fori_loop(0, 16, send_gate, 0)

    back = (bg * gate).astype(BF16).astype(F32)
    backs = [back[h * 64 : (h + 1) * 64] * ones[h] for h in range(HEADS_CORE)]

    def value_part(j, total):
        r0 = pl.multiple_of(j * 256, 256)
        dv = []
        for h in range(HEADS_CORE):
            scale = jnp.exp(mx_chip[h, pl.ds(j, 1), :] - mx_ref[h : h + 1, :])
            dv.append(mm_nt((backs[h] * scale).astype(BF16), p_ref[h, pl.ds(r0, 256), :]))
        return total + mm(jnp.concatenate(dv, axis=0).astype(BF16), hid[pl.ds(r0, 256), :])

    gv = lax.fori_loop(0, RING, value_part, jnp.zeros((192, 768), F32)).astype(BF16)
    gv = mm(gv, lanes96[...]).astype(BF16)
    for j in range(RING):
        vsend[j] = gv[:, j * 128 : (j + 1) * 128]
    vrecv[y] = vsend[y]

    def send_value(k, _):
        to = lax.rem(y + k, RING)
        pltpu.make_async_remote_copy(
            src_ref=vsend.at[to], dst_ref=vrecv.at[y],
            send_sem=vy_sems.at[0], recv_sem=vy_sems.at[1],
            device_id=(s, to * 2 + c), device_id_type=MESH,
        ).start()
        return 0

    lax.fori_loop(1, RING, send_value, 0)

    gated_copy.wait_recv()
    out = nf_ref[...].astype(F32) + (
        mm_tn(gated[c], wo[pl.ds(wo_mine, 192), :]) + mm_tn(gsib[...], wo[pl.ds(wo_sib, 192), :])
    )
    out_b = out.astype(BF16)
    out_ref[...] = out_b
    pushed = mm(psel[0], out_b[:, 0:256])
    pushed = pushed + mm(psel[1], out_b[:, 256:512])
    pushed = pushed + mm(psel[2], out_b[:, 512:768])
    psend[...] = pushed.astype(BF16).reshape(STORE, 16, 256)
    send_all(psend, parr, push_sems.at[0], push_sems.at[1])
    parr[s] = psend[s]

    bulk_wait(vrecv.at[pl.ds(0, RING - 1)], vy_sems.at[1])
    total = vrecv[0].astype(F32)
    for j in range(1, RING):
        total = total + vrecv[j].astype(F32)
    tsend[...] = mm(tile_rows, total.astype(BF16)).astype(BF16).reshape(16, 16, 128)

    def send_tile(i, _):
        dest = lax.rem(s + lax.div(i, 2), 16)
        core = lax.rem(i, 2)
        to = c * 16 + dest
        own_tile = (to == s) & (core == c)

        @pl.when(own_tile)
        def _():
            tfin[s] = tsend[dest]

        @pl.when(jnp.logical_not(own_tile))
        def _():
            pltpu.make_async_remote_copy(
                src_ref=tsend.at[dest], dst_ref=tfin.at[s],
                send_sem=vs_sems.at[0], recv_sem=vs_sems.at[1],
                device_id=(to, y * 2 + core), device_id_type=MESH,
            ).start()

        return 0

    lax.fori_loop(0, 32, send_tile, 0)

    def first_tile(at_b):
        return pl.multiple_of(jnp.minimum(lax.div(at_b * 48, 128), 4) * 128, 128)

    @pl.when(in_half == c)
    def _():
        bulk_wait(grecv.at[others], gs_sems.at[1])
        sum_s = grecv[0].astype(F32)
        for j in range(1, STORE):
            sum_s = sum_s + grecv[j].astype(F32)
        hsend[...] = sum_s.astype(BF16)
        gfin[y] = hsend[:, pl.ds(first_tile(b), 256)]

        def send_rows(k, _):
            to = lax.rem(b + k, 2 * RING)
            pltpu.make_async_remote_copy(
                src_ref=hsend.at[:, pl.ds(first_tile(to), 256)], dst_ref=gfin.at[y],
                send_sem=gy_sems.at[0], recv_sem=gy_sems.at[1],
                device_id=(s, to), device_id_type=MESH,
            ).start()
            return 0

        lax.fori_loop(1, 2 * RING, send_rows, 0)

    bulk_wait(parr.at[others], push_sems.at[1])
    arrived = parr[...].reshape(STORE * 16, 256)
    for u in range(3):
        newh_ref[:, u * 256 : (u + 1) * 256] = mm(nsel[u], arrived).astype(BF16)

    def cut(x, width, offset):
        pick = onehot(
            (iota((width, 128), 0) == iota((width, 128), 1) + offset) & (iota((width, 128), 1) < 48)
        )
        high = x.astype(BF16)
        low = (x - high.astype(F32)).astype(BF16)
        return mm(high, pick) + mm(low, pick)

    @pl.when(in_half == c)
    def _():
        bulk_wait(gfin.at[pl.ds(0, RING - 1)], gy_sems.at[1])
        bulk_wait(tfin.at[others], vs_sems.at[1])

    @pl.when(in_half != c)
    def _():
        bulk_wait(gfin, gy_sems.at[1])
        bulk_wait(tfin, vs_sems.at[1])

    sum_g = gfin[0].astype(F32)
    for j in range(1, RING):
        sum_g = sum_g + gfin[j].astype(F32)
    grad_ref[0:16] = cut(sum_g, 256, b * 48 - first_tile(b))
    sum_v = tfin[0].astype(F32)
    for j in range(1, STORE):
        sum_v = sum_v + tfin[j].astype(F32)
    grad_ref[16:32] = cut(sum_v, 128, c * 48)

    bulk_wait(req_src.at[others], req_sems.at[0])
    for p in range(3):
        bulk_wait(found.at[p, others], pull_send.at[p])
    bulk_wait(psend.at[others], push_sems.at[0])
    cot_copy.wait_send()
    for copy in sent:
        copy.wait_send()
    gated_copy.wait_send()
    bulk_wait(vsend.at[pl.ds(0, RING - 1)], vy_sems.at[0])

    @pl.when(in_half == c)
    def _():
        bulk_wait(gsend.at[pl.ds(0, 15)], gs_sems.at[0])
        bulk_wait(psend.at[pl.ds(0, 15)], gy_sems.at[0])
        bulk_wait(tfin.at[others], vs_sems.at[0])

    @pl.when(in_half != c)
    def _():
        bulk_wait(gsend, gs_sems.at[0])
        bulk_wait(tfin, vs_sems.at[0])


def on_device(
    node_features, history, requests, neighbours, pattern, push_owner, push_slot,
    w_query, w_key, w_value, w_gate, w_out, cotangent,
):
    vmem = pl.BlockSpec(memory_space=pltpu.VMEM)
    hbm = pl.BlockSpec(memory_space=pltpu.HBM)
    out, newh, grads = pl.pallas_call(
        kernel,
        out_shape=(
            jax.ShapeDtypeStruct((128, 768), BF16),
            jax.ShapeDtypeStruct((128, 768), BF16),
            jax.ShapeDtypeStruct((32, 128), F32),
        ),
        in_specs=[hbm] * 13,
        out_specs=(vmem, vmem, vmem),
        scratch_shapes=[
            pltpu.VMEM((128, 768), BF16),
            pltpu.VMEM((128, 768), F32),
            pltpu.VMEM((8, STORE), I32),
            pltpu.VMEM((16, 128), I32),
            pltpu.VMEM((16, 16), I32),
            pltpu.VMEM((1, 128), I32),
            pltpu.VMEM((4, STORE), I32),
            pltpu.VMEM((768, 256), BF16),
            pltpu.VMEM((768, 256), BF16),
            pltpu.VMEM((768, 256), BF16),
            pltpu.VMEM((768, 256), BF16),
            pltpu.VMEM((384, 768), BF16),
            pltpu.VMEM((256, 768), BF16),
            pltpu.VMEM((256, 768), BF16),
            pltpu.VMEM((256, 768), BF16),
            pltpu.VMEM((STORE, 1, 128), I32),
            pltpu.VMEM((STORE, 1, 128), I32),
            pltpu.VMEM((3, STORE, 16, 128), BF16),
            pltpu.VMEM((3, STORE, 16, 128), BF16),
            pltpu.VMEM((256, 512), BF16),
            pltpu.VMEM((3, 512, 128), BF16),
            pltpu.VMEM((3, 128, 512), BF16),
            pltpu.VMEM((16, 256), F32),
            pltpu.VMEM((768, 1024), BF16),
            pltpu.VMEM((2048, 768), BF16),
            pltpu.VMEM((3, 256, 256), BF16),
            pltpu.VMEM((3, 2048, 256), BF16),
            pltpu.VMEM((3, 64, 256), F32),
            pltpu.VMEM((8, 256), F32),
            pltpu.VMEM((8, 256), F32),
            pltpu.VMEM((3, 8, 256), F32),
            pltpu.VMEM((192, 256), BF16),
            pltpu.VMEM((192, 256), BF16),
            pltpu.VMEM((2, 192, 128), BF16),
            pltpu.VMEM((192, 128), BF16),
            pltpu.VMEM((STORE, 16, 256), BF16),
            pltpu.VMEM((STORE, 16, 256), BF16),
            pltpu.VMEM((8, 192, 128), BF16),
            pltpu.VMEM((8, 192, 128), BF16),
            pltpu.VMEM((16, 16, 128), BF16),
            pltpu.VMEM((STORE, 16, 128), BF16),
            pltpu.VMEM((16, 16, 768), BF16),
            pltpu.VMEM((STORE, 16, 768), BF16),
            pltpu.VMEM((16, 768), BF16),
            pltpu.VMEM((8, 16, 256), BF16),
            pltpu.SemaphoreType.DMA((6,)),
            pltpu.SemaphoreType.DMA((7,)),
            pltpu.SemaphoreType.DMA((2,)),
            pltpu.SemaphoreType.DMA((2,)),
            pltpu.SemaphoreType.DMA((3,)),
            pltpu.SemaphoreType.DMA((3,)),
            pltpu.SemaphoreType.DMA((48,)),
            pltpu.SemaphoreType.DMA((48,)),
            pltpu.SemaphoreType.DMA((54,)),
            pltpu.SemaphoreType.DMA((54,)),
            pltpu.SemaphoreType.DMA((2,)),
            pltpu.SemaphoreType.DMA((2,)),
            pltpu.SemaphoreType.DMA((2,)),
            pltpu.SemaphoreType.DMA((2,)),
            pltpu.SemaphoreType.DMA((2,)),
            pltpu.SemaphoreType.DMA((2,)),
        ],
        compiler_params=pltpu.CompilerParams(
            collective_id=0, has_side_effects=True, vmem_limit_bytes=60 * 1024 * 1024
        ),
        cost_estimate=pl.CostEstimate(
            flops=7_000_000_000, bytes_accessed=6_000_000, transcendentals=1_600_000
        ),
    )(
        node_features, history, requests.T, neighbours.T, pattern, push_owner.reshape(1, -1),
        push_slot.T,
        cotangent, w_query, w_key, w_value, w_gate, w_out,
    )
    return (
        out,
        newh.astype(F32),
        grads[0:12, 0:48].T,
        grads[16:28, 0:48].T,
    )


def solution(mesh):
    rows = P(("storage", "batch"), None)
    in_specs = (
        rows, rows, rows, rows, P("storage", None), P(("storage", "batch")), rows,
        P(), P(), P(), P(), P(), rows,
    )
    out_specs = (rows, rows, P("batch", "storage"), P("batch", "storage"))
    return jax.shard_map(
        on_device, mesh=mesh, in_specs=in_specs, out_specs=out_specs, check_vma=False
    )
```

```python
import functools

import jax
import jax.numpy as jnp
from jax import lax
from jax.experimental import pallas as pl
from jax.experimental.pallas import tpu as pltpu
from jax.sharding import PartitionSpec as P

F32, BF16, I32 = jnp.float32, jnp.bfloat16, jnp.int32
MESH = pl.DeviceIdType.MESH
STORE = 32
RING = 8
HEADS_CORE = 3
NEG = 1e30


def iota(shape, dim):
    return lax.broadcasted_iota(I32, shape, dim)


def onehot(cond):
    return jnp.where(cond, 1.0, 0.0).astype(BF16)


def mm(a, b):
    return lax.dot_general(a, b, (((1,), (0,)), ((), ())), preferred_element_type=F32)


def mm_nt(a, b):
    return lax.dot_general(a, b, (((1,), (1,)), ((), ())), preferred_element_type=F32)


def mm_tn(a, b):
    return lax.dot_general(a, b, (((0,), (0,)), ((), ())), preferred_element_type=F32)


def kernel(
    nf_hbm, hist_hbm, req_hbm, nbr_hbm, pat_hbm, owner_hbm, slot_hbm,
    cot_hbm, wq_hbm, wk_hbm, wv_hbm, wg_hbm, wo_hbm,
    rows_ref, grad_ref,
    nf_ref, hist_ref, req_ref, nbr_ref, pat_ref, owner_ref, slot_ref,
    wq, wk, wv, wg, wo, wvt, wgt, cot,
    req_src, asked, found, table, mix, psel, nsel, bias_ref, lanes96,
    hid, qm, p_ref, acc_ref, mx_ref, sum_ref, mx_chip, gate_t, bg_t,
    gated, gsib, psend, parr, vsend, vrecv, tsend, tfin, gsend, grecv, hsend, gfin,
    load_sem, small_sem, cot_sems, req_sems, pull_send, pull_recv,
    ring_send, ring_recv, sib_send, sib_recv,
    gated_sems, push_sems, vy_sems, vs_sems, gs_sems, gy_sems,
):
    s = lax.axis_index("storage")
    b = lax.axis_index("batch")
    y = lax.div(b, 2)
    c = lax.rem(b, 2)
    sib = b + 1 - 2 * c
    in_half = lax.div(s, 16)
    win = pl.multiple_of(c * 128, 128)
    c64 = pl.multiple_of(c * 64, 64)

    small = [
        pltpu.make_async_copy(src, dst, small_sem.at[i])
        for i, (src, dst) in enumerate((
            (req_hbm, req_ref), (hist_hbm, hist_ref), (nbr_hbm, nbr_ref), (owner_hbm, owner_ref),
            (slot_hbm, slot_ref), (pat_hbm, pat_ref), (nf_hbm, nf_ref),
        ))
    ]
    for copy in small:
        copy.start()
    loads = [
        pltpu.make_async_copy(src.at[:, pl.ds(win, 256)], dst, load_sem.at[i])
        for i, (src, dst) in enumerate(((wq_hbm, wq), (wk_hbm, wk), (wv_hbm, wv), (wg_hbm, wg)))
    ]
    loads.append(pltpu.make_async_copy(wo_hbm, wo, load_sem.at[4]))
    loads.append(pltpu.make_async_copy(cot_hbm, cot.at[pl.ds(win, 128)], load_sem.at[5]))
    for copy in loads:
        copy.start()

    barrier = pltpu.get_barrier_semaphore()

    def greet_store(k, _):
        peer = lax.rem(s + k, STORE)
        pl.semaphore_signal(barrier, inc=1, device_id=(peer, b), device_id_type=MESH)
        pl.semaphore_signal(barrier, inc=1, device_id=(peer, sib), device_id_type=MESH)
        return 0

    lax.fori_loop(1, STORE, greet_store, 0)

    def greet_ring(k, _):
        peer = lax.rem(b + k, 2 * RING)
        pl.semaphore_signal(barrier, inc=1, device_id=(s, peer), device_id_type=MESH)
        return 0

    lax.fori_loop(1, 2 * RING, greet_ring, 0)

    small[0].wait()
    eye8 = onehot(iota((8, 128), 0) == iota((8, 128), 1))
    req_src[...] = mm_tn(req_ref[...].astype(F32).astype(BF16), eye8).astype(I32).reshape(STORE, 1, 128)
    for copy in small[1:]:
        copy.wait()
    nbr = nbr_ref[...]
    at = iota((256, 128), 0)
    count = jnp.zeros((256, 128), F32)
    for k in range(16):
        count = count + jnp.where(nbr[k : k + 1, :] == at, 1.0, 0.0)
    count = count.astype(BF16)
    src_i = iota((256, 512), 0)
    dst_i = iota((256, 512), 1)
    home = src_i + (src_i & -8)
    mix[0:128] = mm_tn(count, onehot(dst_i == home)).astype(BF16)
    mix[128:256] = mm_tn(count, onehot(dst_i == home + 8)).astype(BF16)

    owner_row = owner_ref[...]
    i0 = iota((128, 128), 0)
    i1 = iota((128, 128), 1)
    owner_all = jnp.broadcast_to(owner_row, (128, 128))
    owner_col = jnp.sum(jnp.where(i0 == i1, owner_all, 0), axis=1, keepdims=True)
    rank = jnp.sum(
        jnp.where((owner_col == owner_all) & (i0 < i1), 1, 0), axis=0, keepdims=True
    )
    pos = owner_row * 4 + rank
    pr = iota((512, 128), 0)
    place = ((pr >> 4) << 2) + (pr & 3) == pos
    for u in range(3):
        psel[u] = onehot(place & (((pr >> 2) & 3) == u))
    sel = onehot(iota((STORE, 512), 0) == (iota((STORE, 512), 1) >> 4))
    wide = mm(slot_ref[...].astype(F32).astype(BF16), sel)
    slot_row = jnp.sum(
        jnp.where(iota((4, 512), 0) == (iota((4, 512), 1) & 3), wide, 0.0), axis=0, keepdims=True
    ).astype(I32)
    col = iota((128, 512), 1)
    lands = iota((128, 512), 0) == slot_row
    for u in range(3):
        nsel[u] = onehot(lands & (((col >> 2) & 3) == u))

    qsel = onehot(iota((16, 256), 0) == 2 * y + (iota((16, 256), 1) >> 7))
    seen = mm_tn(pat_ref[...].astype(F32).astype(BF16), qsel)
    bias_ref[...] = (seen - 1.0) * NEG
    mx_ref[...] = jnp.full_like(mx_ref, -2.0 * NEG)
    sum_ref[...] = jnp.zeros_like(sum_ref)
    acc_ref[...] = jnp.zeros_like(acc_ref)
    pl.semaphore_wait(barrier, 2 * (STORE - 1) + 2 * RING - 1)

    def store_copy(src, dst, send_sem, recv_sem, peer):
        return pltpu.make_async_remote_copy(
            src_ref=src, dst_ref=dst, send_sem=send_sem, recv_sem=recv_sem,
            device_id=(peer, b), device_id_type=MESH,
        )

    def send_all(src, dst, send_sem, recv_sem):
        def body(k, _):
            peer = lax.rem(s + k, STORE)
            store_copy(src.at[peer], dst.at[s], send_sem, recv_sem, peer).start()
            return 0

        lax.fori_loop(1, STORE, body, 0)

    def bulk_wait(ref, sem):
        pltpu.make_async_copy(ref, ref, sem).wait()

    others = pl.ds(0, STORE - 1)

    send_all(req_src, asked, req_sems.at[0], req_sems.at[1])
    asked[s] = req_src[s]
    cot_copy = pltpu.make_async_remote_copy(
        src_ref=cot_hbm, dst_ref=cot.at[pl.ds(win, 128)],
        send_sem=cot_sems.at[0], recv_sem=cot_sems.at[1],
        device_id=(s, sib), device_id_type=MESH,
    )
    cot_copy.start()

    hist_b = hist_ref[...].astype(BF16)
    hist_l = jnp.concatenate([hist_b[:, p * 256 : p * 256 + 128] for p in range(3)], axis=1)
    hist_r = jnp.concatenate([hist_b[:, p * 256 + 128 : p * 256 + 256] for p in range(3)], axis=1)
    rep = onehot(iota((STORE * 16, STORE), 1) == (iota((STORE * 16, STORE), 0) >> 4))
    for copy in loads:
        copy.wait()
    wvt[...] = wv[...].T
    wgt[...] = wg[...].T
    bulk_wait(asked.at[others], req_sems.at[1])

    asked_f = asked[...].reshape(STORE, 128).astype(F32).astype(BF16)
    spread = mm(rep, asked_f)
    prow = iota((STORE * 16, 128), 0)
    lane = iota((STORE * 16, 128), 1)
    mine = jnp.sum(jnp.where(lane == (prow & 7), spread, 0.0), axis=1, keepdims=True).astype(I32)
    hit = mine == lane
    pick_l = onehot(hit & ((prow & 8) == 0))
    pick_r = onehot(hit & ((prow & 8) != 0))
    rows = (mm(pick_l, hist_l) + mm(pick_r, hist_r)).astype(BF16)
    for p in range(3):
        found[p] = rows[:, p * 128 : (p + 1) * 128].reshape(STORE, 16, 128)
    for p in range(3):
        send_all(found.at[p], table.at[p], pull_send.at[p], pull_recv.at[p])
    for p in range(3):
        table[p, s] = found[p, s]

    lr = iota((768, 1024), 0)
    ll = iota((768, 1024), 1)
    lanes96[...] = onehot((lr == (ll >> 7) * 96 + (ll & 127)) & ((ll & 127) < 96))

    cot_copy.wait_recv()
    wo_mine = pl.multiple_of(c * 192, 64)
    wo_sib = pl.multiple_of((1 - c) * 192, 64)
    bg_t[...] = mm_nt(wo[pl.ds(wo_mine, 192), :], cot[...]).astype(BF16)

    right = lax.rem(y + 1, RING)
    left = lax.rem(y + RING - 1, RING)
    my_rows = pl.multiple_of(b * 128, 128)
    my_chip = pl.multiple_of(y * 256, 256)

    def chip_at(direction, dist):
        return lax.rem(y + (RING - dist if direction == 0 else dist), RING)

    def unit(chip, core, part, half):
        row = pl.multiple_of(chip * 256 + core * 128 + half * 64, 64)
        return hid.at[pl.ds(row, 64), pl.ds(part * 256, 256)]

    def ring_copy(direction, dist, part, half):
        ref = unit(chip_at(direction, dist - 1), c, part, half)
        idx = ((direction * 4 + dist - 1) * 3 + part) * 2 + half
        to = right if direction == 0 else left
        return pltpu.make_async_remote_copy(
            src_ref=ref, dst_ref=ref, send_sem=ring_send.at[idx], recv_sem=ring_recv.at[idx],
            device_id=(s, to * 2 + c), device_id_type=MESH,
        )

    def ring_arrived(direction, dist, part, half):
        ref = unit(chip_at(direction, dist), c, part, half)
        idx = ((direction * 4 + dist - 1) * 3 + part) * 2 + half
        pltpu.make_async_copy(ref, ref, ring_recv.at[idx]).wait()

    def sib_copy(direction, dist, part, half, core):
        ref = unit(chip_at(direction, dist), core, part, half)
        idx = ((direction * 4 + dist - 1) * 3 + part) * 2 + half if dist else 48 + part * 2 + half
        return pltpu.make_async_remote_copy(
            src_ref=ref, dst_ref=ref, send_sem=sib_send.at[idx], recv_sem=sib_recv.at[idx],
            device_id=(s, sib), device_id_type=MESH,
        )

    def halves(direction, dist):
        if dist < 4:
            return (0, 1)
        return (0,) if direction == 0 else (1,)

    sent = []

    def go(copy):
        copy.start()
        sent.append(copy)

    def own(part):
        bulk_wait(table.at[part, others], pull_recv.at[part])
        t = table[part].reshape(STORE * 16, 128)
        mean = mm(mix[...], t) * (1.0 / 16)
        for i in (0, 1):
            col = pl.ds(part * 256 + i * 128, 128)
            hid[pl.ds(my_rows, 128), col] = (
                nf_ref[:, col].astype(F32) + mean[i * 128 : (i + 1) * 128]
            ).astype(BF16)
        for half in (0, 1):
            for direction in (0, 1):
                go(ring_copy(direction, 1, part, half))
        for half in (0, 1):
            go(sib_copy(0, 0, part, half, c))

    def hop(dist, part):
        for half in (0, 1):
            for direction in (0, 1):
                if half not in halves(direction, dist):
                    continue
                ring_arrived(direction, dist, part, half)
                if dist < 4 and half in halves(direction, dist + 1):
                    go(ring_copy(direction, dist + 1, part, half))
                go(sib_copy(direction, dist, part, half, c))

    def wait_sib(direction, dist):
        for part in range(3):
            for half in halves(direction, dist) if dist else (0, 1):
                sib_copy(direction, dist, part, half, 1 - c).wait_recv()

    def process(chip):
        r0 = pl.multiple_of(chip * 256, 256)
        hc = hid[pl.ds(r0, 256), :]
        kc = mm(hc, wk[...]).astype(BF16)
        vt = mm_nt(wvt[pl.ds(c64, 192), :], hc).astype(BF16)
        b0 = bias_ref[pl.ds(2 * chip, 1), :]
        b1 = bias_ref[pl.ds(2 * chip + 1, 1), :]
        for h in range(HEADS_CORE):
            sc = mm_nt(kc, qm[h])
            lo = sc[0:128] + b0
            hi = sc[128:256] + b1
            top = jnp.max(jnp.maximum(lo, hi), axis=0, keepdims=True)
            old = mx_ref[h : h + 1, :]
            new = jnp.maximum(old, top)
            keep = jnp.exp(old - new)
            lo = jnp.exp(lo - new)
            hi = jnp.exp(hi - new)
            mx_ref[h : h + 1, :] = new
            mx_chip[h, pl.ds(chip, 1), :] = new
            sum_ref[h : h + 1, :] = sum_ref[h : h + 1, :] * keep + jnp.sum(lo + hi, axis=0, keepdims=True)
            pb = jnp.concatenate([lo.astype(BF16), hi.astype(BF16)], axis=0)
            p_ref[h, pl.ds(r0, 256), :] = pb
            acc_ref[h] = acc_ref[h] * keep + mm(vt[h * 64 : (h + 1) * 64], pb)

    def near(direction, dist):
        wait_sib(direction, dist)
        process(chip_at(direction, dist))

    own(0)
    own(1)
    hop(1, 0)
    own(2)
    hop(1, 1)
    hop(2, 0)
    wait_sib(0, 0)
    hc_own = hid[pl.ds(my_chip, 256), :]
    q = (mm(hc_own, wq[...]) * 0.125).astype(BF16).astype(F32)
    lq = (iota((256, 256), 1) - c * 64) >> 6
    for h in range(HEADS_CORE):
        qm[h] = jnp.where(lq == h, q, 0.0).astype(BF16)
    hop(1, 2)
    process(y)
    hop(2, 1)
    hop(3, 0)
    near(0, 1)
    hop(2, 2)
    hop(3, 1)
    near(1, 1)
    hop(4, 0)
    hop(3, 2)
    near(0, 2)
    hop(4, 1)
    near(1, 2)
    near(0, 3)
    hop(4, 2)
    gate_t[...] = mm_nt(wgt[pl.ds(c64, 192), :], hid[pl.ds(my_chip, 256), :]).astype(BF16)
    near(1, 3)
    wait_sib(0, 4)
    wait_sib(1, 4)
    process(chip_at(0, 4))

    ones = [1.0 / sum_ref[h : h + 1, :] for h in range(HEADS_CORE)]
    att = jnp.concatenate([acc_ref[h] * ones[h] for h in range(HEADS_CORE)], axis=0)
    att = att.astype(BF16).astype(F32)
    gate = gate_t[...].astype(F32)
    bg = bg_t[...].astype(F32)
    gated_t = (att * gate).astype(BF16)
    for qb in (0, 1):
        gated[qb] = gated_t[:, qb * 128 : (qb + 1) * 128]
    gated_copy = pltpu.make_async_remote_copy(
        src_ref=gated.at[1 - c], dst_ref=gsib, send_sem=gated_sems.at[0],
        recv_sem=gated_sems.at[1], device_id=(s, sib), device_id_type=MESH,
    )
    gated_copy.start()

    e0 = iota((256, 192), 0)
    tile_rows = onehot((iota((256, 192), 1) == (e0 >> 4) * 12 + (e0 & 15)) & ((e0 & 15) < 12))
    gg = mm((bg * att).astype(BF16), hid[pl.ds(my_chip, 256), :]).astype(BF16)
    gsend[...] = mm(tile_rows, gg).astype(BF16).reshape(16, 16, 768)

    def send_gate(i, _):
        to = c * 16 + lax.rem(s + i, 16)
        dest = lax.rem(s + i, 16)

        @pl.when(to == s)
        def _():
            grecv[s] = gsend[dest]

        @pl.when(to != s)
        def _():
            store_copy(gsend.at[dest], grecv.at[s], gs_sems.at[0], gs_sems.at[1], to).start()

        return 0

    lax.fori_loop(0, 16, send_gate, 0)

    back = (bg * gate).astype(BF16).astype(F32)
    backs = [back[h * 64 : (h + 1) * 64] * ones[h] for h in range(HEADS_CORE)]

    def value_part(j, total):
        r0 = pl.multiple_of(j * 256, 256)
        dv = []
        for h in range(HEADS_CORE):
            scale = jnp.exp(mx_chip[h, pl.ds(j, 1), :] - mx_ref[h : h + 1, :])
            dv.append(mm_nt((backs[h] * scale).astype(BF16), p_ref[h, pl.ds(r0, 256), :]))
        return total + mm(jnp.concatenate(dv, axis=0).astype(BF16), hid[pl.ds(r0, 256), :])

    gv = lax.fori_loop(0, RING, value_part, jnp.zeros((192, 768), F32)).astype(BF16)
    gv = mm(gv, lanes96[...])
    tail = jnp.concatenate([gv[144:192, j * 128 : (j + 1) * 128] for j in range(RING)], axis=0)
    tail = tail.astype(BF16)
    lead = iota((128, 128), 0)
    free = iota((128, 128), 1)
    moves = [onehot((free - 96 + 32 * k == lead) & (free >= 96)) for k in range(3)]
    moved = [mm(tail, moves[k]) for k in range(3)]
    for j in range(RING):
        extra = jnp.concatenate([m[j * 48 : (j + 1) * 48] for m in moved], axis=0)
        vsend[j] = (gv[0:144, j * 128 : (j + 1) * 128] + extra).astype(BF16)
    vrecv[y] = vsend[y]

    def send_value(k, _):
        to = lax.rem(y + k, RING)
        pltpu.make_async_remote_copy(
            src_ref=vsend.at[to], dst_ref=vrecv.at[y],
            send_sem=vy_sems.at[0], recv_sem=vy_sems.at[1],
            device_id=(s, to * 2 + c), device_id_type=MESH,
        ).start()
        return 0

    lax.fori_loop(1, RING, send_value, 0)

    gated_copy.wait_recv()
    out = nf_ref[...].astype(F32) + (
        mm_tn(gated[c], wo[pl.ds(wo_mine, 192), :]) + mm_tn(gsib[...], wo[pl.ds(wo_sib, 192), :])
    )
    out_b = out.astype(BF16)
    rows_ref[0] = out_b
    pushed = mm(psel[0], out_b[:, 0:256])
    pushed = pushed + mm(psel[1], out_b[:, 256:512])
    pushed = pushed + mm(psel[2], out_b[:, 512:768])
    psend[...] = pushed.astype(BF16).reshape(STORE, 16, 256)
    send_all(psend, parr, push_sems.at[0], push_sems.at[1])
    parr[s] = psend[s]

    bulk_wait(req_src.at[others], req_sems.at[0])
    for p in range(3):
        bulk_wait(found.at[p, others], pull_send.at[p])
    cot_copy.wait_send()
    for copy in sent:
        copy.wait_send()
    gated_copy.wait_send()

    bulk_wait(vrecv.at[pl.ds(0, RING - 1)], vy_sems.at[1])
    total = vrecv[0].astype(F32)
    for j in range(1, RING):
        total = total + vrecv[j].astype(F32)
    total = total.astype(BF16)
    rest = mm_nt(total[0:48], moves[0]) + mm_nt(total[48:96], moves[1]) + mm_nt(total[96:144], moves[2])
    t0 = iota((256, 144), 0)
    rows_a = onehot((iota((256, 144), 1) == (t0 >> 4) * 12 + (t0 & 15)) & ((t0 & 15) < 12))
    t1 = iota((256, 48), 0)
    rows_b = onehot((iota((256, 48), 1) + 144 == (t1 >> 4) * 12 + (t1 & 15)) & ((t1 & 15) < 12))
    tiles = mm(rows_a, total) + mm(rows_b, rest.astype(BF16))
    tsend[...] = tiles.astype(BF16).reshape(16, 16, 128)

    def send_tile(i, _):
        dest = lax.rem(s + lax.div(i, 2), 16)
        core = lax.rem(i, 2)
        to = c * 16 + dest
        own_tile = (to == s) & (core == c)

        @pl.when(own_tile)
        def _():
            tfin[s] = tsend[dest]

        @pl.when(jnp.logical_not(own_tile))
        def _():
            pltpu.make_async_remote_copy(
                src_ref=tsend.at[dest], dst_ref=tfin.at[s],
                send_sem=vs_sems.at[0], recv_sem=vs_sems.at[1],
                device_id=(to, y * 2 + core), device_id_type=MESH,
            ).start()

        return 0

    lax.fori_loop(0, 32, send_tile, 0)

    def first_tile(at_b):
        return pl.multiple_of(jnp.minimum(lax.div(at_b * 48, 128), 4) * 128, 128)

    @pl.when(in_half == c)
    def _():
        bulk_wait(grecv.at[others], gs_sems.at[1])
        sum_s = grecv[0].astype(F32)
        for j in range(1, STORE):
            sum_s = sum_s + grecv[j].astype(F32)
        hsend[...] = sum_s.astype(BF16)
        gfin[y] = hsend[:, pl.ds(first_tile(b), 256)]

        def send_rows(k, _):
            to = lax.rem(b + k, 2 * RING)
            pltpu.make_async_remote_copy(
                src_ref=hsend.at[:, pl.ds(first_tile(to), 256)], dst_ref=gfin.at[y],
                send_sem=gy_sems.at[0], recv_sem=gy_sems.at[1],
                device_id=(s, to), device_id_type=MESH,
            ).start()
            return 0

        lax.fori_loop(1, 2 * RING, send_rows, 0)

    bulk_wait(parr.at[others], push_sems.at[1])
    arrived = parr[...].reshape(STORE * 16, 256)
    for u in range(3):
        rows_ref[1, :, u * 256 : (u + 1) * 256] = mm(nsel[u], arrived).astype(BF16)

    def cut(x, width, offset):
        pick = onehot(
            (iota((width, 128), 0) == iota((width, 128), 1) + offset) & (iota((width, 128), 1) < 48)
        )
        high = x.astype(BF16)
        low = (x - high.astype(F32)).astype(BF16)
        return mm(high, pick) + mm(low, pick)

    @pl.when(in_half == c)
    def _():
        bulk_wait(gfin.at[pl.ds(0, RING - 1)], gy_sems.at[1])

    @pl.when(in_half != c)
    def _():
        bulk_wait(gfin, gy_sems.at[1])

    sum_g = gfin[0].astype(F32)
    for j in range(1, RING):
        sum_g = sum_g + gfin[j].astype(F32)
    grad_ref[0:16] = cut(sum_g, 256, b * 48 - first_tile(b))

    @pl.when(in_half == c)
    def _():
        bulk_wait(tfin.at[others], vs_sems.at[1])

    @pl.when(in_half != c)
    def _():
        bulk_wait(tfin, vs_sems.at[1])

    sum_v = tfin[0].astype(F32)
    for j in range(1, STORE):
        sum_v = sum_v + tfin[j].astype(F32)
    grad_ref[16:32] = cut(sum_v, 128, c * 48)

    bulk_wait(vsend.at[pl.ds(0, RING - 1)], vy_sems.at[0])
    bulk_wait(psend.at[others], push_sems.at[0])

    @pl.when(in_half == c)
    def _():
        bulk_wait(gsend.at[pl.ds(0, 15)], gs_sems.at[0])
        bulk_wait(psend.at[pl.ds(0, 15)], gy_sems.at[0])
        bulk_wait(tfin.at[others], vs_sems.at[0])

    @pl.when(in_half != c)
    def _():
        bulk_wait(gsend, gs_sems.at[0])
        bulk_wait(tfin, vs_sems.at[0])


def on_device(
    node_features, history, requests, neighbours, pattern, push_owner, push_slot,
    w_query, w_key, w_value, w_gate, w_out, cotangent,
):
    vmem = pl.BlockSpec(memory_space=pltpu.VMEM)
    hbm = pl.BlockSpec(memory_space=pltpu.HBM)
    both, grads = pl.pallas_call(
        kernel,
        out_shape=(
            pltpu.VMEM((2, 128, 768), BF16),
            pltpu.VMEM((32, 128), F32),
        ),
        in_specs=[hbm] * 13,
        out_specs=(vmem, vmem),
        scratch_shapes=[
            pltpu.VMEM((128, 768), BF16),
            pltpu.VMEM((128, 768), F32),
            pltpu.VMEM((8, STORE), I32),
            pltpu.VMEM((16, 128), I32),
            pltpu.VMEM((16, 16), I32),
            pltpu.VMEM((1, 128), I32),
            pltpu.VMEM((4, STORE), I32),
            pltpu.VMEM((768, 256), BF16),
            pltpu.VMEM((768, 256), BF16),
            pltpu.VMEM((768, 256), BF16),
            pltpu.VMEM((768, 256), BF16),
            pltpu.VMEM((384, 768), BF16),
            pltpu.VMEM((256, 768), BF16),
            pltpu.VMEM((256, 768), BF16),
            pltpu.VMEM((256, 768), BF16),
            pltpu.VMEM((STORE, 1, 128), I32),
            pltpu.VMEM((STORE, 1, 128), I32),
            pltpu.VMEM((3, STORE, 16, 128), BF16),
            pltpu.VMEM((3, STORE, 16, 128), BF16),
            pltpu.VMEM((256, 512), BF16),
            pltpu.VMEM((3, 512, 128), BF16),
            pltpu.VMEM((3, 128, 512), BF16),
            pltpu.VMEM((16, 256), F32),
            pltpu.VMEM((768, 1024), BF16),
            pltpu.VMEM((2048, 768), BF16),
            pltpu.VMEM((3, 256, 256), BF16),
            pltpu.VMEM((3, 2048, 256), BF16),
            pltpu.VMEM((3, 64, 256), F32),
            pltpu.VMEM((8, 256), F32),
            pltpu.VMEM((8, 256), F32),
            pltpu.VMEM((3, 8, 256), F32),
            pltpu.VMEM((192, 256), BF16),
            pltpu.VMEM((192, 256), BF16),
            pltpu.VMEM((2, 192, 128), BF16),
            pltpu.VMEM((192, 128), BF16),
            pltpu.VMEM((STORE, 16, 256), BF16),
            pltpu.VMEM((STORE, 16, 256), BF16),
            pltpu.VMEM((8, 144, 128), BF16),
            pltpu.VMEM((8, 144, 128), BF16),
            pltpu.VMEM((16, 16, 128), BF16),
            pltpu.VMEM((STORE, 16, 128), BF16),
            pltpu.VMEM((16, 16, 768), BF16),
            pltpu.VMEM((STORE, 16, 768), BF16),
            pltpu.VMEM((16, 768), BF16),
            pltpu.VMEM((8, 16, 256), BF16),
            pltpu.SemaphoreType.DMA((6,)),
            pltpu.SemaphoreType.DMA((7,)),
            pltpu.SemaphoreType.DMA((2,)),
            pltpu.SemaphoreType.DMA((2,)),
            pltpu.SemaphoreType.DMA((3,)),
            pltpu.SemaphoreType.DMA((3,)),
            pltpu.SemaphoreType.DMA((48,)),
            pltpu.SemaphoreType.DMA((48,)),
            pltpu.SemaphoreType.DMA((54,)),
            pltpu.SemaphoreType.DMA((54,)),
            pltpu.SemaphoreType.DMA((2,)),
            pltpu.SemaphoreType.DMA((2,)),
            pltpu.SemaphoreType.DMA((2,)),
            pltpu.SemaphoreType.DMA((2,)),
            pltpu.SemaphoreType.DMA((2,)),
            pltpu.SemaphoreType.DMA((2,)),
        ],
        compiler_params=pltpu.CompilerParams(
            collective_id=0, has_side_effects=True, vmem_limit_bytes=60 * 1024 * 1024
        ),
        cost_estimate=pl.CostEstimate(
            flops=7_000_000_000, bytes_accessed=6_000_000, transcendentals=1_600_000
        ),
    )(
        node_features, history, requests.T, neighbours.T, pattern, push_owner.reshape(1, -1),
        push_slot.T,
        cotangent, w_query, w_key, w_value, w_gate, w_out,
    )
    return (
        both[0],
        both[1].astype(F32),
        grads[0:12, 0:48].T,
        grads[16:28, 0:48].T,
    )


def solution(mesh):
    rows = P(("storage", "batch"), None)
    in_specs = (
        rows, rows, rows, rows, P("storage", None), P(("storage", "batch")), rows,
        P(), P(), P(), P(), P(), rows,
    )
    out_specs = (rows, rows, P("batch", "storage"), P("batch", "storage"))
    return jax.shard_map(
        on_device, mesh=mesh, in_specs=in_specs, out_specs=out_specs, check_vma=False
    )
```

```python
import functools

import jax
import jax.numpy as jnp
from jax import lax
from jax.experimental import pallas as pl
from jax.experimental.pallas import tpu as pltpu
from jax.sharding import PartitionSpec as P

F32, BF16, I32 = jnp.float32, jnp.bfloat16, jnp.int32
MESH = pl.DeviceIdType.MESH
STORE = 32
RING = 8
HEADS_CORE = 3
NEG = 1e30


def iota(shape, dim):
    return lax.broadcasted_iota(I32, shape, dim)


def onehot(cond):
    return jnp.where(cond, 1.0, 0.0).astype(BF16)


def mm(a, b):
    return lax.dot_general(a, b, (((1,), (0,)), ((), ())), preferred_element_type=F32)


def mm_nt(a, b):
    return lax.dot_general(a, b, (((1,), (1,)), ((), ())), preferred_element_type=F32)


def mm_tn(a, b):
    return lax.dot_general(a, b, (((0,), (0,)), ((), ())), preferred_element_type=F32)


def kernel(
    nf_hbm, hist_hbm, req_hbm, nbr_hbm, pat_hbm, owner_hbm, slot_hbm,
    cot_hbm, wq_hbm, wk_hbm, wv_hbm, wg_hbm, wo_hbm,
    rows_ref, grad_ref,
    nf_ref, hist_ref, req_ref, nbr_ref, pat_ref, owner_ref, slot_ref,
    wq, wk, wv, wg, wo, wvt, wgt, cot,
    req_src, asked, found, table, mix, psel, nsel, bias_ref,
    hid, qm, p_ref, acc_ref, mx_ref, sum_ref, mx_chip, gate_t, bg_t,
    gated, gsib, psend, parr, vsend, vrecv, tsend, tfin, gsend, grecv, hsend, gfin,
    tile_rows, rows_a, rows_b, moves,
    load_sem, small_sem, cot_sems, req_sems, pull_send, pull_recv,
    ring_send, ring_recv, sib_send, sib_recv,
    gated_sems, push_sems, vy_sems, vs_sems, gs_sems, gy_sems,
):
    s = lax.axis_index("storage")
    b = lax.axis_index("batch")
    y = lax.div(b, 2)
    c = lax.rem(b, 2)
    sib = b + 1 - 2 * c
    in_half = lax.div(s, 16)
    win = pl.multiple_of(c * 128, 128)
    c64 = pl.multiple_of(c * 64, 64)

    small = [
        pltpu.make_async_copy(src, dst, small_sem.at[i])
        for i, (src, dst) in enumerate((
            (req_hbm, req_ref), (hist_hbm, hist_ref), (nbr_hbm, nbr_ref), (owner_hbm, owner_ref),
            (slot_hbm, slot_ref), (pat_hbm, pat_ref), (nf_hbm, nf_ref),
        ))
    ]
    for copy in small:
        copy.start()
    loads = [
        pltpu.make_async_copy(src.at[:, pl.ds(win, 256)], dst, load_sem.at[i])
        for i, (src, dst) in enumerate(((wq_hbm, wq), (wk_hbm, wk), (wv_hbm, wv), (wg_hbm, wg)))
    ]
    loads.append(pltpu.make_async_copy(wo_hbm, wo, load_sem.at[4]))
    loads.append(pltpu.make_async_copy(cot_hbm, cot.at[pl.ds(win, 128)], load_sem.at[5]))
    for copy in loads:
        copy.start()

    barrier = pltpu.get_barrier_semaphore()

    def greet_store(k, _):
        peer = lax.rem(s + k, STORE)
        pl.semaphore_signal(barrier, inc=1, device_id=(peer, b), device_id_type=MESH)
        pl.semaphore_signal(barrier, inc=1, device_id=(peer, sib), device_id_type=MESH)
        return 0

    lax.fori_loop(1, STORE, greet_store, 0)

    def greet_ring(k, _):
        peer = lax.rem(b + k, 2 * RING)
        pl.semaphore_signal(barrier, inc=1, device_id=(s, peer), device_id_type=MESH)
        return 0

    lax.fori_loop(1, 2 * RING, greet_ring, 0)

    small[0].wait()
    eye8 = onehot(iota((8, 128), 0) == iota((8, 128), 1))
    req_src[...] = mm_tn(req_ref[...].astype(F32).astype(BF16), eye8).astype(I32).reshape(STORE, 1, 128)
    for copy in small[1:]:
        copy.wait()
    nbr = nbr_ref[...]
    at = iota((256, 128), 0)
    count = jnp.zeros((256, 128), F32)
    for k in range(16):
        count = count + jnp.where(nbr[k : k + 1, :] == at, 1.0, 0.0)
    count = count.astype(BF16)
    src_i = iota((256, 512), 0)
    dst_i = iota((256, 512), 1)
    home = src_i + (src_i & -8)
    mix[0:128] = mm_tn(count, onehot(dst_i == home)).astype(BF16)
    mix[128:256] = mm_tn(count, onehot(dst_i == home + 8)).astype(BF16)

    owner_row = owner_ref[...]
    i0 = iota((128, 128), 0)
    i1 = iota((128, 128), 1)
    owner_all = jnp.broadcast_to(owner_row, (128, 128))
    owner_col = jnp.sum(jnp.where(i0 == i1, owner_all, 0), axis=1, keepdims=True)
    rank = jnp.sum(
        jnp.where((owner_col == owner_all) & (i0 < i1), 1, 0), axis=0, keepdims=True
    )
    pos = owner_row * 4 + rank
    pr = iota((512, 128), 0)
    place = ((pr >> 4) << 2) + (pr & 3) == pos
    for u in range(3):
        psel[u] = onehot(place & (((pr >> 2) & 3) == u))
    sel = onehot(iota((STORE, 512), 0) == (iota((STORE, 512), 1) >> 4))
    wide = mm(slot_ref[...].astype(F32).astype(BF16), sel)
    slot_row = jnp.sum(
        jnp.where(iota((4, 512), 0) == (iota((4, 512), 1) & 3), wide, 0.0), axis=0, keepdims=True
    ).astype(I32)
    col = iota((128, 512), 1)
    lands = iota((128, 512), 0) == slot_row
    for u in range(3):
        nsel[u] = onehot(lands & (((col >> 2) & 3) == u))

    qsel = onehot(iota((16, 256), 0) == 2 * y + (iota((16, 256), 1) >> 7))
    seen = mm_tn(pat_ref[...].astype(F32).astype(BF16), qsel)
    bias_ref[...] = (seen - 1.0) * NEG
    mx_ref[...] = jnp.full_like(mx_ref, -2.0 * NEG)
    sum_ref[...] = jnp.zeros_like(sum_ref)
    acc_ref[...] = jnp.zeros_like(acc_ref)
    pl.semaphore_wait(barrier, 2 * (STORE - 1) + 2 * RING - 1)

    def store_copy(src, dst, send_sem, recv_sem, peer):
        return pltpu.make_async_remote_copy(
            src_ref=src, dst_ref=dst, send_sem=send_sem, recv_sem=recv_sem,
            device_id=(peer, b), device_id_type=MESH,
        )

    def send_all(src, dst, send_sem, recv_sem):
        def body(k, _):
            peer = lax.rem(s + k, STORE)
            store_copy(src.at[peer], dst.at[s], send_sem, recv_sem, peer).start()
            return 0

        lax.fori_loop(1, STORE, body, 0)

    def bulk_wait(ref, sem):
        pltpu.make_async_copy(ref, ref, sem).wait()

    others = pl.ds(0, STORE - 1)

    send_all(req_src, asked, req_sems.at[0], req_sems.at[1])
    asked[s] = req_src[s]
    cot_copy = pltpu.make_async_remote_copy(
        src_ref=cot_hbm, dst_ref=cot.at[pl.ds(win, 128)],
        send_sem=cot_sems.at[0], recv_sem=cot_sems.at[1],
        device_id=(s, sib), device_id_type=MESH,
    )
    cot_copy.start()

    hist_b = hist_ref[...].astype(BF16)
    rep = onehot(iota((STORE * 16, STORE), 1) == (iota((STORE * 16, STORE), 0) >> 4))
    for copy in loads:
        copy.wait()
    wvt[...] = wv[...].T
    wgt[...] = wg[...].T
    bulk_wait(asked.at[others], req_sems.at[1])

    asked_f = asked[...].reshape(STORE, 128).astype(F32).astype(BF16)
    spread = mm(rep, asked_f)
    prow = iota((STORE * 16, 128), 0)
    lane = iota((STORE * 16, 128), 1)
    mine = jnp.sum(jnp.where(lane == (prow & 7), spread, 0.0), axis=1, keepdims=True).astype(I32)
    hit = mine == lane
    pick_l = onehot(hit & ((prow & 8) == 0))
    pick_r = onehot(hit & ((prow & 8) != 0))
    for p in range(3):
        rows = mm(pick_l, hist_b[:, p * 256 : p * 256 + 128])
        rows = rows + mm(pick_r, hist_b[:, p * 256 + 128 : p * 256 + 256])
        found[p] = rows.astype(BF16).reshape(STORE, 16, 128)
        send_all(found.at[p], table.at[p], pull_send.at[p], pull_recv.at[p])
    for p in range(3):
        table[p, s] = found[p, s]


    e0 = iota((256, 192), 0)
    tile_rows[...] = onehot((iota((256, 192), 1) == (e0 >> 4) * 12 + (e0 & 15)) & ((e0 & 15) < 12))
    lead = iota((128, 128), 0)
    free = iota((128, 128), 1)
    for k in range(3):
        moves[k] = onehot((free - 96 + 32 * k == lead) & (free >= 96))
    t0 = iota((256, 144), 0)
    r0 = iota((256, 144), 1)
    col_a = r0 + jnp.where(r0 >= 48, 16, 0) + jnp.where(r0 >= 96, 16, 0)
    rows_a[...] = onehot((col_a == (t0 >> 4) * 12 + (t0 & 15)) & ((t0 & 15) < 12))
    t1 = iota((256, 48), 0)
    r1 = iota((256, 48), 1)
    col_b = (r1 >> 4) * 64 + 48 + (r1 & 15)
    rows_b[...] = onehot((col_b == (t1 >> 4) * 12 + (t1 & 15)) & ((t1 & 15) < 12))
    cot_copy.wait_recv()
    wo_mine = pl.multiple_of(c * 192, 64)
    wo_sib = pl.multiple_of((1 - c) * 192, 64)
    bg_t[...] = mm_nt(wo[pl.ds(wo_mine, 192), :], cot[...]).astype(BF16)

    right = lax.rem(y + 1, RING)
    left = lax.rem(y + RING - 1, RING)
    my_rows = pl.multiple_of(b * 128, 128)
    my_chip = pl.multiple_of(y * 256, 256)

    def chip_at(direction, dist):
        return lax.rem(y + (RING - dist if direction == 0 else dist), RING)

    def unit(chip, core, part, half):
        row = pl.multiple_of(chip * 256 + core * 128 + half * 64, 64)
        return hid.at[pl.ds(row, 64), pl.ds(part * 256, 256)]

    def ring_copy(direction, dist, part, half):
        ref = unit(chip_at(direction, dist - 1), c, part, half)
        idx = ((direction * 4 + dist - 1) * 3 + part) * 2 + half
        to = right if direction == 0 else left
        return pltpu.make_async_remote_copy(
            src_ref=ref, dst_ref=ref, send_sem=ring_send.at[idx], recv_sem=ring_recv.at[idx],
            device_id=(s, to * 2 + c), device_id_type=MESH,
        )

    def ring_arrived(direction, dist, part, half):
        ref = unit(chip_at(direction, dist), c, part, half)
        idx = ((direction * 4 + dist - 1) * 3 + part) * 2 + half
        pltpu.make_async_copy(ref, ref, ring_recv.at[idx]).wait()

    def sib_copy(direction, dist, part, half, core):
        ref = unit(chip_at(direction, dist), core, part, half)
        idx = ((direction * 4 + dist - 1) * 3 + part) * 2 + half if dist else 48 + part * 2 + half
        return pltpu.make_async_remote_copy(
            src_ref=ref, dst_ref=ref, send_sem=sib_send.at[idx], recv_sem=sib_recv.at[idx],
            device_id=(s, sib), device_id_type=MESH,
        )

    def halves(direction, dist):
        if dist < 4:
            return (0, 1)
        return (0,) if direction == 0 else (1,)

    sent = []

    def go(copy):
        copy.start()
        sent.append(copy)

    def own(part):
        bulk_wait(table.at[part, others], pull_recv.at[part])
        t = table[part].reshape(STORE * 16, 128)
        mean = mm(mix[...], t) * (1.0 / 16)
        for i in (0, 1):
            col = pl.ds(part * 256 + i * 128, 128)
            hid[pl.ds(my_rows, 128), col] = (
                nf_ref[:, col].astype(F32) + mean[i * 128 : (i + 1) * 128]
            ).astype(BF16)
        for half in (0, 1):
            for direction in (0, 1):
                go(ring_copy(direction, 1, part, half))
        for half in (0, 1):
            go(sib_copy(0, 0, part, half, c))

    def hop(dist, part):
        for half in (0, 1):
            for direction in (0, 1):
                if half not in halves(direction, dist):
                    continue
                ring_arrived(direction, dist, part, half)
                if dist < 4 and half in halves(direction, dist + 1):
                    go(ring_copy(direction, dist + 1, part, half))
                go(sib_copy(direction, dist, part, half, c))

    def wait_sib(direction, dist):
        for part in range(3):
            for half in halves(direction, dist) if dist else (0, 1):
                sib_copy(direction, dist, part, half, 1 - c).wait_recv()

    def process(chip):
        r0 = pl.multiple_of(chip * 256, 256)
        hc = hid[pl.ds(r0, 256), :]
        kc = mm(hc, wk[...]).astype(BF16)
        vt = mm_nt(wvt[pl.ds(c64, 192), :], hc).astype(BF16)
        b0 = bias_ref[pl.ds(2 * chip, 1), :]
        b1 = bias_ref[pl.ds(2 * chip + 1, 1), :]
        for h in range(HEADS_CORE):
            sc = mm_nt(kc, qm[h])
            lo = sc[0:128] + b0
            hi = sc[128:256] + b1
            top = jnp.max(jnp.maximum(lo, hi), axis=0, keepdims=True)
            old = mx_ref[h : h + 1, :]
            new = jnp.maximum(old, top)
            keep = jnp.exp(old - new)
            lo = jnp.exp(lo - new)
            hi = jnp.exp(hi - new)
            mx_ref[h : h + 1, :] = new
            mx_chip[h, pl.ds(chip, 1), :] = new
            sum_ref[h : h + 1, :] = sum_ref[h : h + 1, :] * keep + jnp.sum(lo + hi, axis=0, keepdims=True)
            pb = jnp.concatenate([lo.astype(BF16), hi.astype(BF16)], axis=0)
            p_ref[h, pl.ds(r0, 256), :] = pb
            acc_ref[h] = acc_ref[h] * keep + mm(vt[h * 64 : (h + 1) * 64], pb)

    def near(direction, dist):
        wait_sib(direction, dist)
        process(chip_at(direction, dist))

    own(0)
    own(1)
    hop(1, 0)
    own(2)
    hop(1, 1)
    hop(2, 0)
    wait_sib(0, 0)
    hc_own = hid[pl.ds(my_chip, 256), :]
    q = (mm(hc_own, wq[...]) * 0.125).astype(BF16).astype(F32)
    lq = (iota((256, 256), 1) - c * 64) >> 6
    for h in range(HEADS_CORE):
        qm[h] = jnp.where(lq == h, q, 0.0).astype(BF16)
    hop(1, 2)
    process(y)
    gate_t[...] = mm_nt(wgt[pl.ds(c64, 192), :], hid[pl.ds(my_chip, 256), :]).astype(BF16)
    hop(2, 1)
    hop(3, 0)
    near(0, 1)
    hop(2, 2)
    hop(3, 1)
    near(1, 1)
    hop(4, 0)
    hop(3, 2)
    near(0, 2)
    hop(4, 1)
    near(1, 2)
    near(0, 3)
    hop(4, 2)
    near(1, 3)
    wait_sib(0, 4)
    wait_sib(1, 4)
    process(chip_at(0, 4))

    ones = [1.0 / sum_ref[h : h + 1, :] for h in range(HEADS_CORE)]
    att = jnp.concatenate([acc_ref[h] * ones[h] for h in range(HEADS_CORE)], axis=0)
    att = att.astype(BF16).astype(F32)
    gate = gate_t[...].astype(F32)
    bg = bg_t[...].astype(F32)
    gated_t = (att * gate).astype(BF16)
    for qb in (0, 1):
        gated[qb] = gated_t[:, qb * 128 : (qb + 1) * 128]
    gated_copy = pltpu.make_async_remote_copy(
        src_ref=gated.at[1 - c], dst_ref=gsib, send_sem=gated_sems.at[0],
        recv_sem=gated_sems.at[1], device_id=(s, sib), device_id_type=MESH,
    )
    gated_copy.start()

    gg = mm((bg * att).astype(BF16), hid[pl.ds(my_chip, 256), :]).astype(BF16)
    gsend[...] = mm(tile_rows[...], gg).astype(BF16).reshape(16, 16, 768)

    def send_gate(i, _):
        to = c * 16 + lax.rem(s + i, 16)
        dest = lax.rem(s + i, 16)

        @pl.when(to == s)
        def _():
            grecv[s] = gsend[dest]

        @pl.when(to != s)
        def _():
            store_copy(gsend.at[dest], grecv.at[s], gs_sems.at[0], gs_sems.at[1], to).start()

        return 0

    lax.fori_loop(0, 16, send_gate, 0)

    back = (bg * gate).astype(BF16).astype(F32)
    backs = [back[h * 64 : (h + 1) * 64] * ones[h] for h in range(HEADS_CORE)]

    for h in range(HEADS_CORE):

        def value_part(j, total):
            r0 = pl.multiple_of(j * 256, 256)
            scale = jnp.exp(mx_chip[h, pl.ds(j, 1), :] - mx_ref[h : h + 1, :])
            dv = mm_nt((backs[h] * scale).astype(BF16), p_ref[h, pl.ds(r0, 256), :])
            return total + mm(dv.astype(BF16), hid[pl.ds(r0, 256), :])

        gv = lax.fori_loop(0, RING, value_part, jnp.zeros((64, 768), F32))
        for j in range(RING):
            chunk = gv[:, j * 96 : (j + 1) * 96]
            tail = jnp.concatenate([chunk[48:64, 32 * k : 32 * k + 32] for k in range(3)], axis=0)
            packed = jnp.concatenate([chunk[0:48], tail], axis=1)
            vsend[j, h * 48 : (h + 1) * 48] = packed.astype(BF16)
        vrecv[y, h * 48 : (h + 1) * 48] = vsend[y, h * 48 : (h + 1) * 48]

        def send_value(k, _):
            to = lax.rem(y + k, RING)
            pltpu.make_async_remote_copy(
                src_ref=vsend.at[to, pl.ds(h * 48, 48)], dst_ref=vrecv.at[y, pl.ds(h * 48, 48)],
                send_sem=vy_sems.at[0], recv_sem=vy_sems.at[1],
                device_id=(s, to * 2 + c), device_id_type=MESH,
            ).start()
            return 0

        lax.fori_loop(1, RING, send_value, 0)

    gated_copy.wait_recv()
    out = nf_ref[...].astype(F32) + (
        mm_tn(gated[c], wo[pl.ds(wo_mine, 192), :]) + mm_tn(gsib[...], wo[pl.ds(wo_sib, 192), :])
    )
    out_b = out.astype(BF16)
    rows_ref[0] = out_b
    pushed = mm(psel[0], out_b[:, 0:256])
    pushed = pushed + mm(psel[1], out_b[:, 256:512])
    pushed = pushed + mm(psel[2], out_b[:, 512:768])
    psend[...] = pushed.astype(BF16).reshape(STORE, 16, 256)
    send_all(psend, parr, push_sems.at[0], push_sems.at[1])
    parr[s] = psend[s]

    bulk_wait(req_src.at[others], req_sems.at[0])
    for p in range(3):
        bulk_wait(found.at[p, others], pull_send.at[p])
    cot_copy.wait_send()
    for copy in sent:
        copy.wait_send()
    gated_copy.wait_send()

    bulk_wait(vrecv.at[pl.ds(0, RING - 1)], vy_sems.at[1])
    total = vrecv[0].astype(F32)
    for j in range(1, RING):
        total = total + vrecv[j].astype(F32)
    total = total.astype(BF16)
    rest = jnp.zeros((48, 128), F32)
    for k in range(3):
        part = [total[h * 48 + k * 16 : h * 48 + k * 16 + 16] for h in range(HEADS_CORE)]
        rest = rest + mm_nt(jnp.concatenate(part, axis=0), moves[k])
    tiles = mm(rows_a[...], total) + mm(rows_b[...], rest.astype(BF16))
    tsend[...] = tiles.astype(BF16).reshape(16, 16, 128)

    def send_tile(i, _):
        dest = lax.rem(s + lax.div(i, 2), 16)
        core = lax.rem(i, 2)
        to = c * 16 + dest
        own_tile = (to == s) & (core == c)

        @pl.when(own_tile)
        def _():
            tfin[s] = tsend[dest]

        @pl.when(jnp.logical_not(own_tile))
        def _():
            pltpu.make_async_remote_copy(
                src_ref=tsend.at[dest], dst_ref=tfin.at[s],
                send_sem=vs_sems.at[0], recv_sem=vs_sems.at[1],
                device_id=(to, y * 2 + core), device_id_type=MESH,
            ).start()

        return 0

    lax.fori_loop(0, 32, send_tile, 0)

    def first_tile(at_b):
        return pl.multiple_of(jnp.minimum(lax.div(at_b * 48, 128), 4) * 128, 128)

    @pl.when(in_half == c)
    def _():
        bulk_wait(grecv.at[others], gs_sems.at[1])
        sum_s = grecv[0].astype(F32)
        for j in range(1, STORE):
            sum_s = sum_s + grecv[j].astype(F32)
        hsend[...] = sum_s.astype(BF16)
        gfin[y] = hsend[:, pl.ds(first_tile(b), 256)]

        def send_rows(k, _):
            to = lax.rem(b + k, 2 * RING)
            pltpu.make_async_remote_copy(
                src_ref=hsend.at[:, pl.ds(first_tile(to), 256)], dst_ref=gfin.at[y],
                send_sem=gy_sems.at[0], recv_sem=gy_sems.at[1],
                device_id=(s, to), device_id_type=MESH,
            ).start()
            return 0

        lax.fori_loop(1, 2 * RING, send_rows, 0)

    bulk_wait(parr.at[others], push_sems.at[1])
    arrived = parr[...].reshape(STORE * 16, 256)
    for u in range(3):
        rows_ref[1, :, u * 256 : (u + 1) * 256] = mm(nsel[u], arrived).astype(BF16)

    def cut(x, width, offset):
        pick = onehot(
            (iota((width, 128), 0) == iota((width, 128), 1) + offset) & (iota((width, 128), 1) < 48)
        )
        high = x.astype(BF16)
        low = (x - high.astype(F32)).astype(BF16)
        return mm(high, pick) + mm(low, pick)

    @pl.when(in_half == c)
    def _():
        bulk_wait(gfin.at[pl.ds(0, RING - 1)], gy_sems.at[1])

    @pl.when(in_half != c)
    def _():
        bulk_wait(gfin, gy_sems.at[1])

    sum_g = gfin[0].astype(F32)
    for j in range(1, RING):
        sum_g = sum_g + gfin[j].astype(F32)
    grad_ref[0:16] = cut(sum_g, 256, b * 48 - first_tile(b))

    @pl.when(in_half == c)
    def _():
        bulk_wait(tfin.at[others], vs_sems.at[1])

    @pl.when(in_half != c)
    def _():
        bulk_wait(tfin, vs_sems.at[1])

    sum_v = tfin[0].astype(F32)
    for j in range(1, STORE):
        sum_v = sum_v + tfin[j].astype(F32)
    grad_ref[16:32, 0:48] = jnp.where(c == 0, sum_v[:, 0:48], sum_v[:, 48:96])

    bulk_wait(vsend.at[pl.ds(0, RING - 1)], vy_sems.at[0])
    bulk_wait(psend.at[others], push_sems.at[0])

    @pl.when(in_half == c)
    def _():
        bulk_wait(gsend.at[pl.ds(0, 15)], gs_sems.at[0])
        bulk_wait(psend.at[pl.ds(0, 15)], gy_sems.at[0])
        bulk_wait(tfin.at[others], vs_sems.at[0])

    @pl.when(in_half != c)
    def _():
        bulk_wait(gsend, gs_sems.at[0])
        bulk_wait(tfin, vs_sems.at[0])


def on_device(
    node_features, history, requests, neighbours, pattern, push_owner, push_slot,
    w_query, w_key, w_value, w_gate, w_out, cotangent,
):
    vmem = pl.BlockSpec(memory_space=pltpu.VMEM)
    hbm = pl.BlockSpec(memory_space=pltpu.HBM)
    both, grads = pl.pallas_call(
        kernel,
        out_shape=(
            pltpu.VMEM((2, 128, 768), BF16),
            pltpu.VMEM((32, 128), F32),
        ),
        in_specs=[hbm] * 13,
        out_specs=(vmem, vmem),
        scratch_shapes=[
            pltpu.VMEM((128, 768), BF16),
            pltpu.VMEM((128, 768), F32),
            pltpu.VMEM((8, STORE), I32),
            pltpu.VMEM((16, 128), I32),
            pltpu.VMEM((16, 16), I32),
            pltpu.VMEM((1, 128), I32),
            pltpu.VMEM((4, STORE), I32),
            pltpu.VMEM((768, 256), BF16),
            pltpu.VMEM((768, 256), BF16),
            pltpu.VMEM((768, 256), BF16),
            pltpu.VMEM((768, 256), BF16),
            pltpu.VMEM((384, 768), BF16),
            pltpu.VMEM((256, 768), BF16),
            pltpu.VMEM((256, 768), BF16),
            pltpu.VMEM((256, 768), BF16),
            pltpu.VMEM((STORE, 1, 128), I32),
            pltpu.VMEM((STORE, 1, 128), I32),
            pltpu.VMEM((3, STORE, 16, 128), BF16),
            pltpu.VMEM((3, STORE, 16, 128), BF16),
            pltpu.VMEM((256, 512), BF16),
            pltpu.VMEM((3, 512, 128), BF16),
            pltpu.VMEM((3, 128, 512), BF16),
            pltpu.VMEM((16, 256), F32),
            pltpu.VMEM((2048, 768), BF16),
            pltpu.VMEM((3, 256, 256), BF16),
            pltpu.VMEM((3, 2048, 256), BF16),
            pltpu.VMEM((3, 64, 256), F32),
            pltpu.VMEM((8, 256), F32),
            pltpu.VMEM((8, 256), F32),
            pltpu.VMEM((3, 8, 256), F32),
            pltpu.VMEM((192, 256), BF16),
            pltpu.VMEM((192, 256), BF16),
            pltpu.VMEM((2, 192, 128), BF16),
            pltpu.VMEM((192, 128), BF16),
            pltpu.VMEM((STORE, 16, 256), BF16),
            pltpu.VMEM((STORE, 16, 256), BF16),
            pltpu.VMEM((8, 144, 128), BF16),
            pltpu.VMEM((8, 144, 128), BF16),
            pltpu.VMEM((16, 16, 128), BF16),
            pltpu.VMEM((STORE, 16, 128), BF16),
            pltpu.VMEM((16, 16, 768), BF16),
            pltpu.VMEM((STORE, 16, 768), BF16),
            pltpu.VMEM((16, 768), BF16),
            pltpu.VMEM((8, 16, 256), BF16),
            pltpu.VMEM((256, 192), BF16),
            pltpu.VMEM((256, 144), BF16),
            pltpu.VMEM((256, 48), BF16),
            pltpu.VMEM((3, 128, 128), BF16),
            pltpu.SemaphoreType.DMA((6,)),
            pltpu.SemaphoreType.DMA((7,)),
            pltpu.SemaphoreType.DMA((2,)),
            pltpu.SemaphoreType.DMA((2,)),
            pltpu.SemaphoreType.DMA((3,)),
            pltpu.SemaphoreType.DMA((3,)),
            pltpu.SemaphoreType.DMA((48,)),
            pltpu.SemaphoreType.DMA((48,)),
            pltpu.SemaphoreType.DMA((54,)),
            pltpu.SemaphoreType.DMA((54,)),
            pltpu.SemaphoreType.DMA((2,)),
            pltpu.SemaphoreType.DMA((2,)),
            pltpu.SemaphoreType.DMA((2,)),
            pltpu.SemaphoreType.DMA((2,)),
            pltpu.SemaphoreType.DMA((2,)),
            pltpu.SemaphoreType.DMA((2,)),
        ],
        compiler_params=pltpu.CompilerParams(
            collective_id=0, has_side_effects=True, vmem_limit_bytes=60 * 1024 * 1024
        ),
        cost_estimate=pl.CostEstimate(
            flops=7_000_000_000, bytes_accessed=6_000_000, transcendentals=1_600_000
        ),
    )(
        node_features, history, requests.T, neighbours.T, pattern, push_owner.reshape(1, -1),
        push_slot.T,
        cotangent, w_query, w_key, w_value, w_gate, w_out,
    )
    return (
        both[0],
        both[1].astype(F32),
        grads[0:12, 0:48].T,
        grads[16:28, 0:48].T,
    )


def solution(mesh):
    rows = P(("storage", "batch"), None)
    in_specs = (
        rows, rows, rows, rows, P("storage", None), P(("storage", "batch")), rows,
        P(), P(), P(), P(), P(), rows,
    )
    out_specs = (rows, rows, P("batch", "storage"), P("batch", "storage"))
    return jax.shard_map(
        on_device, mesh=mesh, in_specs=in_specs, out_specs=out_specs, check_vma=False
    )
```

```python
import functools

import jax
import jax.numpy as jnp
from jax import lax
from jax.experimental import pallas as pl
from jax.experimental.pallas import tpu as pltpu
from jax.sharding import PartitionSpec as P

F32, BF16, I32 = jnp.float32, jnp.bfloat16, jnp.int32
MESH = pl.DeviceIdType.MESH
STORE = 32
RING = 8
HEADS_CORE = 3
NEG = 1e30


def iota(shape, dim):
    return lax.broadcasted_iota(I32, shape, dim)


def onehot(cond):
    return jnp.where(cond, 1.0, 0.0).astype(BF16)


def mm(a, b):
    return lax.dot_general(a, b, (((1,), (0,)), ((), ())), preferred_element_type=F32)


def mm_nt(a, b):
    return lax.dot_general(a, b, (((1,), (1,)), ((), ())), preferred_element_type=F32)


def mm_tn(a, b):
    return lax.dot_general(a, b, (((0,), (0,)), ((), ())), preferred_element_type=F32)


def kernel(
    nf_hbm, hist_hbm, req_hbm, nbr_hbm, pat_hbm, owner_hbm, slot_hbm,
    cot_hbm, wq_hbm, wk_hbm, wv_hbm, wg_hbm, wo_hbm,
    rows_ref, grad_ref,
    nf_ref, hist_ref, req_ref, nbr_ref, pat_ref, owner_ref, slot_ref,
    wq, wk, wv, wg, wo, wvt, wgt, cot,
    req_src, asked, found, table, mix, psel, nsel, bias_ref,
    hid, qm, p_ref, acc_ref, mx_ref, sum_ref, mx_chip, gate_t, bg_t,
    gated, gsib, psend, parr, vsend, vrecv, tsend, tfin, gsend, grecv, hsend, gfin,
    tile_rows, rows_a, rows_b, moves, dvt,
    load_sem, small_sem, cot_sems, req_sems, pull_send, pull_recv,
    ring_send, ring_recv, sib_send, sib_recv,
    gated_sems, push_sems, vy_sems, vs_sems, gs_sems, gy_sems,
):
    s = lax.axis_index("storage")
    b = lax.axis_index("batch")
    y = lax.div(b, 2)
    c = lax.rem(b, 2)
    sib = b + 1 - 2 * c
    in_half = lax.div(s, 16)
    win = pl.multiple_of(c * 128, 128)
    c64 = pl.multiple_of(c * 64, 64)

    small = [
        pltpu.make_async_copy(src, dst, small_sem.at[i])
        for i, (src, dst) in enumerate((
            (req_hbm, req_ref), (hist_hbm, hist_ref), (nbr_hbm, nbr_ref), (owner_hbm, owner_ref),
            (slot_hbm, slot_ref), (pat_hbm, pat_ref), (nf_hbm, nf_ref),
        ))
    ]
    for copy in small:
        copy.start()
    loads = [
        pltpu.make_async_copy(src.at[:, pl.ds(win, 256)], dst, load_sem.at[i])
        for i, (src, dst) in enumerate(((wq_hbm, wq), (wk_hbm, wk), (wv_hbm, wv), (wg_hbm, wg)))
    ]
    loads.append(pltpu.make_async_copy(wo_hbm, wo, load_sem.at[4]))
    loads.append(pltpu.make_async_copy(cot_hbm, cot.at[pl.ds(win, 128)], load_sem.at[5]))
    for copy in loads:
        copy.start()

    barrier = pltpu.get_barrier_semaphore()

    def greet_store(k, _):
        peer = lax.rem(s + k, STORE)
        pl.semaphore_signal(barrier, inc=1, device_id=(peer, b), device_id_type=MESH)
        pl.semaphore_signal(barrier, inc=1, device_id=(peer, sib), device_id_type=MESH)
        return 0

    lax.fori_loop(1, STORE, greet_store, 0)

    def greet_ring(k, _):
        peer = lax.rem(b + k, 2 * RING)
        pl.semaphore_signal(barrier, inc=1, device_id=(s, peer), device_id_type=MESH)
        return 0

    lax.fori_loop(1, 2 * RING, greet_ring, 0)

    small[0].wait()
    eye8 = onehot(iota((8, 128), 0) == iota((8, 128), 1))
    req_src[...] = mm_tn(req_ref[...].astype(F32).astype(BF16), eye8).astype(I32).reshape(STORE, 1, 128)
    for copy in small[1:]:
        copy.wait()
    nbr = nbr_ref[...]
    at = iota((256, 128), 0)
    count = jnp.zeros((256, 128), F32)
    for k in range(16):
        count = count + jnp.where(nbr[k : k + 1, :] == at, 1.0, 0.0)
    count = count.astype(BF16)
    src_i = iota((256, 512), 0)
    dst_i = iota((256, 512), 1)
    home = src_i + (src_i & -8)
    mix[0:128] = mm_tn(count, onehot(dst_i == home)).astype(BF16)
    mix[128:256] = mm_tn(count, onehot(dst_i == home + 8)).astype(BF16)

    owner_row = owner_ref[...]
    i0 = iota((128, 128), 0)
    i1 = iota((128, 128), 1)
    owner_all = jnp.broadcast_to(owner_row, (128, 128))
    owner_col = jnp.sum(jnp.where(i0 == i1, owner_all, 0), axis=1, keepdims=True)
    rank = jnp.sum(
        jnp.where((owner_col == owner_all) & (i0 < i1), 1, 0), axis=0, keepdims=True
    )
    pos = owner_row * 4 + rank
    pr = iota((512, 128), 0)
    place = ((pr >> 4) << 2) + (pr & 3) == pos
    for u in range(3):
        psel[u] = onehot(place & (((pr >> 2) & 3) == u))
    sel = onehot(iota((STORE, 512), 0) == (iota((STORE, 512), 1) >> 4))
    wide = mm(slot_ref[...].astype(F32).astype(BF16), sel)
    slot_row = jnp.sum(
        jnp.where(iota((4, 512), 0) == (iota((4, 512), 1) & 3), wide, 0.0), axis=0, keepdims=True
    ).astype(I32)
    col = iota((128, 512), 1)
    lands = iota((128, 512), 0) == slot_row
    for u in range(3):
        nsel[u] = onehot(lands & (((col >> 2) & 3) == u))

    qsel = onehot(iota((16, 256), 0) == 2 * y + (iota((16, 256), 1) >> 7))
    seen = mm_tn(pat_ref[...].astype(F32).astype(BF16), qsel)
    bias_ref[...] = (seen - 1.0) * NEG
    mx_ref[...] = jnp.full_like(mx_ref, -2.0 * NEG)
    sum_ref[...] = jnp.zeros_like(sum_ref)
    acc_ref[...] = jnp.zeros_like(acc_ref)
    pl.semaphore_wait(barrier, 2 * (STORE - 1) + 2 * RING - 1)

    def store_copy(src, dst, send_sem, recv_sem, peer):
        return pltpu.make_async_remote_copy(
            src_ref=src, dst_ref=dst, send_sem=send_sem, recv_sem=recv_sem,
            device_id=(peer, b), device_id_type=MESH,
        )

    def send_all(src, dst, send_sem, recv_sem):
        def body(k, _):
            peer = lax.rem(s + k, STORE)
            store_copy(src.at[peer], dst.at[s], send_sem, recv_sem, peer).start()
            return 0

        lax.fori_loop(1, STORE, body, 0)

    def bulk_wait(ref, sem):
        pltpu.make_async_copy(ref, ref, sem).wait()

    others = pl.ds(0, STORE - 1)

    send_all(req_src, asked, req_sems.at[0], req_sems.at[1])
    asked[s] = req_src[s]
    cot_copy = pltpu.make_async_remote_copy(
        src_ref=cot_hbm, dst_ref=cot.at[pl.ds(win, 128)],
        send_sem=cot_sems.at[0], recv_sem=cot_sems.at[1],
        device_id=(s, sib), device_id_type=MESH,
    )
    cot_copy.start()

    hist_b = hist_ref[...].astype(BF16)
    rep = onehot(iota((STORE * 16, STORE), 1) == (iota((STORE * 16, STORE), 0) >> 4))
    for copy in loads:
        copy.wait()
    wvt[...] = wv[...].T
    wgt[...] = wg[...].T
    bulk_wait(asked.at[others], req_sems.at[1])

    asked_f = asked[...].reshape(STORE, 128).astype(F32).astype(BF16)
    spread = mm(rep, asked_f)
    prow = iota((STORE * 16, 128), 0)
    lane = iota((STORE * 16, 128), 1)
    mine = jnp.sum(jnp.where(lane == (prow & 7), spread, 0.0), axis=1, keepdims=True).astype(I32)
    hit = mine == lane
    pick_l = onehot(hit & ((prow & 8) == 0))
    pick_r = onehot(hit & ((prow & 8) != 0))
    for p in range(3):
        rows = mm(pick_l, hist_b[:, p * 256 : p * 256 + 128])
        rows = rows + mm(pick_r, hist_b[:, p * 256 + 128 : p * 256 + 256])
        found[p] = rows.astype(BF16).reshape(STORE, 16, 128)
        send_all(found.at[p], table.at[p], pull_send.at[p], pull_recv.at[p])
    for p in range(3):
        table[p, s] = found[p, s]

    e0 = iota((256, 192), 0)
    tile_rows[...] = onehot((iota((256, 192), 1) == (e0 >> 4) * 12 + (e0 & 15)) & ((e0 & 15) < 12))
    lead = iota((128, 128), 0)
    free = iota((128, 128), 1)
    for k in range(3):
        moves[k] = onehot((free - 96 + 32 * k == lead) & (free >= 96))
    t0 = iota((256, 144), 0)
    rows_a[...] = onehot((iota((256, 144), 1) == (t0 >> 4) * 12 + (t0 & 15)) & ((t0 & 15) < 12))
    t1 = iota((256, 48), 0)
    rows_b[...] = onehot((iota((256, 48), 1) + 144 == (t1 >> 4) * 12 + (t1 & 15)) & ((t1 & 15) < 12))
    cot_copy.wait_recv()
    wo_mine = pl.multiple_of(c * 192, 64)
    wo_sib = pl.multiple_of((1 - c) * 192, 64)
    bg_t[...] = mm_nt(wo[pl.ds(wo_mine, 192), :], cot[...]).astype(BF16)

    right = lax.rem(y + 1, RING)
    left = lax.rem(y + RING - 1, RING)
    my_rows = pl.multiple_of(b * 128, 128)
    my_chip = pl.multiple_of(y * 256, 256)

    def chip_at(direction, dist):
        return lax.rem(y + (RING - dist if direction == 0 else dist), RING)

    def unit(chip, core, part, half):
        row = pl.multiple_of(chip * 256 + core * 128 + half * 64, 64)
        return hid.at[pl.ds(row, 64), pl.ds(part * 256, 256)]

    def ring_copy(direction, dist, part, half):
        ref = unit(chip_at(direction, dist - 1), c, part, half)
        idx = ((direction * 4 + dist - 1) * 3 + part) * 2 + half
        to = right if direction == 0 else left
        return pltpu.make_async_remote_copy(
            src_ref=ref, dst_ref=ref, send_sem=ring_send.at[idx], recv_sem=ring_recv.at[idx],
            device_id=(s, to * 2 + c), device_id_type=MESH,
        )

    def ring_arrived(direction, dist, part, half):
        ref = unit(chip_at(direction, dist), c, part, half)
        idx = ((direction * 4 + dist - 1) * 3 + part) * 2 + half
        pltpu.make_async_copy(ref, ref, ring_recv.at[idx]).wait()

    def sib_copy(direction, dist, part, half, core):
        ref = unit(chip_at(direction, dist), core, part, half)
        idx = ((direction * 4 + dist - 1) * 3 + part) * 2 + half if dist else 48 + part * 2 + half
        return pltpu.make_async_remote_copy(
            src_ref=ref, dst_ref=ref, send_sem=sib_send.at[idx], recv_sem=sib_recv.at[idx],
            device_id=(s, sib), device_id_type=MESH,
        )

    def halves(direction, dist):
        if dist < 4:
            return (0, 1)
        return (0,) if direction == 0 else (1,)

    sent = []

    def go(copy):
        copy.start()
        sent.append(copy)

    def own(part):
        bulk_wait(table.at[part, others], pull_recv.at[part])
        t = table[part].reshape(STORE * 16, 128)
        mean = mm(mix[...], t) * (1.0 / 16)
        for i in (0, 1):
            col = pl.ds(part * 256 + i * 128, 128)
            hid[pl.ds(my_rows, 128), col] = (
                nf_ref[:, col].astype(F32) + mean[i * 128 : (i + 1) * 128]
            ).astype(BF16)
        for half in (0, 1):
            for direction in (0, 1):
                go(ring_copy(direction, 1, part, half))
        for half in (0, 1):
            go(sib_copy(0, 0, part, half, c))

    def hop(dist, part):
        for half in (0, 1):
            for direction in (0, 1):
                if half not in halves(direction, dist):
                    continue
                ring_arrived(direction, dist, part, half)
                if dist < 4 and half in halves(direction, dist + 1):
                    go(ring_copy(direction, dist + 1, part, half))
                go(sib_copy(direction, dist, part, half, c))

    def wait_sib(direction, dist):
        for part in range(3):
            for half in halves(direction, dist) if dist else (0, 1):
                sib_copy(direction, dist, part, half, 1 - c).wait_recv()

    def process(chip):
        r0 = pl.multiple_of(chip * 256, 256)
        hc = hid[pl.ds(r0, 256), :]
        kc = mm(hc, wk[...]).astype(BF16)
        vt = mm_nt(wvt[pl.ds(c64, 192), :], hc).astype(BF16)
        b0 = bias_ref[pl.ds(2 * chip, 1), :]
        b1 = bias_ref[pl.ds(2 * chip + 1, 1), :]
        for h in range(HEADS_CORE):
            sc = mm_nt(kc, qm[h])
            lo = sc[0:128] + b0
            hi = sc[128:256] + b1
            top = jnp.max(jnp.maximum(lo, hi), axis=0, keepdims=True)
            old = mx_ref[h : h + 1, :]
            new = jnp.maximum(old, top)
            keep = jnp.exp(old - new)
            lo = jnp.exp(lo - new)
            hi = jnp.exp(hi - new)
            mx_ref[h : h + 1, :] = new
            mx_chip[h, pl.ds(chip, 1), :] = new
            sum_ref[h : h + 1, :] = sum_ref[h : h + 1, :] * keep + jnp.sum(lo + hi, axis=0, keepdims=True)
            pb = jnp.concatenate([lo.astype(BF16), hi.astype(BF16)], axis=0)
            p_ref[h, pl.ds(r0, 256), :] = pb
            acc_ref[h] = acc_ref[h] * keep + mm(vt[h * 64 : (h + 1) * 64], pb)

    def near(direction, dist):
        wait_sib(direction, dist)
        process(chip_at(direction, dist))

    own(0)
    own(1)
    hop(1, 0)
    own(2)
    hop(1, 1)
    hop(2, 0)
    wait_sib(0, 0)
    hc_own = hid[pl.ds(my_chip, 256), :]
    q = (mm(hc_own, wq[...]) * 0.125).astype(BF16).astype(F32)
    lq = (iota((256, 256), 1) - c * 64) >> 6
    for h in range(HEADS_CORE):
        qm[h] = jnp.where(lq == h, q, 0.0).astype(BF16)
    hop(1, 2)
    process(y)
    gate_t[...] = mm_nt(wgt[pl.ds(c64, 192), :], hid[pl.ds(my_chip, 256), :]).astype(BF16)
    hop(2, 1)
    hop(3, 0)
    near(0, 1)
    hop(2, 2)
    hop(3, 1)
    near(1, 1)
    hop(4, 0)
    hop(3, 2)
    near(0, 2)
    hop(4, 1)
    near(1, 2)
    near(0, 3)
    hop(4, 2)
    near(1, 3)
    wait_sib(0, 4)
    wait_sib(1, 4)
    process(chip_at(0, 4))

    ones = [1.0 / sum_ref[h : h + 1, :] for h in range(HEADS_CORE)]
    att = jnp.concatenate([acc_ref[h] * ones[h] for h in range(HEADS_CORE)], axis=0)
    att = att.astype(BF16).astype(F32)
    gate = gate_t[...].astype(F32)
    bg = bg_t[...].astype(F32)
    gated_t = (att * gate).astype(BF16)
    for qb in (0, 1):
        gated[qb] = gated_t[:, qb * 128 : (qb + 1) * 128]
    gated_copy = pltpu.make_async_remote_copy(
        src_ref=gated.at[1 - c], dst_ref=gsib, send_sem=gated_sems.at[0],
        recv_sem=gated_sems.at[1], device_id=(s, sib), device_id_type=MESH,
    )
    gated_copy.start()

    gg = mm((bg * att).astype(BF16), hid[pl.ds(my_chip, 256), :]).astype(BF16)
    gsend[...] = mm(tile_rows[...], gg).astype(BF16).reshape(16, 16, 768)

    def send_gate(i, _):
        to = c * 16 + lax.rem(s + i, 16)
        dest = lax.rem(s + i, 16)

        @pl.when(to == s)
        def _():
            grecv[s] = gsend[dest]

        @pl.when(to != s)
        def _():
            store_copy(gsend.at[dest], grecv.at[s], gs_sems.at[0], gs_sems.at[1], to).start()

        return 0

    lax.fori_loop(0, 16, send_gate, 0)

    back = (bg * gate).astype(BF16).astype(F32)
    backs = [back[h * 64 : (h + 1) * 64] * ones[h] for h in range(HEADS_CORE)]

    for j in range(RING):
        dv = []
        for h in range(HEADS_CORE):
            scale = jnp.exp(mx_chip[h, j : j + 1, :] - mx_ref[h : h + 1, :])
            dv.append(mm_nt((backs[h] * scale).astype(BF16), p_ref[h, j * 256 : (j + 1) * 256, :]))
        dvt[:, j * 256 : (j + 1) * 256] = jnp.concatenate(dv, axis=0).astype(BF16)
    gv = mm(dvt[...], hid[...])
    for j in range(RING):
        chunk = gv[:, j * 96 : (j + 1) * 96]
        tail = jnp.concatenate([chunk[144:192, 32 * k : 32 * k + 32] for k in range(3)], axis=0)
        vsend[j] = jnp.concatenate([chunk[0:144], tail], axis=1).astype(BF16)
    vrecv[y] = vsend[y]

    def send_value(k, _):
        to = lax.rem(y + k, RING)
        pltpu.make_async_remote_copy(
            src_ref=vsend.at[to], dst_ref=vrecv.at[y],
            send_sem=vy_sems.at[0], recv_sem=vy_sems.at[1],
            device_id=(s, to * 2 + c), device_id_type=MESH,
        ).start()
        return 0

    lax.fori_loop(1, RING, send_value, 0)

    gated_copy.wait_recv()
    out = nf_ref[...].astype(F32) + (
        mm_tn(gated[c], wo[pl.ds(wo_mine, 192), :]) + mm_tn(gsib[...], wo[pl.ds(wo_sib, 192), :])
    )
    out_b = out.astype(BF16)
    rows_ref[0] = out_b
    pushed = mm(psel[0], out_b[:, 0:256])
    pushed = pushed + mm(psel[1], out_b[:, 256:512])
    pushed = pushed + mm(psel[2], out_b[:, 512:768])
    psend[...] = pushed.astype(BF16).reshape(STORE, 16, 256)
    send_all(psend, parr, push_sems.at[0], push_sems.at[1])
    parr[s] = psend[s]

    bulk_wait(req_src.at[others], req_sems.at[0])
    for p in range(3):
        bulk_wait(found.at[p, others], pull_send.at[p])
    cot_copy.wait_send()
    for copy in sent:
        copy.wait_send()
    gated_copy.wait_send()

    bulk_wait(vrecv.at[pl.ds(0, RING - 1)], vy_sems.at[1])
    total = vrecv[0].astype(F32)
    for j in range(1, RING):
        total = total + vrecv[j].astype(F32)
    total = total.astype(BF16)
    rest = mm_nt(total[0:48], moves[0]) + mm_nt(total[48:96], moves[1]) + mm_nt(total[96:144], moves[2])
    tiles = mm(rows_a[...], total) + mm(rows_b[...], rest.astype(BF16))
    tsend[...] = tiles.astype(BF16).reshape(16, 16, 128)

    def send_tile(i, _):
        dest = lax.rem(s + lax.div(i, 2), 16)
        core = lax.rem(i, 2)
        to = c * 16 + dest
        own_tile = (to == s) & (core == c)

        @pl.when(own_tile)
        def _():
            tfin[s] = tsend[dest]

        @pl.when(jnp.logical_not(own_tile))
        def _():
            pltpu.make_async_remote_copy(
                src_ref=tsend.at[dest], dst_ref=tfin.at[s],
                send_sem=vs_sems.at[0], recv_sem=vs_sems.at[1],
                device_id=(to, y * 2 + core), device_id_type=MESH,
            ).start()

        return 0

    lax.fori_loop(0, 32, send_tile, 0)

    def first_tile(at_b):
        return pl.multiple_of(jnp.minimum(lax.div(at_b * 48, 128), 4) * 128, 128)

    @pl.when(in_half == c)
    def _():
        bulk_wait(grecv.at[others], gs_sems.at[1])
        sum_s = grecv[0].astype(F32)
        for j in range(1, STORE):
            sum_s = sum_s + grecv[j].astype(F32)
        hsend[...] = sum_s.astype(BF16)
        gfin[y] = hsend[:, pl.ds(first_tile(b), 256)]

        def send_rows(k, _):
            to = lax.rem(b + k, 2 * RING)
            pltpu.make_async_remote_copy(
                src_ref=hsend.at[:, pl.ds(first_tile(to), 256)], dst_ref=gfin.at[y],
                send_sem=gy_sems.at[0], recv_sem=gy_sems.at[1],
                device_id=(s, to), device_id_type=MESH,
            ).start()
            return 0

        lax.fori_loop(1, 2 * RING, send_rows, 0)

    bulk_wait(parr.at[others], push_sems.at[1])
    arrived = parr[...].reshape(STORE * 16, 256)
    for u in range(3):
        rows_ref[1, :, u * 256 : (u + 1) * 256] = mm(nsel[u], arrived).astype(BF16)

    def cut(x, width, offset):
        pick = onehot(
            (iota((width, 128), 0) == iota((width, 128), 1) + offset) & (iota((width, 128), 1) < 48)
        )
        high = x.astype(BF16)
        low = (x - high.astype(F32)).astype(BF16)
        return mm(high, pick) + mm(low, pick)

    @pl.when(in_half == c)
    def _():
        bulk_wait(gfin.at[pl.ds(0, RING - 1)], gy_sems.at[1])

    @pl.when(in_half != c)
    def _():
        bulk_wait(gfin, gy_sems.at[1])

    sum_g = gfin[0].astype(F32)
    for j in range(1, RING):
        sum_g = sum_g + gfin[j].astype(F32)
    grad_ref[0:16] = cut(sum_g, 256, b * 48 - first_tile(b))

    @pl.when(in_half == c)
    def _():
        bulk_wait(tfin.at[others], vs_sems.at[1])

    @pl.when(in_half != c)
    def _():
        bulk_wait(tfin, vs_sems.at[1])

    sum_v = tfin[0].astype(F32)
    for j in range(1, STORE):
        sum_v = sum_v + tfin[j].astype(F32)
    grad_ref[16:32, 0:48] = jnp.where(c == 0, sum_v[:, 0:48], sum_v[:, 48:96])

    bulk_wait(vsend.at[pl.ds(0, RING - 1)], vy_sems.at[0])
    bulk_wait(psend.at[others], push_sems.at[0])

    @pl.when(in_half == c)
    def _():
        bulk_wait(gsend.at[pl.ds(0, 15)], gs_sems.at[0])
        bulk_wait(psend.at[pl.ds(0, 15)], gy_sems.at[0])
        bulk_wait(tfin.at[others], vs_sems.at[0])

    @pl.when(in_half != c)
    def _():
        bulk_wait(gsend, gs_sems.at[0])
        bulk_wait(tfin, vs_sems.at[0])


def on_device(
    node_features, history, requests, neighbours, pattern, push_owner, push_slot,
    w_query, w_key, w_value, w_gate, w_out, cotangent,
):
    vmem = pl.BlockSpec(memory_space=pltpu.VMEM)
    hbm = pl.BlockSpec(memory_space=pltpu.HBM)
    both, grads = pl.pallas_call(
        kernel,
        out_shape=(
            pltpu.VMEM((2, 128, 768), BF16),
            pltpu.VMEM((32, 128), F32),
        ),
        in_specs=[hbm] * 13,
        out_specs=(vmem, vmem),
        scratch_shapes=[
            pltpu.VMEM((128, 768), BF16),
            pltpu.VMEM((128, 768), F32),
            pltpu.VMEM((8, STORE), I32),
            pltpu.VMEM((16, 128), I32),
            pltpu.VMEM((16, 16), I32),
            pltpu.VMEM((1, 128), I32),
            pltpu.VMEM((4, STORE), I32),
            pltpu.VMEM((768, 256), BF16),
            pltpu.VMEM((768, 256), BF16),
            pltpu.VMEM((768, 256), BF16),
            pltpu.VMEM((768, 256), BF16),
            pltpu.VMEM((384, 768), BF16),
            pltpu.VMEM((256, 768), BF16),
            pltpu.VMEM((256, 768), BF16),
            pltpu.VMEM((256, 768), BF16),
            pltpu.VMEM((STORE, 1, 128), I32),
            pltpu.VMEM((STORE, 1, 128), I32),
            pltpu.VMEM((3, STORE, 16, 128), BF16),
            pltpu.VMEM((3, STORE, 16, 128), BF16),
            pltpu.VMEM((256, 512), BF16),
            pltpu.VMEM((3, 512, 128), BF16),
            pltpu.VMEM((3, 128, 512), BF16),
            pltpu.VMEM((16, 256), F32),
            pltpu.VMEM((2048, 768), BF16),
            pltpu.VMEM((3, 256, 256), BF16),
            pltpu.VMEM((3, 2048, 256), BF16),
            pltpu.VMEM((3, 64, 256), F32),
            pltpu.VMEM((8, 256), F32),
            pltpu.VMEM((8, 256), F32),
            pltpu.VMEM((3, 8, 256), F32),
            pltpu.VMEM((192, 256), BF16),
            pltpu.VMEM((192, 256), BF16),
            pltpu.VMEM((2, 192, 128), BF16),
            pltpu.VMEM((192, 128), BF16),
            pltpu.VMEM((STORE, 16, 256), BF16),
            pltpu.VMEM((STORE, 16, 256), BF16),
            pltpu.VMEM((8, 144, 128), BF16),
            pltpu.VMEM((8, 144, 128), BF16),
            pltpu.VMEM((16, 16, 128), BF16),
            pltpu.VMEM((STORE, 16, 128), BF16),
            pltpu.VMEM((16, 16, 768), BF16),
            pltpu.VMEM((STORE, 16, 768), BF16),
            pltpu.VMEM((16, 768), BF16),
            pltpu.VMEM((8, 16, 256), BF16),
            pltpu.VMEM((256, 192), BF16),
            pltpu.VMEM((256, 144), BF16),
            pltpu.VMEM((256, 48), BF16),
            pltpu.VMEM((3, 128, 128), BF16),
            pltpu.VMEM((192, 2048), BF16),
            pltpu.SemaphoreType.DMA((6,)),
            pltpu.SemaphoreType.DMA((7,)),
            pltpu.SemaphoreType.DMA((2,)),
            pltpu.SemaphoreType.DMA((2,)),
            pltpu.SemaphoreType.DMA((3,)),
            pltpu.SemaphoreType.DMA((3,)),
            pltpu.SemaphoreType.DMA((48,)),
            pltpu.SemaphoreType.DMA((48,)),
            pltpu.SemaphoreType.DMA((54,)),
            pltpu.SemaphoreType.DMA((54,)),
            pltpu.SemaphoreType.DMA((2,)),
            pltpu.SemaphoreType.DMA((2,)),
            pltpu.SemaphoreType.DMA((2,)),
            pltpu.SemaphoreType.DMA((2,)),
            pltpu.SemaphoreType.DMA((2,)),
            pltpu.SemaphoreType.DMA((2,)),
        ],
        compiler_params=pltpu.CompilerParams(
            collective_id=0, has_side_effects=True, vmem_limit_bytes=60 * 1024 * 1024
        ),
        cost_estimate=pl.CostEstimate(
            flops=7_000_000_000, bytes_accessed=6_000_000, transcendentals=1_600_000
        ),
    )(
        node_features, history, requests.T, neighbours.T, pattern, push_owner.reshape(1, -1),
        push_slot.T,
        cotangent, w_query, w_key, w_value, w_gate, w_out,
    )
    return (
        both[0],
        both[1].astype(F32),
        grads[0:12, 0:48].T,
        grads[16:28, 0:48].T,
    )


def solution(mesh):
    rows = P(("storage", "batch"), None)
    in_specs = (
        rows, rows, rows, rows, P("storage", None), P(("storage", "batch")), rows,
        P(), P(), P(), P(), P(), rows,
    )
    out_specs = (rows, rows, P("batch", "storage"), P("batch", "storage"))
    return jax.shard_map(
        on_device, mesh=mesh, in_specs=in_specs, out_specs=out_specs, check_vma=False
    )
```

```python
import functools

import jax
import jax.numpy as jnp
from jax import lax
from jax.experimental import pallas as pl
from jax.experimental.pallas import tpu as pltpu
from jax.sharding import PartitionSpec as P

F32, BF16, I32 = jnp.float32, jnp.bfloat16, jnp.int32
MESH = pl.DeviceIdType.MESH
STORE = 32
RING = 8
HEADS_CORE = 3
NEG = 1e30


def iota(shape, dim):
    return lax.broadcasted_iota(I32, shape, dim)


def onehot(cond):
    return jnp.where(cond, 1.0, 0.0).astype(BF16)


def mm(a, b):
    return lax.dot_general(a, b, (((1,), (0,)), ((), ())), preferred_element_type=F32)


def mm_nt(a, b):
    return lax.dot_general(a, b, (((1,), (1,)), ((), ())), preferred_element_type=F32)


def mm_tn(a, b):
    return lax.dot_general(a, b, (((0,), (0,)), ((), ())), preferred_element_type=F32)


def kernel(
    nf_hbm, hist_hbm, req_hbm, nbr_hbm, pat_hbm, owner_hbm, slot_hbm,
    cot_hbm, wq_hbm, wk_hbm, wv_hbm, wg_hbm, wo_hbm,
    rows_ref, grad_ref,
    nf_ref, hist_ref, req_ref, nbr_ref, pat_ref, owner_ref, slot_ref,
    wq, wk, wv, wg, wo, wvt, wgt, cot,
    req_src, asked, found, table, mix, psel, nsel, bias_ref,
    hid, qm, p_ref, acc_ref, mx_ref, sum_ref, mx_chip, gate_t, bg_t,
    gated, gsib, psend, parr, vsend, vrecv, tsend, tfin, gsend, grecv, hsend, gfin,
    tile_rows, rows_a, rows_b, moves, dvt, odd_rows, unpack,
    load_sem, small_sem, cot_sems, req_sems, pull_send, pull_recv,
    ring_send, ring_recv, sib_send, sib_recv,
    gated_sems, push_sems, vy_sems, vs_sems, gs_sems, gy_sems,
):
    s = lax.axis_index("storage")
    b = lax.axis_index("batch")
    y = lax.div(b, 2)
    c = lax.rem(b, 2)
    sib = b + 1 - 2 * c
    in_half = lax.div(s, 16)
    win = pl.multiple_of(c * 128, 128)
    c64 = pl.multiple_of(c * 64, 64)

    small = [
        pltpu.make_async_copy(src, dst, small_sem.at[i])
        for i, (src, dst) in enumerate((
            (req_hbm, req_ref), (hist_hbm, hist_ref), (nbr_hbm, nbr_ref), (owner_hbm, owner_ref),
            (slot_hbm, slot_ref), (pat_hbm, pat_ref), (nf_hbm, nf_ref),
        ))
    ]
    for copy in small:
        copy.start()
    loads = [
        pltpu.make_async_copy(src.at[:, pl.ds(win, 256)], dst, load_sem.at[i])
        for i, (src, dst) in enumerate(((wq_hbm, wq), (wk_hbm, wk), (wv_hbm, wv), (wg_hbm, wg)))
    ]
    loads.append(pltpu.make_async_copy(wo_hbm, wo, load_sem.at[4]))
    loads.append(pltpu.make_async_copy(cot_hbm, cot.at[pl.ds(win, 128)], load_sem.at[5]))
    for copy in loads:
        copy.start()

    barrier = pltpu.get_barrier_semaphore()

    def greet_store(k, _):
        peer = lax.rem(s + k, STORE)
        pl.semaphore_signal(barrier, inc=1, device_id=(peer, b), device_id_type=MESH)
        pl.semaphore_signal(barrier, inc=1, device_id=(peer, sib), device_id_type=MESH)
        return 0

    lax.fori_loop(1, STORE, greet_store, 0)

    def greet_ring(k, _):
        peer = lax.rem(b + k, 2 * RING)
        pl.semaphore_signal(barrier, inc=1, device_id=(s, peer), device_id_type=MESH)
        return 0

    lax.fori_loop(1, 2 * RING, greet_ring, 0)

    small[0].wait()
    eye8 = onehot(iota((8, 128), 0) == iota((8, 128), 1))
    req_src[...] = mm_tn(req_ref[...].astype(F32).astype(BF16), eye8).astype(I32).reshape(STORE, 1, 128)
    for copy in small[1:]:
        copy.wait()
    nbr = nbr_ref[...]
    at = iota((256, 128), 0)
    count = jnp.zeros((256, 128), F32)
    for k in range(16):
        count = count + jnp.where(nbr[k : k + 1, :] == at, 1.0, 0.0)
    count = count.astype(BF16)
    src_i = iota((256, 512), 0)
    dst_i = iota((256, 512), 1)
    home = src_i + (src_i & -8)
    mix[0:128] = mm_tn(count, onehot(dst_i == home)).astype(BF16)
    mix[128:256] = mm_tn(count, onehot(dst_i == home + 8)).astype(BF16)

    owner_row = owner_ref[...]
    i0 = iota((128, 128), 0)
    i1 = iota((128, 128), 1)
    owner_all = jnp.broadcast_to(owner_row, (128, 128))
    owner_col = jnp.sum(jnp.where(i0 == i1, owner_all, 0), axis=1, keepdims=True)
    rank = jnp.sum(
        jnp.where((owner_col == owner_all) & (i0 < i1), 1, 0), axis=0, keepdims=True
    )
    pos = owner_row * 4 + rank
    pr = iota((512, 128), 0)
    place = ((pr >> 4) << 2) + (pr & 3) == pos
    for u in range(3):
        psel[u] = onehot(place & (((pr >> 2) & 3) == u))
    sel = onehot(iota((STORE, 512), 0) == (iota((STORE, 512), 1) >> 4))
    wide = mm(slot_ref[...].astype(F32).astype(BF16), sel)
    slot_row = jnp.sum(
        jnp.where(iota((4, 512), 0) == (iota((4, 512), 1) & 3), wide, 0.0), axis=0, keepdims=True
    ).astype(I32)
    col = iota((128, 512), 1)
    lands = iota((128, 512), 0) == slot_row
    for u in range(3):
        nsel[u] = onehot(lands & (((col >> 2) & 3) == u))

    qsel = onehot(iota((16, 256), 0) == 2 * y + (iota((16, 256), 1) >> 7))
    seen = mm_tn(pat_ref[...].astype(F32).astype(BF16), qsel)
    bias_ref[...] = (seen - 1.0) * NEG
    mx_ref[...] = jnp.full_like(mx_ref, -2.0 * NEG)
    sum_ref[...] = jnp.zeros_like(sum_ref)
    acc_ref[...] = jnp.zeros_like(acc_ref)
    pl.semaphore_wait(barrier, 2 * (STORE - 1) + 2 * RING - 1)

    def store_copy(src, dst, send_sem, recv_sem, peer):
        return pltpu.make_async_remote_copy(
            src_ref=src, dst_ref=dst, send_sem=send_sem, recv_sem=recv_sem,
            device_id=(peer, b), device_id_type=MESH,
        )

    def send_all(src, dst, send_sem, recv_sem):
        def body(k, _):
            peer = lax.rem(s + k, STORE)
            store_copy(src.at[peer], dst.at[s], send_sem, recv_sem, peer).start()
            return 0

        lax.fori_loop(1, STORE, body, 0)

    def bulk_wait(ref, sem):
        pltpu.make_async_copy(ref, ref, sem).wait()

    others = pl.ds(0, STORE - 1)

    send_all(req_src, asked, req_sems.at[0], req_sems.at[1])
    asked[s] = req_src[s]
    cot_copy = pltpu.make_async_remote_copy(
        src_ref=cot_hbm, dst_ref=cot.at[pl.ds(win, 128)],
        send_sem=cot_sems.at[0], recv_sem=cot_sems.at[1],
        device_id=(s, sib), device_id_type=MESH,
    )
    cot_copy.start()

    hist_b = hist_ref[...].astype(BF16)
    rep = onehot(iota((STORE * 16, STORE), 1) == (iota((STORE * 16, STORE), 0) >> 4))
    for copy in loads:
        copy.wait()
    wvt[...] = wv[...].T
    wgt[...] = wg[...].T
    bulk_wait(asked.at[others], req_sems.at[1])

    asked_f = asked[...].reshape(STORE, 128).astype(F32).astype(BF16)
    spread = mm(rep, asked_f)
    prow = iota((STORE * 16, 128), 0)
    lane = iota((STORE * 16, 128), 1)
    mine = jnp.sum(jnp.where(lane == (prow & 7), spread, 0.0), axis=1, keepdims=True).astype(I32)
    hit = mine == lane
    pick_l = onehot(hit & ((prow & 8) == 0))
    pick_r = onehot(hit & ((prow & 8) != 0))
    for p in range(3):
        rows = mm(pick_l, hist_b[:, p * 256 : p * 256 + 128])
        rows = rows + mm(pick_r, hist_b[:, p * 256 + 128 : p * 256 + 256])
        found[p] = rows.astype(BF16).reshape(STORE, 16, 128)
        send_all(found.at[p], table.at[p], pull_send.at[p], pull_recv.at[p])
    for p in range(3):
        table[p, s] = found[p, s]

    e0 = iota((256, 192), 0)
    tile_rows[...] = onehot((iota((256, 192), 1) == (e0 >> 4) * 12 + (e0 & 15)) & ((e0 & 15) < 12))
    e2 = iota((128, 192), 0)
    odd_rows[...] = onehot((iota((128, 192), 1) == (e2 >> 3) * 12 + (e2 & 7) + 4) & ((e2 & 7) >= 4))
    ut = iota((16, 80), 0)
    ur = iota((16, 80), 1)
    for u in range(6):
        far = 48 + (u // 2) * 8 + (u % 2) * 4 - 8
        unpack[u] = onehot((ur == ut + jnp.where(ut < 8, u * 8, far)) & (ut < 12))
    lead = iota((128, 128), 0)
    free = iota((128, 128), 1)
    for k in range(3):
        moves[k] = onehot((free - 96 + 32 * k == lead) & (free >= 96))
    t0 = iota((256, 144), 0)
    rows_a[...] = onehot((iota((256, 144), 1) == (t0 >> 4) * 12 + (t0 & 15)) & ((t0 & 15) < 12))
    t1 = iota((256, 48), 0)
    rows_b[...] = onehot((iota((256, 48), 1) + 144 == (t1 >> 4) * 12 + (t1 & 15)) & ((t1 & 15) < 12))
    cot_copy.wait_recv()
    wo_mine = pl.multiple_of(c * 192, 64)
    wo_sib = pl.multiple_of((1 - c) * 192, 64)
    bg_t[...] = mm_nt(wo[pl.ds(wo_mine, 192), :], cot[...]).astype(BF16)

    right = lax.rem(y + 1, RING)
    left = lax.rem(y + RING - 1, RING)
    my_rows = pl.multiple_of(b * 128, 128)
    my_chip = pl.multiple_of(y * 256, 256)

    def chip_at(direction, dist):
        return lax.rem(y + (RING - dist if direction == 0 else dist), RING)

    def unit(chip, core, part, half):
        row = pl.multiple_of(chip * 256 + core * 128 + half * 64, 64)
        return hid.at[pl.ds(row, 64), pl.ds(part * 256, 256)]

    def ring_copy(direction, dist, part, half):
        ref = unit(chip_at(direction, dist - 1), c, part, half)
        idx = ((direction * 4 + dist - 1) * 3 + part) * 2 + half
        to = right if direction == 0 else left
        return pltpu.make_async_remote_copy(
            src_ref=ref, dst_ref=ref, send_sem=ring_send.at[idx], recv_sem=ring_recv.at[idx],
            device_id=(s, to * 2 + c), device_id_type=MESH,
        )

    def ring_arrived(direction, dist, part, half):
        ref = unit(chip_at(direction, dist), c, part, half)
        idx = ((direction * 4 + dist - 1) * 3 + part) * 2 + half
        pltpu.make_async_copy(ref, ref, ring_recv.at[idx]).wait()

    def sib_copy(direction, dist, part, half, core):
        ref = unit(chip_at(direction, dist), core, part, half)
        idx = ((direction * 4 + dist - 1) * 3 + part) * 2 + half if dist else 48 + part * 2 + half
        return pltpu.make_async_remote_copy(
            src_ref=ref, dst_ref=ref, send_sem=sib_send.at[idx], recv_sem=sib_recv.at[idx],
            device_id=(s, sib), device_id_type=MESH,
        )

    def halves(direction, dist):
        if dist < 4:
            return (0, 1)
        return (0,) if direction == 0 else (1,)

    sent = []

    def go(copy):
        copy.start()
        sent.append(copy)

    def own(part):
        bulk_wait(table.at[part, others], pull_recv.at[part])
        t = table[part].reshape(STORE * 16, 128)
        mean = mm(mix[...], t) * (1.0 / 16)
        for i in (0, 1):
            col = pl.ds(part * 256 + i * 128, 128)
            hid[pl.ds(my_rows, 128), col] = (
                nf_ref[:, col].astype(F32) + mean[i * 128 : (i + 1) * 128]
            ).astype(BF16)
        for half in (0, 1):
            for direction in (0, 1):
                go(ring_copy(direction, 1, part, half))
        for half in (0, 1):
            go(sib_copy(0, 0, part, half, c))

    def hop(dist, part):
        for half in (0, 1):
            for direction in (0, 1):
                if half not in halves(direction, dist):
                    continue
                ring_arrived(direction, dist, part, half)
                if dist < 4 and half in halves(direction, dist + 1):
                    go(ring_copy(direction, dist + 1, part, half))
                go(sib_copy(direction, dist, part, half, c))

    def wait_sib(direction, dist):
        for part in range(3):
            for half in halves(direction, dist) if dist else (0, 1):
                sib_copy(direction, dist, part, half, 1 - c).wait_recv()

    def process(chip):
        r0 = pl.multiple_of(chip * 256, 256)
        hc = hid[pl.ds(r0, 256), :]
        kc = mm(hc, wk[...]).astype(BF16)
        vt = mm_nt(wvt[pl.ds(c64, 192), :], hc).astype(BF16)
        b0 = bias_ref[pl.ds(2 * chip, 1), :]
        b1 = bias_ref[pl.ds(2 * chip + 1, 1), :]
        for h in range(HEADS_CORE):
            sc = mm_nt(kc, qm[h])
            lo = sc[0:128] + b0
            hi = sc[128:256] + b1
            top = jnp.max(jnp.maximum(lo, hi), axis=0, keepdims=True)
            old = mx_ref[h : h + 1, :]
            new = jnp.maximum(old, top)
            keep = jnp.exp(old - new)
            lo = jnp.exp(lo - new)
            hi = jnp.exp(hi - new)
            mx_ref[h : h + 1, :] = new
            mx_chip[h, pl.ds(chip, 1), :] = new
            sum_ref[h : h + 1, :] = sum_ref[h : h + 1, :] * keep + jnp.sum(lo + hi, axis=0, keepdims=True)
            pb = jnp.concatenate([lo.astype(BF16), hi.astype(BF16)], axis=0)
            p_ref[h, pl.ds(r0, 256), :] = pb
            acc_ref[h] = acc_ref[h] * keep + mm(vt[h * 64 : (h + 1) * 64], pb)

    def near(direction, dist):
        wait_sib(direction, dist)
        process(chip_at(direction, dist))

    own(0)
    own(1)
    hop(1, 0)
    own(2)
    hop(1, 1)
    hop(2, 0)
    wait_sib(0, 0)
    hc_own = hid[pl.ds(my_chip, 256), :]
    q = (mm(hc_own, wq[...]) * 0.125).astype(BF16).astype(F32)
    lq = (iota((256, 256), 1) - c * 64) >> 6
    for h in range(HEADS_CORE):
        qm[h] = jnp.where(lq == h, q, 0.0).astype(BF16)
    hop(1, 2)
    process(y)
    gate_t[...] = mm_nt(wgt[pl.ds(c64, 192), :], hid[pl.ds(my_chip, 256), :]).astype(BF16)
    hop(2, 1)
    hop(3, 0)
    near(0, 1)
    hop(2, 2)
    hop(3, 1)
    near(1, 1)
    hop(4, 0)
    hop(3, 2)
    near(0, 2)
    hop(4, 1)
    near(1, 2)
    near(0, 3)
    hop(4, 2)
    near(1, 3)
    wait_sib(0, 4)
    wait_sib(1, 4)
    process(chip_at(0, 4))

    ones = [1.0 / sum_ref[h : h + 1, :] for h in range(HEADS_CORE)]
    att = jnp.concatenate([acc_ref[h] * ones[h] for h in range(HEADS_CORE)], axis=0)
    att = att.astype(BF16).astype(F32)
    gate = gate_t[...].astype(F32)
    bg = bg_t[...].astype(F32)
    gated_t = (att * gate).astype(BF16)
    for qb in (0, 1):
        gated[qb] = gated_t[:, qb * 128 : (qb + 1) * 128]
    gated_copy = pltpu.make_async_remote_copy(
        src_ref=gated.at[1 - c], dst_ref=gsib, send_sem=gated_sems.at[0],
        recv_sem=gated_sems.at[1], device_id=(s, sib), device_id_type=MESH,
    )
    gated_copy.start()

    gg = mm((bg * att).astype(BF16), hid[pl.ds(my_chip, 256), :]).astype(BF16)
    ga = mm(tile_rows[...], gg)
    gb = mm(odd_rows[...], gg)
    for i in range(16):
        packed = [ga[i * 16 : i * 16 + 8, u * 128 : (u + 1) * 128] for u in range(6)]
        for u in range(0, 6, 2):
            even = ga[i * 16 + 8 : i * 16 + 16, u * 128 : (u + 1) * 128]
            packed.append(even + gb[i * 8 : i * 8 + 8, (u + 1) * 128 : (u + 2) * 128])
        packed.append(jnp.zeros((8, 128), F32))
        gsend[i] = jnp.concatenate(packed, axis=0).astype(BF16)

    def send_gate(i, _):
        to = c * 16 + lax.rem(s + i, 16)
        dest = lax.rem(s + i, 16)

        @pl.when(to == s)
        def _():
            grecv[s] = gsend[dest]

        @pl.when(to != s)
        def _():
            store_copy(gsend.at[dest], grecv.at[s], gs_sems.at[0], gs_sems.at[1], to).start()

        return 0

    lax.fori_loop(0, 16, send_gate, 0)

    back = (bg * gate).astype(BF16).astype(F32)
    backs = [back[h * 64 : (h + 1) * 64] * ones[h] for h in range(HEADS_CORE)]

    for j in range(RING):
        dv = []
        for h in range(HEADS_CORE):
            scale = jnp.exp(mx_chip[h, j : j + 1, :] - mx_ref[h : h + 1, :])
            dv.append(mm_nt((backs[h] * scale).astype(BF16), p_ref[h, j * 256 : (j + 1) * 256, :]))
        dvt[:, j * 256 : (j + 1) * 256] = jnp.concatenate(dv, axis=0).astype(BF16)
    gv = mm(dvt[...], hid[...])
    for j in range(RING):
        chunk = gv[:, j * 96 : (j + 1) * 96]
        tail = jnp.concatenate([chunk[144:192, 32 * k : 32 * k + 32] for k in range(3)], axis=0)
        vsend[j] = jnp.concatenate([chunk[0:144], tail], axis=1).astype(BF16)
    vrecv[y] = vsend[y]

    def send_value(k, _):
        to = lax.rem(y + k, RING)
        pltpu.make_async_remote_copy(
            src_ref=vsend.at[to], dst_ref=vrecv.at[y],
            send_sem=vy_sems.at[0], recv_sem=vy_sems.at[1],
            device_id=(s, to * 2 + c), device_id_type=MESH,
        ).start()
        return 0

    lax.fori_loop(1, RING, send_value, 0)

    gated_copy.wait_recv()
    out = nf_ref[...].astype(F32) + (
        mm_tn(gated[c], wo[pl.ds(wo_mine, 192), :]) + mm_tn(gsib[...], wo[pl.ds(wo_sib, 192), :])
    )
    out_b = out.astype(BF16)
    rows_ref[0] = out_b
    pushed = mm(psel[0], out_b[:, 0:256])
    pushed = pushed + mm(psel[1], out_b[:, 256:512])
    pushed = pushed + mm(psel[2], out_b[:, 512:768])
    psend[...] = pushed.astype(BF16).reshape(STORE, 16, 256)
    @pl.when(in_half == c)
    def _():
        bulk_wait(gsend.at[pl.ds(0, 15)], gs_sems.at[0])

    @pl.when(in_half != c)
    def _():
        bulk_wait(gsend, gs_sems.at[0])

    send_all(psend, parr, push_sems.at[0], push_sems.at[1])
    parr[s] = psend[s]

    bulk_wait(req_src.at[others], req_sems.at[0])
    for p in range(3):
        bulk_wait(found.at[p, others], pull_send.at[p])
    cot_copy.wait_send()
    for copy in sent:
        copy.wait_send()
    gated_copy.wait_send()

    bulk_wait(vrecv.at[pl.ds(0, RING - 1)], vy_sems.at[1])
    total = vrecv[0].astype(F32)
    for j in range(1, RING):
        total = total + vrecv[j].astype(F32)
    total = total.astype(BF16)
    rest = mm_nt(total[0:48], moves[0]) + mm_nt(total[48:96], moves[1]) + mm_nt(total[96:144], moves[2])
    tiles = mm(rows_a[...], total) + mm(rows_b[...], rest.astype(BF16))
    tsend[...] = tiles.astype(BF16).reshape(16, 16, 128)

    def send_tile(i, _):
        dest = lax.rem(s + lax.div(i, 2), 16)
        core = lax.rem(i, 2)
        to = c * 16 + dest
        own_tile = (to == s) & (core == c)

        @pl.when(own_tile)
        def _():
            tfin[s] = tsend[dest]

        @pl.when(jnp.logical_not(own_tile))
        def _():
            pltpu.make_async_remote_copy(
                src_ref=tsend.at[dest], dst_ref=tfin.at[s],
                send_sem=vs_sems.at[0], recv_sem=vs_sems.at[1],
                device_id=(to, y * 2 + core), device_id_type=MESH,
            ).start()

        return 0

    lax.fori_loop(0, 32, send_tile, 0)

    def first_tile(at_b):
        return pl.multiple_of(jnp.minimum(lax.div(at_b * 48, 128), 4) * 128, 128)

    @pl.when(in_half == c)
    def _():
        bulk_wait(grecv.at[others], gs_sems.at[1])
        sum_s = grecv[0].astype(F32)
        for j in range(1, STORE):
            sum_s = sum_s + grecv[j].astype(F32)
        sum_s = sum_s.astype(BF16)
        for u in range(6):
            hsend[:, u * 128 : (u + 1) * 128] = mm(unpack[u], sum_s).astype(BF16)
        gfin[y] = hsend[:, pl.ds(first_tile(b), 256)]

        def send_rows(k, _):
            to = lax.rem(b + k, 2 * RING)
            pltpu.make_async_remote_copy(
                src_ref=hsend.at[:, pl.ds(first_tile(to), 256)], dst_ref=gfin.at[y],
                send_sem=gy_sems.at[0], recv_sem=gy_sems.at[1],
                device_id=(s, to), device_id_type=MESH,
            ).start()
            return 0

        lax.fori_loop(1, 2 * RING, send_rows, 0)

    bulk_wait(parr.at[others], push_sems.at[1])
    arrived = parr[...].reshape(STORE * 16, 256)
    for u in range(3):
        rows_ref[1, :, u * 256 : (u + 1) * 256] = mm(nsel[u], arrived).astype(BF16)

    def cut(x, width, offset):
        pick = onehot(
            (iota((width, 128), 0) == iota((width, 128), 1) + offset) & (iota((width, 128), 1) < 48)
        )
        high = x.astype(BF16)
        low = (x - high.astype(F32)).astype(BF16)
        return mm(high, pick) + mm(low, pick)

    @pl.when(in_half == c)
    def _():
        bulk_wait(gfin.at[pl.ds(0, RING - 1)], gy_sems.at[1])

    @pl.when(in_half != c)
    def _():
        bulk_wait(gfin, gy_sems.at[1])

    sum_g = gfin[0].astype(F32)
    for j in range(1, RING):
        sum_g = sum_g + gfin[j].astype(F32)
    grad_ref[0:16] = cut(sum_g, 256, b * 48 - first_tile(b))

    @pl.when(in_half == c)
    def _():
        bulk_wait(tfin.at[others], vs_sems.at[1])

    @pl.when(in_half != c)
    def _():
        bulk_wait(tfin, vs_sems.at[1])

    sum_v = tfin[0].astype(F32)
    for j in range(1, STORE):
        sum_v = sum_v + tfin[j].astype(F32)
    grad_ref[16:32, 0:48] = jnp.where(c == 0, sum_v[:, 0:48], sum_v[:, 48:96])

    bulk_wait(vsend.at[pl.ds(0, RING - 1)], vy_sems.at[0])
    bulk_wait(psend.at[others], push_sems.at[0])

    @pl.when(in_half == c)
    def _():
        bulk_wait(psend.at[pl.ds(0, 15)], gy_sems.at[0])
        bulk_wait(tfin.at[others], vs_sems.at[0])

    @pl.when(in_half != c)
    def _():
        bulk_wait(tfin, vs_sems.at[0])


def on_device(
    node_features, history, requests, neighbours, pattern, push_owner, push_slot,
    w_query, w_key, w_value, w_gate, w_out, cotangent,
):
    vmem = pl.BlockSpec(memory_space=pltpu.VMEM)
    hbm = pl.BlockSpec(memory_space=pltpu.HBM)
    both, grads = pl.pallas_call(
        kernel,
        out_shape=(
            pltpu.VMEM((2, 128, 768), BF16),
            pltpu.VMEM((32, 128), F32),
        ),
        in_specs=[hbm] * 13,
        out_specs=(vmem, vmem),
        scratch_shapes=[
            pltpu.VMEM((128, 768), BF16),
            pltpu.VMEM((128, 768), F32),
            pltpu.VMEM((8, STORE), I32),
            pltpu.VMEM((16, 128), I32),
            pltpu.VMEM((16, 16), I32),
            pltpu.VMEM((1, 128), I32),
            pltpu.VMEM((4, STORE), I32),
            pltpu.VMEM((768, 256), BF16),
            pltpu.VMEM((768, 256), BF16),
            pltpu.VMEM((768, 256), BF16),
            pltpu.VMEM((768, 256), BF16),
            pltpu.VMEM((384, 768), BF16),
            pltpu.VMEM((256, 768), BF16),
            pltpu.VMEM((256, 768), BF16),
            pltpu.VMEM((256, 768), BF16),
            pltpu.VMEM((STORE, 1, 128), I32),
            pltpu.VMEM((STORE, 1, 128), I32),
            pltpu.VMEM((3, STORE, 16, 128), BF16),
            pltpu.VMEM((3, STORE, 16, 128), BF16),
            pltpu.VMEM((256, 512), BF16),
            pltpu.VMEM((3, 512, 128), BF16),
            pltpu.VMEM((3, 128, 512), BF16),
            pltpu.VMEM((16, 256), F32),
            pltpu.VMEM((2048, 768), BF16),
            pltpu.VMEM((3, 256, 256), BF16),
            pltpu.VMEM((3, 2048, 256), BF16),
            pltpu.VMEM((3, 64, 256), F32),
            pltpu.VMEM((8, 256), F32),
            pltpu.VMEM((8, 256), F32),
            pltpu.VMEM((3, 8, 256), F32),
            pltpu.VMEM((192, 256), BF16),
            pltpu.VMEM((192, 256), BF16),
            pltpu.VMEM((2, 192, 128), BF16),
            pltpu.VMEM((192, 128), BF16),
            pltpu.VMEM((STORE, 16, 256), BF16),
            pltpu.VMEM((STORE, 16, 256), BF16),
            pltpu.VMEM((8, 144, 128), BF16),
            pltpu.VMEM((8, 144, 128), BF16),
            pltpu.VMEM((16, 16, 128), BF16),
            pltpu.VMEM((STORE, 16, 128), BF16),
            pltpu.VMEM((16, 80, 128), BF16),
            pltpu.VMEM((STORE, 80, 128), BF16),
            pltpu.VMEM((16, 768), BF16),
            pltpu.VMEM((8, 16, 256), BF16),
            pltpu.VMEM((256, 192), BF16),
            pltpu.VMEM((256, 144), BF16),
            pltpu.VMEM((256, 48), BF16),
            pltpu.VMEM((3, 128, 128), BF16),
            pltpu.VMEM((192, 2048), BF16),
            pltpu.VMEM((128, 192), BF16),
            pltpu.VMEM((6, 16, 80), BF16),
            pltpu.SemaphoreType.DMA((6,)),
            pltpu.SemaphoreType.DMA((7,)),
            pltpu.SemaphoreType.DMA((2,)),
            pltpu.SemaphoreType.DMA((2,)),
            pltpu.SemaphoreType.DMA((3,)),
            pltpu.SemaphoreType.DMA((3,)),
            pltpu.SemaphoreType.DMA((48,)),
            pltpu.SemaphoreType.DMA((48,)),
            pltpu.SemaphoreType.DMA((54,)),
            pltpu.SemaphoreType.DMA((54,)),
            pltpu.SemaphoreType.DMA((2,)),
            pltpu.SemaphoreType.DMA((2,)),
            pltpu.SemaphoreType.DMA((2,)),
            pltpu.SemaphoreType.DMA((2,)),
            pltpu.SemaphoreType.DMA((2,)),
            pltpu.SemaphoreType.DMA((2,)),
        ],
        compiler_params=pltpu.CompilerParams(
            collective_id=0, has_side_effects=True, vmem_limit_bytes=60 * 1024 * 1024
        ),
        cost_estimate=pl.CostEstimate(
            flops=7_000_000_000, bytes_accessed=6_000_000, transcendentals=1_600_000
        ),
    )(
        node_features, history, requests.T, neighbours.T, pattern, push_owner.reshape(1, -1),
        push_slot.T,
        cotangent, w_query, w_key, w_value, w_gate, w_out,
    )
    return (
        both[0],
        both[1].astype(F32),
        grads[0:12, 0:48].T,
        grads[16:28, 0:48].T,
    )


def solution(mesh):
    rows = P(("storage", "batch"), None)
    in_specs = (
        rows, rows, rows, rows, P("storage", None), P(("storage", "batch")), rows,
        P(), P(), P(), P(), P(), rows,
    )
    out_specs = (rows, rows, P("batch", "storage"), P("batch", "storage"))
    return jax.shard_map(
        on_device, mesh=mesh, in_specs=in_specs, out_specs=out_specs, check_vma=False
    )
```

```python
import functools

import jax
import jax.numpy as jnp
from jax import lax
from jax.experimental import pallas as pl
from jax.experimental.pallas import tpu as pltpu
from jax.sharding import PartitionSpec as P

F32, BF16, I32 = jnp.float32, jnp.bfloat16, jnp.int32
MESH = pl.DeviceIdType.MESH
STORE = 32
RING = 8
HEADS_CORE = 3
NEG = 1e30


def iota(shape, dim):
    return lax.broadcasted_iota(I32, shape, dim)


def onehot(cond):
    return jnp.where(cond, 1.0, 0.0).astype(BF16)


def mm(a, b):
    return lax.dot_general(a, b, (((1,), (0,)), ((), ())), preferred_element_type=F32)


def mm_nt(a, b):
    return lax.dot_general(a, b, (((1,), (1,)), ((), ())), preferred_element_type=F32)


def mm_tn(a, b):
    return lax.dot_general(a, b, (((0,), (0,)), ((), ())), preferred_element_type=F32)


def kernel(
    nf_hbm, hist_hbm, req_hbm, nbr_hbm, pat_hbm, owner_hbm, slot_hbm,
    cot_hbm, wq_hbm, wk_hbm, wv_hbm, wg_hbm, wo_hbm,
    rows_ref, grad_ref,
    nf_ref, hist_ref, req_ref, nbr_ref, pat_ref, owner_ref, slot_ref,
    wq, wk, wv, wg, wo, wvt, wgt, cot,
    req_src, asked, found, table, mix, psel, nsel, bias_ref,
    hid, qm, p_ref, acc_ref, mx_ref, sum_ref, mx_chip, gate_t, bg_t,
    gated, gsib, psend, parr, vsend, vrecv, tsend, tfin, gsend, grecv, hsend, gfin,
    tile_rows, rows_a, rows_b, moves, dvt, odd_rows, unpack,
    load_sem, small_sem, cot_sems, req_sems, pull_send, pull_recv,
    ring_send, ring_recv, sib_send, sib_recv,
    gated_sems, push_sems, vy_sems, vs_sems, gs_sems, gy_sems,
):
    s = lax.axis_index("storage")
    b = lax.axis_index("batch")
    y = lax.div(b, 2)
    c = lax.rem(b, 2)
    sib = b + 1 - 2 * c
    in_half = lax.div(s, 16)
    win = pl.multiple_of(c * 128, 128)
    c64 = pl.multiple_of(c * 64, 64)

    small = [
        pltpu.make_async_copy(src, dst, small_sem.at[i])
        for i, (src, dst) in enumerate((
            (req_hbm, req_ref), (hist_hbm, hist_ref), (nbr_hbm, nbr_ref), (owner_hbm, owner_ref),
            (slot_hbm, slot_ref), (pat_hbm, pat_ref), (nf_hbm, nf_ref),
        ))
    ]
    for copy in small:
        copy.start()
    loads = [
        pltpu.make_async_copy(src.at[:, pl.ds(win, 256)], dst, load_sem.at[i])
        for i, (src, dst) in enumerate(((wq_hbm, wq), (wk_hbm, wk), (wv_hbm, wv), (wg_hbm, wg)))
    ]
    loads.append(pltpu.make_async_copy(wo_hbm, wo, load_sem.at[4]))
    loads.append(pltpu.make_async_copy(cot_hbm, cot.at[pl.ds(win, 128)], load_sem.at[5]))
    for copy in loads:
        copy.start()

    barrier = pltpu.get_barrier_semaphore()

    def greet_store(k, _):
        peer = lax.rem(s + k, STORE)
        pl.semaphore_signal(barrier, inc=1, device_id=(peer, b), device_id_type=MESH)
        pl.semaphore_signal(barrier, inc=1, device_id=(peer, sib), device_id_type=MESH)
        return 0

    lax.fori_loop(1, STORE, greet_store, 0)

    def greet_ring(k, _):
        peer = lax.rem(b + k, 2 * RING)
        pl.semaphore_signal(barrier, inc=1, device_id=(s, peer), device_id_type=MESH)
        return 0

    lax.fori_loop(1, 2 * RING, greet_ring, 0)

    small[0].wait()
    eye8 = onehot(iota((8, 128), 0) == iota((8, 128), 1))
    req_src[...] = mm_tn(req_ref[...].astype(F32).astype(BF16), eye8).astype(I32).reshape(STORE, 1, 128)
    for copy in small[1:]:
        copy.wait()
    nbr = nbr_ref[...]
    at = iota((256, 128), 0)
    count = jnp.zeros((256, 128), F32)
    for k in range(16):
        count = count + jnp.where(nbr[k : k + 1, :] == at, 1.0, 0.0)
    count = count.astype(BF16)
    src_i = iota((256, 512), 0)
    dst_i = iota((256, 512), 1)
    home = src_i + (src_i & -8)
    mix[0:128] = mm_tn(count, onehot(dst_i == home)).astype(BF16)
    mix[128:256] = mm_tn(count, onehot(dst_i == home + 8)).astype(BF16)

    owner_row = owner_ref[...]
    i0 = iota((128, 128), 0)
    i1 = iota((128, 128), 1)
    owner_all = jnp.broadcast_to(owner_row, (128, 128))
    owner_col = jnp.sum(jnp.where(i0 == i1, owner_all, 0), axis=1, keepdims=True)
    rank = jnp.sum(
        jnp.where((owner_col == owner_all) & (i0 < i1), 1, 0), axis=0, keepdims=True
    )
    pos = owner_row * 4 + rank
    pr = iota((512, 128), 0)
    place = ((pr >> 4) << 2) + (pr & 3) == pos
    for u in range(3):
        psel[u] = onehot(place & (((pr >> 2) & 3) == u))
    sel = onehot(iota((STORE, 512), 0) == (iota((STORE, 512), 1) >> 4))
    wide = mm(slot_ref[...].astype(F32).astype(BF16), sel)
    slot_row = jnp.sum(
        jnp.where(iota((4, 512), 0) == (iota((4, 512), 1) & 3), wide, 0.0), axis=0, keepdims=True
    ).astype(I32)
    col = iota((128, 512), 1)
    lands = iota((128, 512), 0) == slot_row
    for u in range(3):
        nsel[u] = onehot(lands & (((col >> 2) & 3) == u))

    qsel = onehot(iota((16, 256), 0) == 2 * y + (iota((16, 256), 1) >> 7))
    seen = mm_tn(pat_ref[...].astype(F32).astype(BF16), qsel)
    bias_ref[...] = (seen - 1.0) * NEG
    mx_ref[...] = jnp.full_like(mx_ref, -2.0 * NEG)
    sum_ref[...] = jnp.zeros_like(sum_ref)
    acc_ref[...] = jnp.zeros_like(acc_ref)
    pl.semaphore_wait(barrier, 2 * (STORE - 1) + 2 * RING - 1)

    def swing(i, mid):
        return mid + lax.div(i + 1, 2) * (1 - 2 * lax.rem(i, 2))

    my_x = lax.div(s, 8)
    my_z = lax.rem(s, 8)

    def far_z(i):
        return lax.rem(my_z + swing(i, 4), 8)

    def store_copy(src, dst, send_sem, recv_sem, peer):
        return pltpu.make_async_remote_copy(
            src_ref=src, dst_ref=dst, send_sem=send_sem, recv_sem=recv_sem,
            device_id=(peer, b), device_id_type=MESH,
        )

    def send_all(src, dst, send_sem, recv_sem):
        def body(n, _):
            peer = lax.rem(my_x + swing(lax.rem(n, 4), 2), 4) * 8 + far_z(lax.div(n, 4))
            store_copy(src.at[peer], dst.at[s], send_sem, recv_sem, peer).start()
            return 0

        lax.fori_loop(0, STORE - 1, body, 0)

    def bulk_wait(ref, sem):
        pltpu.make_async_copy(ref, ref, sem).wait()

    others = pl.ds(0, STORE - 1)

    send_all(req_src, asked, req_sems.at[0], req_sems.at[1])
    asked[s] = req_src[s]
    cot_copy = pltpu.make_async_remote_copy(
        src_ref=cot_hbm, dst_ref=cot.at[pl.ds(win, 128)],
        send_sem=cot_sems.at[0], recv_sem=cot_sems.at[1],
        device_id=(s, sib), device_id_type=MESH,
    )
    cot_copy.start()

    hist_b = hist_ref[...].astype(BF16)
    rep = onehot(iota((STORE * 16, STORE), 1) == (iota((STORE * 16, STORE), 0) >> 4))
    for copy in loads:
        copy.wait()
    wvt[...] = wv[...].T
    wgt[...] = wg[...].T
    bulk_wait(asked.at[others], req_sems.at[1])

    asked_f = asked[...].reshape(STORE, 128).astype(F32).astype(BF16)
    spread = mm(rep, asked_f)
    prow = iota((STORE * 16, 128), 0)
    lane = iota((STORE * 16, 128), 1)
    mine = jnp.sum(jnp.where(lane == (prow & 7), spread, 0.0), axis=1, keepdims=True).astype(I32)
    hit = mine == lane
    pick_l = onehot(hit & ((prow & 8) == 0))
    pick_r = onehot(hit & ((prow & 8) != 0))
    for p in range(3):
        rows = mm(pick_l, hist_b[:, p * 256 : p * 256 + 128])
        rows = rows + mm(pick_r, hist_b[:, p * 256 + 128 : p * 256 + 256])
        found[p] = rows.astype(BF16).reshape(STORE, 16, 128)
        send_all(found.at[p], table.at[p], pull_send.at[p], pull_recv.at[p])
    for p in range(3):
        table[p, s] = found[p, s]

    e0 = iota((256, 192), 0)
    tile_rows[...] = onehot((iota((256, 192), 1) == (e0 >> 4) * 12 + (e0 & 15)) & ((e0 & 15) < 12))
    e2 = iota((128, 192), 0)
    odd_rows[...] = onehot((iota((128, 192), 1) == (e2 >> 3) * 12 + (e2 & 7) + 4) & ((e2 & 7) >= 4))
    ut = iota((16, 80), 0)
    ur = iota((16, 80), 1)
    for u in range(6):
        far = 48 + (u // 2) * 8 + (u % 2) * 4 - 8
        unpack[u] = onehot((ur == ut + jnp.where(ut < 8, u * 8, far)) & (ut < 12))
    lead = iota((128, 128), 0)
    free = iota((128, 128), 1)
    for k in range(3):
        moves[k] = onehot((free - 96 + 32 * k == lead) & (free >= 96))
    t0 = iota((256, 144), 0)
    rows_a[...] = onehot((iota((256, 144), 1) == (t0 >> 4) * 12 + (t0 & 15)) & ((t0 & 15) < 12))
    t1 = iota((256, 48), 0)
    rows_b[...] = onehot((iota((256, 48), 1) + 144 == (t1 >> 4) * 12 + (t1 & 15)) & ((t1 & 15) < 12))
    cot_copy.wait_recv()
    wo_mine = pl.multiple_of(c * 192, 64)
    wo_sib = pl.multiple_of((1 - c) * 192, 64)
    bg_t[...] = mm_nt(wo[pl.ds(wo_mine, 192), :], cot[...]).astype(BF16)

    right = lax.rem(y + 1, RING)
    left = lax.rem(y + RING - 1, RING)
    my_rows = pl.multiple_of(b * 128, 128)
    my_chip = pl.multiple_of(y * 256, 256)

    def chip_at(direction, dist):
        return lax.rem(y + (RING - dist if direction == 0 else dist), RING)

    def unit(chip, core, part, half):
        row = pl.multiple_of(chip * 256 + core * 128 + half * 64, 64)
        return hid.at[pl.ds(row, 64), pl.ds(part * 256, 256)]

    def ring_copy(direction, dist, part, half):
        ref = unit(chip_at(direction, dist - 1), c, part, half)
        idx = ((direction * 4 + dist - 1) * 3 + part) * 2 + half
        to = right if direction == 0 else left
        return pltpu.make_async_remote_copy(
            src_ref=ref, dst_ref=ref, send_sem=ring_send.at[idx], recv_sem=ring_recv.at[idx],
            device_id=(s, to * 2 + c), device_id_type=MESH,
        )

    def ring_arrived(direction, dist, part, half):
        ref = unit(chip_at(direction, dist), c, part, half)
        idx = ((direction * 4 + dist - 1) * 3 + part) * 2 + half
        pltpu.make_async_copy(ref, ref, ring_recv.at[idx]).wait()

    def sib_copy(direction, dist, part, half, core):
        ref = unit(chip_at(direction, dist), core, part, half)
        idx = ((direction * 4 + dist - 1) * 3 + part) * 2 + half if dist else 48 + part * 2 + half
        return pltpu.make_async_remote_copy(
            src_ref=ref, dst_ref=ref, send_sem=sib_send.at[idx], recv_sem=sib_recv.at[idx],
            device_id=(s, sib), device_id_type=MESH,
        )

    def halves(direction, dist):
        if dist < 4:
            return (0, 1)
        return (0,) if direction == 0 else (1,)

    sent = []

    def go(copy):
        copy.start()
        sent.append(copy)

    def own(part):
        bulk_wait(table.at[part, others], pull_recv.at[part])
        t = table[part].reshape(STORE * 16, 128)
        mean = mm(mix[...], t) * (1.0 / 16)
        for i in (0, 1):
            col = pl.ds(part * 256 + i * 128, 128)
            hid[pl.ds(my_rows, 128), col] = (
                nf_ref[:, col].astype(F32) + mean[i * 128 : (i + 1) * 128]
            ).astype(BF16)
        for half in (0, 1):
            for direction in (0, 1):
                go(ring_copy(direction, 1, part, half))
        for half in (0, 1):
            go(sib_copy(0, 0, part, half, c))

    def hop(dist, part):
        for half in (0, 1):
            for direction in (0, 1):
                if half not in halves(direction, dist):
                    continue
                ring_arrived(direction, dist, part, half)
                if dist < 4 and half in halves(direction, dist + 1):
                    go(ring_copy(direction, dist + 1, part, half))
                go(sib_copy(direction, dist, part, half, c))

    def wait_sib(direction, dist):
        for part in range(3):
            for half in halves(direction, dist) if dist else (0, 1):
                sib_copy(direction, dist, part, half, 1 - c).wait_recv()

    def process(chip):
        r0 = pl.multiple_of(chip * 256, 256)
        hc = hid[pl.ds(r0, 256), :]
        kc = mm(hc, wk[...]).astype(BF16)
        vt = mm_nt(wvt[pl.ds(c64, 192), :], hc).astype(BF16)
        b0 = bias_ref[pl.ds(2 * chip, 1), :]
        b1 = bias_ref[pl.ds(2 * chip + 1, 1), :]
        for h in range(HEADS_CORE):
            sc = mm_nt(kc, qm[h])
            lo = sc[0:128] + b0
            hi = sc[128:256] + b1
            top = jnp.max(jnp.maximum(lo, hi), axis=0, keepdims=True)
            old = mx_ref[h : h + 1, :]
            new = jnp.maximum(old, top)
            keep = jnp.exp(old - new)
            lo = jnp.exp(lo - new)
            hi = jnp.exp(hi - new)
            mx_ref[h : h + 1, :] = new
            mx_chip[h, pl.ds(chip, 1), :] = new
            sum_ref[h : h + 1, :] = sum_ref[h : h + 1, :] * keep + jnp.sum(lo + hi, axis=0, keepdims=True)
            pb = jnp.concatenate([lo.astype(BF16), hi.astype(BF16)], axis=0)
            p_ref[h, pl.ds(r0, 256), :] = pb
            acc_ref[h] = acc_ref[h] * keep + mm(vt[h * 64 : (h + 1) * 64], pb)

    def near(direction, dist):
        wait_sib(direction, dist)
        process(chip_at(direction, dist))

    own(0)
    own(1)
    hop(1, 0)
    own(2)
    hop(1, 1)
    hop(2, 0)
    wait_sib(0, 0)
    hc_own = hid[pl.ds(my_chip, 256), :]
    q = (mm(hc_own, wq[...]) * 0.125).astype(BF16).astype(F32)
    lq = (iota((256, 256), 1) - c * 64) >> 6
    for h in range(HEADS_CORE):
        qm[h] = jnp.where(lq == h, q, 0.0).astype(BF16)
    hop(1, 2)
    process(y)
    gate_t[...] = mm_nt(wgt[pl.ds(c64, 192), :], hid[pl.ds(my_chip, 256), :]).astype(BF16)
    hop(2, 1)
    hop(3, 0)
    near(0, 1)
    hop(2, 2)
    hop(3, 1)
    near(1, 1)
    hop(4, 0)
    hop(3, 2)
    near(0, 2)
    hop(4, 1)
    near(1, 2)
    near(0, 3)
    hop(4, 2)
    near(1, 3)
    wait_sib(0, 4)
    wait_sib(1, 4)
    process(chip_at(0, 4))

    ones = [1.0 / sum_ref[h : h + 1, :] for h in range(HEADS_CORE)]
    att = jnp.concatenate([acc_ref[h] * ones[h] for h in range(HEADS_CORE)], axis=0)
    att = att.astype(BF16).astype(F32)
    gate = gate_t[...].astype(F32)
    bg = bg_t[...].astype(F32)
    gated_t = (att * gate).astype(BF16)
    for qb in (0, 1):
        gated[qb] = gated_t[:, qb * 128 : (qb + 1) * 128]
    gated_copy = pltpu.make_async_remote_copy(
        src_ref=gated.at[1 - c], dst_ref=gsib, send_sem=gated_sems.at[0],
        recv_sem=gated_sems.at[1], device_id=(s, sib), device_id_type=MESH,
    )
    gated_copy.start()

    gg = mm((bg * att).astype(BF16), hid[pl.ds(my_chip, 256), :]).astype(BF16)
    ga = mm(tile_rows[...], gg)
    gb = mm(odd_rows[...], gg)
    for i in range(16):
        packed = [ga[i * 16 : i * 16 + 8, u * 128 : (u + 1) * 128] for u in range(6)]
        for u in range(0, 6, 2):
            even = ga[i * 16 + 8 : i * 16 + 16, u * 128 : (u + 1) * 128]
            packed.append(even + gb[i * 8 : i * 8 + 8, (u + 1) * 128 : (u + 2) * 128])
        packed.append(jnp.zeros((8, 128), F32))
        gsend[i] = jnp.concatenate(packed, axis=0).astype(BF16)

    def send_gate(i, _):
        dest = lax.rem(i, 2) * 8 + far_z(lax.div(i, 2))
        to = c * 16 + dest

        @pl.when(to == s)
        def _():
            grecv[s] = gsend[dest]

        @pl.when(to != s)
        def _():
            store_copy(gsend.at[dest], grecv.at[s], gs_sems.at[0], gs_sems.at[1], to).start()

        return 0

    lax.fori_loop(0, 16, send_gate, 0)

    back = (bg * gate).astype(BF16).astype(F32)
    backs = [back[h * 64 : (h + 1) * 64] * ones[h] for h in range(HEADS_CORE)]

    for j in range(RING):
        dv = []
        for h in range(HEADS_CORE):
            scale = jnp.exp(mx_chip[h, j : j + 1, :] - mx_ref[h : h + 1, :])
            dv.append(mm_nt((backs[h] * scale).astype(BF16), p_ref[h, j * 256 : (j + 1) * 256, :]))
        dvt[:, j * 256 : (j + 1) * 256] = jnp.concatenate(dv, axis=0).astype(BF16)
    gv = mm(dvt[...], hid[...])
    for j in range(RING):
        chunk = gv[:, j * 96 : (j + 1) * 96]
        tail = jnp.concatenate([chunk[144:192, 32 * k : 32 * k + 32] for k in range(3)], axis=0)
        vsend[j] = jnp.concatenate([chunk[0:144], tail], axis=1).astype(BF16)
    vrecv[y] = vsend[y]

    def send_value(k, _):
        to = lax.rem(y + swing(k, 4), RING)
        pltpu.make_async_remote_copy(
            src_ref=vsend.at[to], dst_ref=vrecv.at[y],
            send_sem=vy_sems.at[0], recv_sem=vy_sems.at[1],
            device_id=(s, to * 2 + c), device_id_type=MESH,
        ).start()
        return 0

    lax.fori_loop(0, RING - 1, send_value, 0)

    gated_copy.wait_recv()
    out = nf_ref[...].astype(F32) + (
        mm_tn(gated[c], wo[pl.ds(wo_mine, 192), :]) + mm_tn(gsib[...], wo[pl.ds(wo_sib, 192), :])
    )
    out_b = out.astype(BF16)
    rows_ref[0] = out_b
    pushed = mm(psel[0], out_b[:, 0:256])
    pushed = pushed + mm(psel[1], out_b[:, 256:512])
    pushed = pushed + mm(psel[2], out_b[:, 512:768])
    psend[...] = pushed.astype(BF16).reshape(STORE, 16, 256)
    @pl.when(in_half == c)
    def _():
        bulk_wait(gsend.at[pl.ds(0, 15)], gs_sems.at[0])

    @pl.when(in_half != c)
    def _():
        bulk_wait(gsend, gs_sems.at[0])

    send_all(psend, parr, push_sems.at[0], push_sems.at[1])
    parr[s] = psend[s]

    bulk_wait(req_src.at[others], req_sems.at[0])
    for p in range(3):
        bulk_wait(found.at[p, others], pull_send.at[p])
    cot_copy.wait_send()
    for copy in sent:
        copy.wait_send()
    gated_copy.wait_send()

    bulk_wait(vrecv.at[pl.ds(0, RING - 1)], vy_sems.at[1])
    total = vrecv[0].astype(F32)
    for j in range(1, RING):
        total = total + vrecv[j].astype(F32)
    total = total.astype(BF16)
    rest = mm_nt(total[0:48], moves[0]) + mm_nt(total[48:96], moves[1]) + mm_nt(total[96:144], moves[2])
    tiles = mm(rows_a[...], total) + mm(rows_b[...], rest.astype(BF16))
    tsend[...] = tiles.astype(BF16).reshape(16, 16, 128)

    def send_tile(i, _):
        core = lax.rem(i, 2)
        dest = lax.rem(lax.div(i, 2), 2) * 8 + far_z(lax.div(i, 4))
        to = c * 16 + dest
        own_tile = (to == s) & (core == c)

        @pl.when(own_tile)
        def _():
            tfin[s] = tsend[dest]

        @pl.when(jnp.logical_not(own_tile))
        def _():
            pltpu.make_async_remote_copy(
                src_ref=tsend.at[dest], dst_ref=tfin.at[s],
                send_sem=vs_sems.at[0], recv_sem=vs_sems.at[1],
                device_id=(to, y * 2 + core), device_id_type=MESH,
            ).start()

        return 0

    lax.fori_loop(0, 32, send_tile, 0)

    def first_tile(at_b):
        return pl.multiple_of(jnp.minimum(lax.div(at_b * 48, 128), 4) * 128, 128)

    @pl.when(in_half == c)
    def _():
        bulk_wait(grecv.at[others], gs_sems.at[1])
        sum_s = grecv[0].astype(F32)
        for j in range(1, STORE):
            sum_s = sum_s + grecv[j].astype(F32)
        sum_s = sum_s.astype(BF16)
        for u in range(6):
            hsend[:, u * 128 : (u + 1) * 128] = mm(unpack[u], sum_s).astype(BF16)
        gfin[y] = hsend[:, pl.ds(first_tile(b), 256)]

        def send_rows(k, _):
            to = lax.rem(b + k, 2 * RING)
            pltpu.make_async_remote_copy(
                src_ref=hsend.at[:, pl.ds(first_tile(to), 256)], dst_ref=gfin.at[y],
                send_sem=gy_sems.at[0], recv_sem=gy_sems.at[1],
                device_id=(s, to), device_id_type=MESH,
            ).start()
            return 0

        lax.fori_loop(1, 2 * RING, send_rows, 0)

    bulk_wait(parr.at[others], push_sems.at[1])
    arrived = parr[...].reshape(STORE * 16, 256)
    for u in range(3):
        rows_ref[1, :, u * 256 : (u + 1) * 256] = mm(nsel[u], arrived).astype(BF16)

    def cut(x, width, offset):
        pick = onehot(
            (iota((width, 128), 0) == iota((width, 128), 1) + offset) & (iota((width, 128), 1) < 48)
        )
        high = x.astype(BF16)
        low = (x - high.astype(F32)).astype(BF16)
        return mm(high, pick) + mm(low, pick)

    @pl.when(in_half == c)
    def _():
        bulk_wait(gfin.at[pl.ds(0, RING - 1)], gy_sems.at[1])

    @pl.when(in_half != c)
    def _():
        bulk_wait(gfin, gy_sems.at[1])

    sum_g = gfin[0].astype(F32)
    for j in range(1, RING):
        sum_g = sum_g + gfin[j].astype(F32)
    grad_ref[0:16] = cut(sum_g, 256, b * 48 - first_tile(b))

    @pl.when(in_half == c)
    def _():
        bulk_wait(tfin.at[others], vs_sems.at[1])

    @pl.when(in_half != c)
    def _():
        bulk_wait(tfin, vs_sems.at[1])

    sum_v = tfin[0].astype(F32)
    for j in range(1, STORE):
        sum_v = sum_v + tfin[j].astype(F32)
    grad_ref[16:32, 0:48] = jnp.where(c == 0, sum_v[:, 0:48], sum_v[:, 48:96])

    bulk_wait(vsend.at[pl.ds(0, RING - 1)], vy_sems.at[0])
    bulk_wait(psend.at[others], push_sems.at[0])

    @pl.when(in_half == c)
    def _():
        bulk_wait(psend.at[pl.ds(0, 15)], gy_sems.at[0])
        bulk_wait(tfin.at[others], vs_sems.at[0])

    @pl.when(in_half != c)
    def _():
        bulk_wait(tfin, vs_sems.at[0])


def on_device(
    node_features, history, requests, neighbours, pattern, push_owner, push_slot,
    w_query, w_key, w_value, w_gate, w_out, cotangent,
):
    vmem = pl.BlockSpec(memory_space=pltpu.VMEM)
    hbm = pl.BlockSpec(memory_space=pltpu.HBM)
    both, grads = pl.pallas_call(
        kernel,
        out_shape=(
            pltpu.VMEM((2, 128, 768), BF16),
            pltpu.VMEM((32, 128), F32),
        ),
        in_specs=[hbm] * 13,
        out_specs=(vmem, vmem),
        scratch_shapes=[
            pltpu.VMEM((128, 768), BF16),
            pltpu.VMEM((128, 768), F32),
            pltpu.VMEM((8, STORE), I32),
            pltpu.VMEM((16, 128), I32),
            pltpu.VMEM((16, 16), I32),
            pltpu.VMEM((1, 128), I32),
            pltpu.VMEM((4, STORE), I32),
            pltpu.VMEM((768, 256), BF16),
            pltpu.VMEM((768, 256), BF16),
            pltpu.VMEM((768, 256), BF16),
            pltpu.VMEM((768, 256), BF16),
            pltpu.VMEM((384, 768), BF16),
            pltpu.VMEM((256, 768), BF16),
            pltpu.VMEM((256, 768), BF16),
            pltpu.VMEM((256, 768), BF16),
            pltpu.VMEM((STORE, 1, 128), I32),
            pltpu.VMEM((STORE, 1, 128), I32),
            pltpu.VMEM((3, STORE, 16, 128), BF16),
            pltpu.VMEM((3, STORE, 16, 128), BF16),
            pltpu.VMEM((256, 512), BF16),
            pltpu.VMEM((3, 512, 128), BF16),
            pltpu.VMEM((3, 128, 512), BF16),
            pltpu.VMEM((16, 256), F32),
            pltpu.VMEM((2048, 768), BF16),
            pltpu.VMEM((3, 256, 256), BF16),
            pltpu.VMEM((3, 2048, 256), BF16),
            pltpu.VMEM((3, 64, 256), F32),
            pltpu.VMEM((8, 256), F32),
            pltpu.VMEM((8, 256), F32),
            pltpu.VMEM((3, 8, 256), F32),
            pltpu.VMEM((192, 256), BF16),
            pltpu.VMEM((192, 256), BF16),
            pltpu.VMEM((2, 192, 128), BF16),
            pltpu.VMEM((192, 128), BF16),
            pltpu.VMEM((STORE, 16, 256), BF16),
            pltpu.VMEM((STORE, 16, 256), BF16),
            pltpu.VMEM((8, 144, 128), BF16),
            pltpu.VMEM((8, 144, 128), BF16),
            pltpu.VMEM((16, 16, 128), BF16),
            pltpu.VMEM((STORE, 16, 128), BF16),
            pltpu.VMEM((16, 80, 128), BF16),
            pltpu.VMEM((STORE, 80, 128), BF16),
            pltpu.VMEM((16, 768), BF16),
            pltpu.VMEM((8, 16, 256), BF16),
            pltpu.VMEM((256, 192), BF16),
            pltpu.VMEM((256, 144), BF16),
            pltpu.VMEM((256, 48), BF16),
            pltpu.VMEM((3, 128, 128), BF16),
            pltpu.VMEM((192, 2048), BF16),
            pltpu.VMEM((128, 192), BF16),
            pltpu.VMEM((6, 16, 80), BF16),
            pltpu.SemaphoreType.DMA((6,)),
            pltpu.SemaphoreType.DMA((7,)),
            pltpu.SemaphoreType.DMA((2,)),
            pltpu.SemaphoreType.DMA((2,)),
            pltpu.SemaphoreType.DMA((3,)),
            pltpu.SemaphoreType.DMA((3,)),
            pltpu.SemaphoreType.DMA((48,)),
            pltpu.SemaphoreType.DMA((48,)),
            pltpu.SemaphoreType.DMA((54,)),
            pltpu.SemaphoreType.DMA((54,)),
            pltpu.SemaphoreType.DMA((2,)),
            pltpu.SemaphoreType.DMA((2,)),
            pltpu.SemaphoreType.DMA((2,)),
            pltpu.SemaphoreType.DMA((2,)),
            pltpu.SemaphoreType.DMA((2,)),
            pltpu.SemaphoreType.DMA((2,)),
        ],
        compiler_params=pltpu.CompilerParams(
            collective_id=0, has_side_effects=True, vmem_limit_bytes=60 * 1024 * 1024
        ),
        cost_estimate=pl.CostEstimate(
            flops=7_000_000_000, bytes_accessed=6_000_000, transcendentals=1_600_000
        ),
    )(
        node_features, history, requests.T, neighbours.T, pattern, push_owner.reshape(1, -1),
        push_slot.T,
        cotangent, w_query, w_key, w_value, w_gate, w_out,
    )
    return (
        both[0],
        both[1].astype(F32),
        grads[0:12, 0:48].T,
        grads[16:28, 0:48].T,
    )


def solution(mesh):
    rows = P(("storage", "batch"), None)
    in_specs = (
        rows, rows, rows, rows, P("storage", None), P(("storage", "batch")), rows,
        P(), P(), P(), P(), P(), rows,
    )
    out_specs = (rows, rows, P("batch", "storage"), P("batch", "storage"))
    return jax.shard_map(
        on_device, mesh=mesh, in_specs=in_specs, out_specs=out_specs, check_vma=False
    )
```

```python
import functools

import jax
import jax.numpy as jnp
from jax import lax
from jax.experimental import pallas as pl
from jax.experimental.pallas import tpu as pltpu
from jax.sharding import PartitionSpec as P

F32, BF16, I32 = jnp.float32, jnp.bfloat16, jnp.int32
MESH = pl.DeviceIdType.MESH
STORE = 32
RING = 8
HEADS_CORE = 3
NEG = 1e30


def iota(shape, dim):
    return lax.broadcasted_iota(I32, shape, dim)


def onehot(cond):
    return jnp.where(cond, 1.0, 0.0).astype(BF16)


def mm(a, b):
    return lax.dot_general(a, b, (((1,), (0,)), ((), ())), preferred_element_type=F32)


def mm_nt(a, b):
    return lax.dot_general(a, b, (((1,), (1,)), ((), ())), preferred_element_type=F32)


def mm_tn(a, b):
    return lax.dot_general(a, b, (((0,), (0,)), ((), ())), preferred_element_type=F32)


def kernel(
    nf_hbm, hist_hbm, req_hbm, nbr_hbm, pat_hbm, owner_hbm, slot_hbm,
    cot_hbm, wq_hbm, wk_hbm, wv_hbm, wg_hbm, wo_hbm,
    rows_ref, grad_ref,
    nf_ref, hist_ref, req_ref, nbr_ref, pat_ref, owner_ref, slot_ref,
    wq, wk, wv, wg, wo, wvt, wgt, cot,
    req_src, asked, found, table, mix, psel, nsel, bias_ref,
    hid, qm, p_ref, acc_ref, mx_ref, sum_ref, mx_chip, gate_t, bg_t,
    gated, gsib, psend, parr, vsend, vrecv, tsend, tfin, gsend, grecv, hsend, gfin,
    tile_rows, rows_a, rows_b, moves, dvt, odd_rows, unpack,
    load_sem, small_sem, cot_sems, req_sems, pull_send, pull_recv,
    ring_send, ring_recv, sib_send, sib_recv,
    gated_sems, push_sems, vy_sems, vs_sems, gs_sems, gy_sems,
):
    s = lax.axis_index("storage")
    b = lax.axis_index("batch")
    y = lax.div(b, 2)
    c = lax.rem(b, 2)
    sib = b + 1 - 2 * c
    in_half = lax.div(s, 16)
    win = pl.multiple_of(c * 128, 128)
    c64 = pl.multiple_of(c * 64, 64)

    small = [
        pltpu.make_async_copy(src, dst, small_sem.at[i])
        for i, (src, dst) in enumerate((
            (req_hbm, req_ref), (hist_hbm, hist_ref), (nbr_hbm, nbr_ref), (owner_hbm, owner_ref),
            (slot_hbm, slot_ref), (pat_hbm, pat_ref), (nf_hbm, nf_ref),
        ))
    ]
    for copy in small:
        copy.start()
    loads = [
        pltpu.make_async_copy(src.at[:, pl.ds(win, 256)], dst, load_sem.at[i])
        for i, (src, dst) in enumerate(((wq_hbm, wq), (wk_hbm, wk), (wv_hbm, wv), (wg_hbm, wg)))
    ]
    loads.append(pltpu.make_async_copy(wo_hbm, wo, load_sem.at[4]))
    loads.append(pltpu.make_async_copy(cot_hbm, cot.at[pl.ds(win, 128)], load_sem.at[5]))
    for copy in loads:
        copy.start()

    barrier = pltpu.get_barrier_semaphore()

    def greet_store(k, _):
        peer = lax.rem(s + k, STORE)
        pl.semaphore_signal(barrier, inc=1, device_id=(peer, b), device_id_type=MESH)
        pl.semaphore_signal(barrier, inc=1, device_id=(peer, sib), device_id_type=MESH)
        return 0

    lax.fori_loop(1, STORE, greet_store, 0)

    def greet_ring(k, _):
        peer = lax.rem(b + k, 2 * RING)
        pl.semaphore_signal(barrier, inc=1, device_id=(s, peer), device_id_type=MESH)
        return 0

    lax.fori_loop(1, 2 * RING, greet_ring, 0)

    small[0].wait()
    eye8 = onehot(iota((8, 128), 0) == iota((8, 128), 1))
    req_src[...] = mm_tn(req_ref[...].astype(F32).astype(BF16), eye8).astype(I32).reshape(STORE, 1, 128)
    for copy in small[1:]:
        copy.wait()
    nbr = nbr_ref[...]
    at = iota((256, 128), 0)
    count = jnp.zeros((256, 128), F32)
    for k in range(16):
        count = count + jnp.where(nbr[k : k + 1, :] == at, 1.0, 0.0)
    count = count.astype(BF16)
    src_i = iota((256, 512), 0)
    dst_i = iota((256, 512), 1)
    home = src_i + (src_i & -8)
    mix[0:128] = mm_tn(count, onehot(dst_i == home)).astype(BF16)
    mix[128:256] = mm_tn(count, onehot(dst_i == home + 8)).astype(BF16)

    owner_row = owner_ref[...]
    i0 = iota((128, 128), 0)
    i1 = iota((128, 128), 1)
    owner_all = jnp.broadcast_to(owner_row, (128, 128))
    owner_col = jnp.sum(jnp.where(i0 == i1, owner_all, 0), axis=1, keepdims=True)
    rank = jnp.sum(
        jnp.where((owner_col == owner_all) & (i0 < i1), 1, 0), axis=0, keepdims=True
    )
    pos = owner_row * 4 + rank
    pr = iota((512, 128), 0)
    place = ((pr >> 4) << 2) + (pr & 3) == pos
    for u in range(3):
        psel[u] = onehot(place & (((pr >> 2) & 3) == u))
    sel = onehot(iota((STORE, 512), 0) == (iota((STORE, 512), 1) >> 4))
    wide = mm(slot_ref[...].astype(F32).astype(BF16), sel)
    slot_row = jnp.sum(
        jnp.where(iota((4, 512), 0) == (iota((4, 512), 1) & 3), wide, 0.0), axis=0, keepdims=True
    ).astype(I32)
    col = iota((128, 512), 1)
    lands = iota((128, 512), 0) == slot_row
    for u in range(3):
        nsel[u] = onehot(lands & (((col >> 2) & 3) == u))

    qsel = onehot(iota((16, 256), 0) == 2 * y + (iota((16, 256), 1) >> 7))
    seen = mm_tn(pat_ref[...].astype(F32).astype(BF16), qsel)
    bias_ref[...] = (seen - 1.0) * NEG
    mx_ref[...] = jnp.full_like(mx_ref, -2.0 * NEG)
    sum_ref[...] = jnp.zeros_like(sum_ref)
    acc_ref[...] = jnp.zeros_like(acc_ref)
    pl.semaphore_wait(barrier, 2 * (STORE - 1) + 2 * RING - 1)

    def swing(i, mid):
        return mid + lax.div(i + 1, 2) * (1 - 2 * lax.rem(i, 2))

    my_x = lax.div(s, 8)
    my_z = lax.rem(s, 8)

    def far_z(i):
        return lax.rem(my_z + swing(i, 4), 8)

    def store_copy(src, dst, send_sem, recv_sem, peer):
        return pltpu.make_async_remote_copy(
            src_ref=src, dst_ref=dst, send_sem=send_sem, recv_sem=recv_sem,
            device_id=(peer, b), device_id_type=MESH,
        )

    def send_all(src, dst, send_sem, recv_sem):
        def body(n, _):
            peer = lax.rem(my_x + swing(lax.rem(n, 4), 2), 4) * 8 + far_z(lax.div(n, 4))
            store_copy(src.at[peer], dst.at[s], send_sem, recv_sem, peer).start()
            return 0

        lax.fori_loop(0, STORE - 1, body, 0)

    def bulk_wait(ref, sem):
        pltpu.make_async_copy(ref, ref, sem).wait()

    others = pl.ds(0, STORE - 1)

    send_all(req_src, asked, req_sems.at[0], req_sems.at[1])
    asked[s] = req_src[s]
    cot_copy = pltpu.make_async_remote_copy(
        src_ref=cot_hbm, dst_ref=cot.at[pl.ds(win, 128)],
        send_sem=cot_sems.at[0], recv_sem=cot_sems.at[1],
        device_id=(s, sib), device_id_type=MESH,
    )
    cot_copy.start()

    hist_b = hist_ref[...].astype(BF16)
    rep = onehot(iota((STORE * 16, STORE), 1) == (iota((STORE * 16, STORE), 0) >> 4))
    for copy in loads:
        copy.wait()
    wvt[...] = wv[...].T
    wgt[...] = wg[...].T
    bulk_wait(asked.at[others], req_sems.at[1])

    asked_f = asked[...].reshape(STORE, 128).astype(F32).astype(BF16)
    spread = mm(rep, asked_f)
    prow = iota((STORE * 16, 128), 0)
    lane = iota((STORE * 16, 128), 1)
    mine = jnp.sum(jnp.where(lane == (prow & 7), spread, 0.0), axis=1, keepdims=True).astype(I32)
    hit = mine == lane
    pick_l = onehot(hit & ((prow & 8) == 0))
    pick_r = onehot(hit & ((prow & 8) != 0))
    for p in range(3):
        rows = mm(pick_l, hist_b[:, p * 256 : p * 256 + 128])
        rows = rows + mm(pick_r, hist_b[:, p * 256 + 128 : p * 256 + 256])
        found[p] = rows.astype(BF16).reshape(STORE, 16, 128)
        send_all(found.at[p], table.at[p], pull_send.at[p], pull_recv.at[p])
    for p in range(3):
        table[p, s] = found[p, s]

    e0 = iota((256, 192), 0)
    tile_rows[...] = onehot((iota((256, 192), 1) == (e0 >> 4) * 12 + (e0 & 15)) & ((e0 & 15) < 12))
    e2 = iota((128, 192), 0)
    odd_rows[...] = onehot((iota((128, 192), 1) == (e2 >> 3) * 12 + (e2 & 7) + 4) & ((e2 & 7) >= 4))
    ut = iota((16, 80), 0)
    ur = iota((16, 80), 1)
    for u in range(6):
        far = 48 + (u // 2) * 8 + (u % 2) * 4 - 8
        unpack[u] = onehot((ur == ut + jnp.where(ut < 8, u * 8, far)) & (ut < 12))
    lead = iota((128, 128), 0)
    free = iota((128, 128), 1)
    for k in range(3):
        moves[k] = onehot((free - 96 + 32 * k == lead) & (free >= 96))
    t0 = iota((256, 144), 0)
    rows_a[...] = onehot((iota((256, 144), 1) == (t0 >> 4) * 12 + (t0 & 15)) & ((t0 & 15) < 12))
    t1 = iota((256, 48), 0)
    rows_b[...] = onehot((iota((256, 48), 1) + 144 == (t1 >> 4) * 12 + (t1 & 15)) & ((t1 & 15) < 12))
    cot_copy.wait_recv()
    wo_mine = pl.multiple_of(c * 192, 64)
    wo_sib = pl.multiple_of((1 - c) * 192, 64)
    bg_t[...] = mm_nt(wo[pl.ds(wo_mine, 192), :], cot[...]).astype(BF16)

    right = lax.rem(y + 1, RING)
    left = lax.rem(y + RING - 1, RING)
    my_rows = pl.multiple_of(b * 128, 128)
    my_chip = pl.multiple_of(y * 256, 256)

    def chip_at(direction, dist):
        return lax.rem(y + (RING - dist if direction == 0 else dist), RING)

    def unit(chip, core, part, half):
        row = pl.multiple_of(chip * 256 + core * 128 + half * 64, 64)
        return hid.at[pl.ds(row, 64), pl.ds(part * 256, 256)]

    def ring_copy(direction, dist, part, half):
        ref = unit(chip_at(direction, dist - 1), c, part, half)
        idx = ((direction * 4 + dist - 1) * 3 + part) * 2 + half
        to = right if direction == 0 else left
        return pltpu.make_async_remote_copy(
            src_ref=ref, dst_ref=ref, send_sem=ring_send.at[idx], recv_sem=ring_recv.at[idx],
            device_id=(s, to * 2 + c), device_id_type=MESH,
        )

    def ring_arrived(direction, dist, part, half):
        ref = unit(chip_at(direction, dist), c, part, half)
        idx = ((direction * 4 + dist - 1) * 3 + part) * 2 + half
        pltpu.make_async_copy(ref, ref, ring_recv.at[idx]).wait()

    def sib_copy(direction, dist, part, half, core):
        ref = unit(chip_at(direction, dist), core, part, half)
        idx = ((direction * 4 + dist - 1) * 3 + part) * 2 + half if dist else 48 + part * 2 + half
        return pltpu.make_async_remote_copy(
            src_ref=ref, dst_ref=ref, send_sem=sib_send.at[idx], recv_sem=sib_recv.at[idx],
            device_id=(s, sib), device_id_type=MESH,
        )

    def halves(direction, dist):
        if dist < 4:
            return (0, 1)
        return (0,) if direction == 0 else (1,)

    sent = []

    def go(copy):
        copy.start()
        sent.append(copy)

    def own(part):
        bulk_wait(table.at[part, others], pull_recv.at[part])
        t = table[part].reshape(STORE * 16, 128)
        mean = mm(mix[...], t) * (1.0 / 16)
        for i in (0, 1):
            col = pl.ds(part * 256 + i * 128, 128)
            hid[pl.ds(my_rows, 128), col] = (
                nf_ref[:, col].astype(F32) + mean[i * 128 : (i + 1) * 128]
            ).astype(BF16)
        for half in (0, 1):
            for direction in (0, 1):
                go(ring_copy(direction, 1, part, half))
        for half in (0, 1):
            go(sib_copy(0, 0, part, half, c))

    def hop(dist, part):
        for half in (0, 1):
            for direction in (0, 1):
                if half not in halves(direction, dist):
                    continue
                ring_arrived(direction, dist, part, half)
                if dist < 4 and half in halves(direction, dist + 1):
                    go(ring_copy(direction, dist + 1, part, half))
                go(sib_copy(direction, dist, part, half, c))

    def wait_sib(direction, dist):
        for part in range(3):
            for half in halves(direction, dist) if dist else (0, 1):
                sib_copy(direction, dist, part, half, 1 - c).wait_recv()

    def process(chip):
        r0 = pl.multiple_of(chip * 256, 256)
        hc = hid[pl.ds(r0, 256), :]
        kc = mm(hc, wk[...]).astype(BF16)
        vt = mm_nt(wvt[pl.ds(c64, 192), :], hc).astype(BF16)
        b0 = bias_ref[pl.ds(2 * chip, 1), :]
        b1 = bias_ref[pl.ds(2 * chip + 1, 1), :]
        for h in range(HEADS_CORE):
            sc = mm_nt(kc, qm[h])
            lo = sc[0:128] + b0
            hi = sc[128:256] + b1
            top = jnp.max(jnp.maximum(lo, hi), axis=0, keepdims=True)
            old = mx_ref[h : h + 1, :]
            new = jnp.maximum(old, top)
            keep = jnp.exp(old - new)
            lo = jnp.exp(lo - new)
            hi = jnp.exp(hi - new)
            mx_ref[h : h + 1, :] = new
            mx_chip[h, pl.ds(chip, 1), :] = new
            sum_ref[h : h + 1, :] = sum_ref[h : h + 1, :] * keep + jnp.sum(lo + hi, axis=0, keepdims=True)
            pb = jnp.concatenate([lo.astype(BF16), hi.astype(BF16)], axis=0)
            p_ref[h, pl.ds(r0, 256), :] = pb
            acc_ref[h] = acc_ref[h] * keep + mm(vt[h * 64 : (h + 1) * 64], pb)

    def near(direction, dist):
        wait_sib(direction, dist)
        process(chip_at(direction, dist))

    own(0)
    own(1)
    hop(1, 0)
    own(2)
    hop(1, 1)
    hop(2, 0)
    wait_sib(0, 0)
    hc_own = hid[pl.ds(my_chip, 256), :]
    q = (mm(hc_own, wq[...]) * 0.125).astype(BF16).astype(F32)
    lq = (iota((256, 256), 1) - c * 64) >> 6
    for h in range(HEADS_CORE):
        qm[h] = jnp.where(lq == h, q, 0.0).astype(BF16)
    hop(1, 2)
    process(y)
    gate_t[...] = mm_nt(wgt[pl.ds(c64, 192), :], hid[pl.ds(my_chip, 256), :]).astype(BF16)
    hop(2, 1)
    hop(3, 0)
    near(0, 1)
    hop(2, 2)
    hop(3, 1)
    near(1, 1)
    hop(4, 0)
    near(0, 2)
    hop(3, 2)
    near(1, 2)
    hop(4, 1)
    near(0, 3)
    near(1, 3)
    hop(4, 2)
    wait_sib(0, 4)
    wait_sib(1, 4)
    process(chip_at(0, 4))

    ones = [1.0 / sum_ref[h : h + 1, :] for h in range(HEADS_CORE)]
    att = jnp.concatenate([acc_ref[h] * ones[h] for h in range(HEADS_CORE)], axis=0)
    att = att.astype(BF16).astype(F32)
    gate = gate_t[...].astype(F32)
    bg = bg_t[...].astype(F32)
    gated_t = (att * gate).astype(BF16)
    for qb in (0, 1):
        gated[qb] = gated_t[:, qb * 128 : (qb + 1) * 128]
    gated_copy = pltpu.make_async_remote_copy(
        src_ref=gated.at[1 - c], dst_ref=gsib, send_sem=gated_sems.at[0],
        recv_sem=gated_sems.at[1], device_id=(s, sib), device_id_type=MESH,
    )
    gated_copy.start()

    gg = mm((bg * att).astype(BF16), hid[pl.ds(my_chip, 256), :]).astype(BF16)
    ga = mm(tile_rows[...], gg)
    gb = mm(odd_rows[...], gg)
    for i in range(16):
        packed = [ga[i * 16 : i * 16 + 8, u * 128 : (u + 1) * 128] for u in range(6)]
        for u in range(0, 6, 2):
            even = ga[i * 16 + 8 : i * 16 + 16, u * 128 : (u + 1) * 128]
            packed.append(even + gb[i * 8 : i * 8 + 8, (u + 1) * 128 : (u + 2) * 128])
        packed.append(jnp.zeros((8, 128), F32))
        gsend[i] = jnp.concatenate(packed, axis=0).astype(BF16)

    def send_gate(i, _):
        dest = lax.rem(i, 2) * 8 + far_z(lax.div(i, 2))
        to = c * 16 + dest

        @pl.when(to == s)
        def _():
            grecv[s] = gsend[dest]

        @pl.when(to != s)
        def _():
            store_copy(gsend.at[dest], grecv.at[s], gs_sems.at[0], gs_sems.at[1], to).start()

        return 0

    lax.fori_loop(0, 16, send_gate, 0)

    back = (bg * gate).astype(BF16).astype(F32)
    backs = [back[h * 64 : (h + 1) * 64] * ones[h] for h in range(HEADS_CORE)]

    for j in range(RING):
        dv = []
        for h in range(HEADS_CORE):
            scale = jnp.exp(mx_chip[h, j : j + 1, :] - mx_ref[h : h + 1, :])
            dv.append(mm_nt((backs[h] * scale).astype(BF16), p_ref[h, j * 256 : (j + 1) * 256, :]))
        dvt[:, j * 256 : (j + 1) * 256] = jnp.concatenate(dv, axis=0).astype(BF16)
    gv = mm(dvt[...], hid[...])
    for j in range(RING):
        chunk = gv[:, j * 96 : (j + 1) * 96]
        tail = jnp.concatenate([chunk[144:192, 32 * k : 32 * k + 32] for k in range(3)], axis=0)
        vsend[j] = jnp.concatenate([chunk[0:144], tail], axis=1).astype(BF16)
    vrecv[y] = vsend[y]

    def send_value(k, _):
        to = lax.rem(y + swing(k, 4), RING)
        pltpu.make_async_remote_copy(
            src_ref=vsend.at[to], dst_ref=vrecv.at[y],
            send_sem=vy_sems.at[0], recv_sem=vy_sems.at[1],
            device_id=(s, to * 2 + c), device_id_type=MESH,
        ).start()
        return 0

    lax.fori_loop(0, RING - 1, send_value, 0)

    gated_copy.wait_recv()
    out = nf_ref[...].astype(F32) + (
        mm_tn(gated[c], wo[pl.ds(wo_mine, 192), :]) + mm_tn(gsib[...], wo[pl.ds(wo_sib, 192), :])
    )
    out_b = out.astype(BF16)
    rows_ref[0] = out_b
    pushed = mm(psel[0], out_b[:, 0:256])
    pushed = pushed + mm(psel[1], out_b[:, 256:512])
    pushed = pushed + mm(psel[2], out_b[:, 512:768])
    psend[...] = pushed.astype(BF16).reshape(STORE, 16, 256)
    @pl.when(in_half == c)
    def _():
        bulk_wait(gsend.at[pl.ds(0, 15)], gs_sems.at[0])

    @pl.when(in_half != c)
    def _():
        bulk_wait(gsend, gs_sems.at[0])

    send_all(psend, parr, push_sems.at[0], push_sems.at[1])
    parr[s] = psend[s]

    bulk_wait(req_src.at[others], req_sems.at[0])
    for p in range(3):
        bulk_wait(found.at[p, others], pull_send.at[p])
    cot_copy.wait_send()
    for copy in sent:
        copy.wait_send()
    gated_copy.wait_send()

    bulk_wait(vrecv.at[pl.ds(0, RING - 1)], vy_sems.at[1])
    total = vrecv[0].astype(F32)
    for j in range(1, RING):
        total = total + vrecv[j].astype(F32)
    total = total.astype(BF16)
    rest = mm_nt(total[0:48], moves[0]) + mm_nt(total[48:96], moves[1]) + mm_nt(total[96:144], moves[2])
    tiles = mm(rows_a[...], total) + mm(rows_b[...], rest.astype(BF16))
    tsend[...] = tiles.astype(BF16).reshape(16, 16, 128)

    def send_tile(i, _):
        core = lax.rem(i, 2)
        dest = lax.rem(lax.div(i, 2), 2) * 8 + far_z(lax.div(i, 4))
        to = c * 16 + dest
        own_tile = (to == s) & (core == c)

        @pl.when(own_tile)
        def _():
            tfin[s] = tsend[dest]

        @pl.when(jnp.logical_not(own_tile))
        def _():
            pltpu.make_async_remote_copy(
                src_ref=tsend.at[dest], dst_ref=tfin.at[s],
                send_sem=vs_sems.at[0], recv_sem=vs_sems.at[1],
                device_id=(to, y * 2 + core), device_id_type=MESH,
            ).start()

        return 0

    lax.fori_loop(0, 32, send_tile, 0)

    def first_tile(at_b):
        return pl.multiple_of(jnp.minimum(lax.div(at_b * 48, 128), 4) * 128, 128)

    @pl.when(in_half == c)
    def _():
        bulk_wait(grecv.at[others], gs_sems.at[1])
        sum_s = grecv[0].astype(F32)
        for j in range(1, STORE):
            sum_s = sum_s + grecv[j].astype(F32)
        sum_s = sum_s.astype(BF16)
        for u in range(6):
            hsend[:, u * 128 : (u + 1) * 128] = mm(unpack[u], sum_s).astype(BF16)
        gfin[y] = hsend[:, pl.ds(first_tile(b), 256)]

        def send_rows(k, _):
            to = lax.rem(b + k, 2 * RING)
            pltpu.make_async_remote_copy(
                src_ref=hsend.at[:, pl.ds(first_tile(to), 256)], dst_ref=gfin.at[y],
                send_sem=gy_sems.at[0], recv_sem=gy_sems.at[1],
                device_id=(s, to), device_id_type=MESH,
            ).start()
            return 0

        lax.fori_loop(1, 2 * RING, send_rows, 0)

    bulk_wait(parr.at[others], push_sems.at[1])
    arrived = parr[...].reshape(STORE * 16, 256)
    for u in range(3):
        rows_ref[1, :, u * 256 : (u + 1) * 256] = mm(nsel[u], arrived).astype(BF16)

    def cut(x, width, offset):
        pick = onehot(
            (iota((width, 128), 0) == iota((width, 128), 1) + offset) & (iota((width, 128), 1) < 48)
        )
        high = x.astype(BF16)
        low = (x - high.astype(F32)).astype(BF16)
        return mm(high, pick) + mm(low, pick)

    @pl.when(in_half == c)
    def _():
        bulk_wait(gfin.at[pl.ds(0, RING - 1)], gy_sems.at[1])

    @pl.when(in_half != c)
    def _():
        bulk_wait(gfin, gy_sems.at[1])

    sum_g = gfin[0].astype(F32)
    for j in range(1, RING):
        sum_g = sum_g + gfin[j].astype(F32)
    grad_ref[0:16] = cut(sum_g, 256, b * 48 - first_tile(b))

    @pl.when(in_half == c)
    def _():
        bulk_wait(tfin.at[others], vs_sems.at[1])

    @pl.when(in_half != c)
    def _():
        bulk_wait(tfin, vs_sems.at[1])

    sum_v = tfin[0].astype(F32)
    for j in range(1, STORE):
        sum_v = sum_v + tfin[j].astype(F32)
    grad_ref[16:32, 0:48] = jnp.where(c == 0, sum_v[:, 0:48], sum_v[:, 48:96])

    bulk_wait(vsend.at[pl.ds(0, RING - 1)], vy_sems.at[0])
    bulk_wait(psend.at[others], push_sems.at[0])

    @pl.when(in_half == c)
    def _():
        bulk_wait(psend.at[pl.ds(0, 15)], gy_sems.at[0])
        bulk_wait(tfin.at[others], vs_sems.at[0])

    @pl.when(in_half != c)
    def _():
        bulk_wait(tfin, vs_sems.at[0])


def on_device(
    node_features, history, requests, neighbours, pattern, push_owner, push_slot,
    w_query, w_key, w_value, w_gate, w_out, cotangent,
):
    vmem = pl.BlockSpec(memory_space=pltpu.VMEM)
    hbm = pl.BlockSpec(memory_space=pltpu.HBM)
    both, grads = pl.pallas_call(
        kernel,
        out_shape=(
            pltpu.VMEM((2, 128, 768), BF16),
            pltpu.VMEM((32, 128), F32),
        ),
        in_specs=[hbm] * 13,
        out_specs=(vmem, vmem),
        scratch_shapes=[
            pltpu.VMEM((128, 768), BF16),
            pltpu.VMEM((128, 768), F32),
            pltpu.VMEM((8, STORE), I32),
            pltpu.VMEM((16, 128), I32),
            pltpu.VMEM((16, 16), I32),
            pltpu.VMEM((1, 128), I32),
            pltpu.VMEM((4, STORE), I32),
            pltpu.VMEM((768, 256), BF16),
            pltpu.VMEM((768, 256), BF16),
            pltpu.VMEM((768, 256), BF16),
            pltpu.VMEM((768, 256), BF16),
            pltpu.VMEM((384, 768), BF16),
            pltpu.VMEM((256, 768), BF16),
            pltpu.VMEM((256, 768), BF16),
            pltpu.VMEM((256, 768), BF16),
            pltpu.VMEM((STORE, 1, 128), I32),
            pltpu.VMEM((STORE, 1, 128), I32),
            pltpu.VMEM((3, STORE, 16, 128), BF16),
            pltpu.VMEM((3, STORE, 16, 128), BF16),
            pltpu.VMEM((256, 512), BF16),
            pltpu.VMEM((3, 512, 128), BF16),
            pltpu.VMEM((3, 128, 512), BF16),
            pltpu.VMEM((16, 256), F32),
            pltpu.VMEM((2048, 768), BF16),
            pltpu.VMEM((3, 256, 256), BF16),
            pltpu.VMEM((3, 2048, 256), BF16),
            pltpu.VMEM((3, 64, 256), F32),
            pltpu.VMEM((8, 256), F32),
            pltpu.VMEM((8, 256), F32),
            pltpu.VMEM((3, 8, 256), F32),
            pltpu.VMEM((192, 256), BF16),
            pltpu.VMEM((192, 256), BF16),
            pltpu.VMEM((2, 192, 128), BF16),
            pltpu.VMEM((192, 128), BF16),
            pltpu.VMEM((STORE, 16, 256), BF16),
            pltpu.VMEM((STORE, 16, 256), BF16),
            pltpu.VMEM((8, 144, 128), BF16),
            pltpu.VMEM((8, 144, 128), BF16),
            pltpu.VMEM((16, 16, 128), BF16),
            pltpu.VMEM((STORE, 16, 128), BF16),
            pltpu.VMEM((16, 80, 128), BF16),
            pltpu.VMEM((STORE, 80, 128), BF16),
            pltpu.VMEM((16, 768), BF16),
            pltpu.VMEM((8, 16, 256), BF16),
            pltpu.VMEM((256, 192), BF16),
            pltpu.VMEM((256, 144), BF16),
            pltpu.VMEM((256, 48), BF16),
            pltpu.VMEM((3, 128, 128), BF16),
            pltpu.VMEM((192, 2048), BF16),
            pltpu.VMEM((128, 192), BF16),
            pltpu.VMEM((6, 16, 80), BF16),
            pltpu.SemaphoreType.DMA((6,)),
            pltpu.SemaphoreType.DMA((7,)),
            pltpu.SemaphoreType.DMA((2,)),
            pltpu.SemaphoreType.DMA((2,)),
            pltpu.SemaphoreType.DMA((3,)),
            pltpu.SemaphoreType.DMA((3,)),
            pltpu.SemaphoreType.DMA((48,)),
            pltpu.SemaphoreType.DMA((48,)),
            pltpu.SemaphoreType.DMA((54,)),
            pltpu.SemaphoreType.DMA((54,)),
            pltpu.SemaphoreType.DMA((2,)),
            pltpu.SemaphoreType.DMA((2,)),
            pltpu.SemaphoreType.DMA((2,)),
            pltpu.SemaphoreType.DMA((2,)),
            pltpu.SemaphoreType.DMA((2,)),
            pltpu.SemaphoreType.DMA((2,)),
        ],
        compiler_params=pltpu.CompilerParams(
            collective_id=0, has_side_effects=True, vmem_limit_bytes=60 * 1024 * 1024
        ),
        cost_estimate=pl.CostEstimate(
            flops=7_000_000_000, bytes_accessed=6_000_000, transcendentals=1_600_000
        ),
    )(
        node_features, history, requests.T, neighbours.T, pattern, push_owner.reshape(1, -1),
        push_slot.T,
        cotangent, w_query, w_key, w_value, w_gate, w_out,
    )
    return (
        both[0],
        both[1].astype(F32),
        grads[0:12, 0:48].T,
        grads[16:28, 0:48].T,
    )


def solution(mesh):
    rows = P(("storage", "batch"), None)
    in_specs = (
        rows, rows, rows, rows, P("storage", None), P(("storage", "batch")), rows,
        P(), P(), P(), P(), P(), rows,
    )
    out_specs = (rows, rows, P("batch", "storage"), P("batch", "storage"))
    return jax.shard_map(
        on_device, mesh=mesh, in_specs=in_specs, out_specs=out_specs, check_vma=False
    )
```
